256 devices in a mesh: tok: 32 (over x, z_lo, y), exp: 8 (over z_hi, core).
Axes of the slice: x: 4, y: 4, z: 8 (z_hi: 4, z_lo: 2; z = z_hi * 2 + z_lo), core: 2. Of those that a mesh axis runs over, the one named last changes fastest.
Arguments:
- tokens: bfloat16 [16384, 4096], P('tok'), may hold values from -64 to 64
- slot_params: bfloat16 [4096, 2048], P(None, 'exp'), may hold values from -1 to 1
- weight_in: bfloat16 [32, 4096, 2048], P('exp', 'tok'), may hold values from -0.09375 to 0.09375
- weight_out: bfloat16 [32, 2048, 4096], P('exp', None, 'tok'), may hold values from -0.125 to 0.125
Outputs:
- mixed: bfloat16 [16384, 4096], P('tok', 'exp')
The draws below stay inside these ranges and needn't reach their ends.
All inputs are finite; a program needn't handle non-finite values.
Results may differ from the reference program's by a relative error of at most 0.0071.
Values may be sent and summed in bfloat16 or wider, within the bound.
No kernel may reach another device: no remote copies, remote signals or barrier semaphores. Data moves between devices by JAX's collectives and lax.ppermute only.
A program may use at most 128 MiB of HBM per device.

```python
import math
import jax
import jax.numpy as jnp
from jax import lax

D = 4096
FF = 2048
SLOTS = 64
EXPERTS = 32
TOKENS = 16384


def shared_params(key):
    base = jax.random.normal(key, (D, EXPERTS * SLOTS), jnp.float32)
    return jnp.clip(base * (3.0 / math.sqrt(D)), -1.0, 1.0)


def draw_slot_params(key, part):
    return shared_params(key).astype(jnp.bfloat16)


def draw_tokens(key, part):
    key = jax.random.fold_in(key, 2)
    values = jnp.clip(jax.random.normal(key, (TOKENS, D), jnp.float32), -6.0, 6.0)
    return values.astype(jnp.bfloat16)


def levels(rng, extent, pieces, smallest, largest):
    loudness = 1.0
    for axis_at, blocks in pieces:
        heights = jax.random.uniform(jax.random.fold_in(jax.random.fold_in(rng, 6), axis_at), (blocks,), jnp.float32, smallest / len(pieces), largest / len(pieces))
        loudness = loudness * jnp.repeat(jnp.exp(heights), extent[axis_at] // blocks).reshape((-1,) + (1,) * (len(extent) - 1 - axis_at))
    return loudness


def normal_values(stream_key, shape, width, reach, shards=(), dtype=jnp.bfloat16):
    array = jax.random.normal(stream_key, shape, jnp.float32) * width
    if len(shards) > 0:
        array = levels(stream_key, shape, shards, -0.22, 0.18) * array
    return jnp.clip(array, min=-reach, max=reach).astype(dtype)


def setup_inputs(seed: int = 0) -> dict:
    arg_keys = jax.random.split(jax.random.key(seed), 5)
    return {
        "tokens": draw_tokens(jax.random.fold_in(arg_keys[4], 71), 0),
        "slot_params": draw_slot_params(jax.random.fold_in(arg_keys[4], 71), 0),
        "weight_in": normal_values(arg_keys[2], (EXPERTS, D, FF), D ** -0.5, 0.09375, ((0, 8), (1, 32))),
        "weight_out": normal_values(arg_keys[3], (EXPERTS, FF, D), FF ** -0.5, 0.125, ((0, 8), (2, 32))),
    }


def run_expert(packed):
    inputs, first, second = packed
    pre = jnp.dot(inputs, first, preferred_element_type=jnp.float32)
    hidden = jax.nn.gelu(pre, approximate=False).astype(jnp.bfloat16)
    return jnp.dot(hidden, second, preferred_element_type=jnp.float32).astype(jnp.bfloat16)


def reference(tokens, slot_params, weight_in, weight_out):
    logits = jnp.dot(tokens, slot_params, preferred_element_type=jnp.float32)
    col_max = jnp.max(logits, axis=0)
    shifted = jnp.exp(logits - col_max[None, :])
    col_total = jnp.sum(shifted, axis=0)
    dispatch = shifted.astype(jnp.bfloat16)
    slot_sums = jnp.dot(dispatch.T, tokens, preferred_element_type=jnp.float32)
    slot_inputs = (slot_sums / col_total[:, None]).astype(jnp.bfloat16)
    experts = weight_in.shape[0]
    grouped = slot_inputs.reshape(experts, -1, slot_inputs.shape[1])
    produced = lax.map(run_expert, (grouped, weight_in, weight_out))
    slot_outputs = produced.reshape(-1, produced.shape[2])
    combine = jax.nn.softmax(logits, axis=1).astype(jnp.bfloat16)
    return jnp.dot(combine, slot_outputs, preferred_element_type=jnp.float32).astype(jnp.bfloat16)
```

```python
import jax
import jax.numpy as jnp
from jax import lax
from jax.sharding import PartitionSpec as P

BF16, F32 = jnp.bfloat16, jnp.float32


def split3(value):
    head = lax.reduce_precision(value, 8, 7)
    rest = value - head
    mid = lax.reduce_precision(rest, 8, 7)
    return [head.astype(BF16), mid.astype(BF16), (rest - mid).astype(BF16)]


def join3(parts):
    return parts[0].astype(F32) + parts[1].astype(F32) + parts[2].astype(F32)


def local(tokens, slot_params, weight_in, weight_out):
    n_tok, n_exp = lax.axis_size("tok"), lax.axis_size("exp")
    rows, width = tokens.shape
    experts, block, ff = weight_in.shape
    slots = slot_params.shape[1]
    logits = jnp.dot(tokens, slot_params, preferred_element_type=F32)

    row_max = jnp.max(logits, axis=1)
    row_exp = jnp.exp(logits - row_max[:, None])
    row_total = jnp.sum(row_exp, axis=1)
    row_stats = split3(row_max.reshape(-1, slots)) + split3(row_total.reshape(-1, slots))
    per = rows // slots
    pad = (-len(row_stats) * per) % 16
    own = jnp.concatenate(
        [row_exp.astype(BF16)] + row_stats + [jnp.zeros((pad, slots), BF16)], axis=0
    )
    every = lax.all_gather(own, "exp", axis=0)

    col_max = jnp.max(logits, axis=0)
    shifted = jnp.exp(logits - col_max[None, :])
    col_total = jnp.sum(shifted, axis=0)
    sums = lax.dot_general(
        tokens, shifted.astype(BF16), (((0,), (0,)), ((), ())), preferred_element_type=F32
    ).astype(BF16)
    stats = jnp.stack(split3(col_max) + split3(col_total) + [jnp.zeros((slots,), BF16)] * 10)
    sent = jnp.concatenate(
        [sums.reshape(n_tok, block, slots), jnp.broadcast_to(stats[None], (n_tok, 16, slots))], axis=1
    )
    came = lax.all_to_all(sent, "tok", 0, 0, tiled=True)
    peaks = join3([came[:, block + i] for i in range(3)])
    totals = join3([came[:, block + 3 + i] for i in range(3)])
    scale = jnp.exp(peaks - jnp.max(peaks, axis=0)[None])
    scale = scale / jnp.sum(scale * totals, axis=0)[None]
    slot_inputs = jnp.sum(came[:, :block].astype(F32) * scale[:, None, :], axis=0).astype(BF16)

    slot_inputs = slot_inputs.reshape(block, experts, slots // experts)
    pre_part = jnp.einsum(
        "des,edf->esf", slot_inputs, weight_in, preferred_element_type=F32
    ).astype(BF16)
    pre = lax.all_to_all(pre_part.reshape(n_tok, slots // n_tok, ff), "tok", 0, 0, tiled=True)
    pre = jnp.sum(pre.astype(F32), axis=0)
    hidden = jax.nn.gelu(pre, approximate=False).astype(BF16)
    hidden = lax.all_to_all(
        jnp.broadcast_to(hidden[None], (n_tok,) + hidden.shape), "tok", 0, 0, tiled=True
    )
    hidden = hidden.reshape(experts, slots // experts, ff)
    produced = jnp.einsum(
        "esf,efd->esd", hidden, weight_out, preferred_element_type=F32
    ).astype(BF16).reshape(slots, block)

    group = n_tok // n_exp
    moves = [
        (t * n_exp + e, (e * group + t % group) * n_exp + t // group)
        for t in range(n_tok)
        for e in range(n_exp)
    ]
    piece = lax.ppermute(produced, ("tok", "exp"), moves)
    pieces = lax.all_to_all(
        jnp.broadcast_to(piece[None], (n_tok,) + piece.shape), "tok", 0, 0, tiled=True
    ).reshape(n_exp, group, slots, block)

    def parts(first):
        return [every[:, rows + (first + i) * per : rows + (first + i + 1) * per].reshape(n_exp, rows) for i in range(3)]

    peak, total = join3(parts(0)), join3(parts(3))
    weight = jnp.exp(peak - jnp.max(peak, axis=0)[None])
    weight = weight / jnp.sum(weight * total, axis=0)[None]
    combine = (every[:, :rows].astype(F32) * weight[:, :, None]).astype(BF16)
    mixed = jnp.einsum("eks,eqsd->kqd", combine, pieces, preferred_element_type=F32)
    return mixed.astype(BF16).reshape(rows, group * block)


def solution(mesh):
    placed = (P("tok", None), P(None, "exp"), P("exp", "tok", None), P("exp", None, "tok"))
    return jax.shard_map(
        local, mesh=mesh, in_specs=placed, out_specs=P("tok", "exp"), check_vma=False
    )
```

```python
import functools

import jax
import jax.numpy as jnp
from jax import lax
from jax.experimental import pallas as pl
from jax.experimental.pallas import tpu as pltpu
from jax.sharding import Mesh, PartitionSpec as P

BF16, F32 = jnp.bfloat16, jnp.float32
TOK, EXP = ("x", "zl", "y"), ("zh", "c")
CHUNKS = 4
STATS = 16
VMEM = 60 * 2**20


def split3(value):
    head = value.astype(BF16)
    rest = value - head.astype(F32)
    mid = rest.astype(BF16)
    return [head, mid, (rest - mid.astype(F32)).astype(BF16)]


def join3(parts):
    return parts[0].astype(F32) + parts[1].astype(F32) + parts[2].astype(F32)


def route_kernel(tokens_hbm, params_hbm, own_ref, sent_ref, tokens, params, logits, sem):
    rows, width = tokens.shape
    slots = params.shape[1]
    n_tok, _, block = sent_ref.shape
    span = width // CHUNKS

    def copies(i):
        cut = pl.ds(i * span, span)
        return (
            pltpu.make_async_copy(tokens_hbm.at[:, cut], tokens.at[:, cut], sem.at[0, i]),
            pltpu.make_async_copy(params_hbm.at[cut, :], params.at[cut, :], sem.at[1, i]),
        )

    for i in range(CHUNKS):
        for copy in copies(i):
            copy.start()
    for i in range(CHUNKS):
        for copy in copies(i):
            copy.wait()
        part = jnp.dot(
            tokens[:, i * span : (i + 1) * span],
            params[i * span : (i + 1) * span, :],
            preferred_element_type=F32,
        )
        if i == 0:
            logits[...] = part
        else:
            logits[...] += part

    values = logits[...]
    row_max = jnp.max(values, axis=1, keepdims=True)
    row_exp = jnp.exp(values - row_max)
    row_total = jnp.sum(row_exp, axis=1, keepdims=True)
    own_ref[:rows, :] = row_exp.astype(BF16)
    lane = lax.broadcasted_iota(jnp.int32, (rows, 128), 1)
    pair = jnp.where(lane == 0, row_max, jnp.where(lane == 1, row_total, 0.0)).T[:8]
    terms = jnp.concatenate([term.astype(F32)[:2] for term in split3(pair)] + [jnp.zeros((2, rows), F32)], axis=0)
    own_ref[rows:, :] = jnp.concatenate([terms[:, i * slots : (i + 1) * slots] for i in range(rows // slots)], axis=0).astype(BF16)

    col_max = jnp.max(values, axis=0, keepdims=True)
    shifted = jnp.exp(values - col_max)
    col_total = jnp.sum(shifted, axis=0, keepdims=True)
    dispatch = shifted.T.astype(BF16)
    terms = split3(col_max) + split3(col_total)
    stats = jnp.concatenate([t[:, i * block : (i + 1) * block].astype(F32) for t in terms for i in range(slots // block)]
                            + [jnp.zeros((STATS - len(terms) * (slots // block), block), F32)], axis=0).astype(BF16)
    for i in range(CHUNKS):
        sums = jnp.dot(dispatch, tokens[:, i * span : (i + 1) * span], preferred_element_type=F32).astype(BF16)
        for j in range(span // block):
            sent_ref[i * (span // block) + j, :slots, :] = sums[:, j * block : (j + 1) * block]
    for t in range(n_tok):
        sent_ref[t, slots:, :] = stats


def route(tokens, params, n_tok):
    rows, width = tokens.shape
    slots = params.shape[1]
    return pl.pallas_call(
        route_kernel,
        out_shape=(
            jax.ShapeDtypeStruct((rows + STATS, slots), BF16),
            jax.ShapeDtypeStruct((n_tok, slots + STATS, width // n_tok), BF16),
        ),
        in_specs=[pl.BlockSpec(memory_space=pl.ANY)] * 2,
        out_specs=[pl.BlockSpec(memory_space=pltpu.VMEM)] * 2,
        scratch_shapes=[
            pltpu.VMEM((rows, width), BF16),
            pltpu.VMEM((width, slots), BF16),
            pltpu.VMEM((rows, slots), F32),
            pltpu.SemaphoreType.DMA((2, CHUNKS)),
        ],
        compiler_params=pltpu.CompilerParams(vmem_limit_bytes=40 * 2**20),
        cost_estimate=pl.CostEstimate(flops=4 * rows * width * slots, bytes_accessed=10 * 2**20, transcendentals=2 * rows * slots),
        name="route",
    )(tokens, params)


def final_kernel(own_ref, other_ref, pieces_ref, out_ref):
    groups, total_rows, slots = own_ref.shape
    rows = total_rows - STATS
    _, quarter, _, block = pieces_ref.shape
    core = lax.axis_index("c")
    peaks, totals = [], []
    for ref in (own_ref, other_ref):
        for g in range(groups):
            stats = ref[g, rows:, :].astype(F32)
            stats = jnp.concatenate([stats[i * 8 : (i + 1) * 8] for i in range(rows // slots)], axis=1)
            joined = stats[0:2] + stats[2:4] + stats[4:6]
            peaks.append(joined[0:1])
            totals.append(joined[1:2])
    peaks, totals = jnp.concatenate(peaks, axis=0), jnp.concatenate(totals, axis=0)
    scale = jnp.exp(peaks - jnp.max(peaks, axis=0, keepdims=True))
    scale = scale / jnp.sum(scale * totals, axis=0, keepdims=True)
    scale = jnp.concatenate([scale, jnp.zeros((128 - scale.shape[0], rows), F32)], axis=0).T
    total = None
    for k, ref in enumerate((own_ref, other_ref)):
        for g in range(groups):
            at = k * groups + g
            weights = (ref[g, :rows, :].astype(F32) * scale[:, at : at + 1]).astype(BF16)
            e = 2 * g + (core if k == 0 else 1 - core)
            values = jnp.concatenate([pieces_ref[e, q] for q in range(quarter)], axis=1)
            part = jnp.dot(weights, values, preferred_element_type=F32)
            total = part if total is None else total + part
    out_ref[...] = total.astype(BF16)


def final(own, other, pieces):
    groups, total_rows, slots = own.shape
    rows = total_rows - STATS
    columns = pieces.shape[1] * pieces.shape[3]
    return pl.pallas_call(
        final_kernel,
        out_shape=jax.ShapeDtypeStruct((rows, columns), BF16),
        in_specs=[pl.BlockSpec(memory_space=pltpu.VMEM)] * 3,
        out_specs=pl.BlockSpec(memory_space=pltpu.VMEM),
        compiler_params=pltpu.CompilerParams(vmem_limit_bytes=40 * 2**20),
        cost_estimate=pl.CostEstimate(flops=4 * groups * rows * slots * columns, bytes_accessed=5 * 2**20, transcendentals=0),
        name="final",
    )(own, other, pieces)


def local(tokens, slot_params, weight_in, weight_out):
    n_tok, n_exp = lax.axis_size(TOK), lax.axis_size(EXP)
    experts, block, ff = weight_in.shape
    slots = slot_params.shape[1]
    own, sent = route(tokens, slot_params, n_tok)

    groups = lax.axis_size("zh")
    own, sent = lax.optimization_barrier((own, sent))
    same = lax.all_to_all(jnp.broadcast_to(own[None], (groups,) + own.shape), "zh", 0, 0, tiled=True)
    other = lax.ppermute(same, "c", [(0, 1), (1, 0)])

    came = lax.all_to_all(sent, TOK, 0, 0, tiled=True)
    stats = came[:, slots : slots + 12].reshape(n_tok, 6, slots)
    peaks = join3([stats[:, i] for i in range(3)])
    totals = join3([stats[:, 3 + i] for i in range(3)])
    scale = jnp.exp(peaks - jnp.max(peaks, axis=0)[None])
    scale = scale / jnp.sum(scale * totals, axis=0)[None]
    slot_inputs = jnp.sum(came[:, :slots].astype(F32) * scale[:, :, None], axis=0).astype(BF16)

    slot_inputs = slot_inputs.reshape(experts, slots // experts, block)
    pre_part = jnp.einsum(
        "esd,edf->esf", slot_inputs, weight_in, preferred_element_type=F32
    ).astype(BF16)
    pre = lax.all_to_all(pre_part.reshape(n_tok, slots // n_tok, ff), TOK, 0, 0, tiled=True)
    pre = jnp.sum(pre.astype(F32), axis=0)
    hidden = jax.nn.gelu(pre, approximate=False).astype(BF16)
    hidden = lax.all_to_all(
        jnp.broadcast_to(hidden[None], (n_tok,) + hidden.shape), TOK, 0, 0, tiled=True
    )
    hidden = hidden.reshape(experts, slots // experts, ff)
    produced = jnp.einsum(
        "esf,efd->esd", hidden, weight_out, preferred_element_type=F32
    ).astype(BF16).reshape(slots, block)

    group = n_tok // n_exp
    moves = [
        (t * n_exp + e, (e * group + t % group) * n_exp + t // group)
        for t in range(n_tok)
        for e in range(n_exp)
    ]
    piece = lax.ppermute(produced, TOK + EXP, moves)
    pieces = lax.all_to_all(
        jnp.broadcast_to(piece[None], (n_tok,) + piece.shape), TOK, 0, 0, tiled=True
    ).reshape(n_exp, group, slots, block)
    return final(same, other, pieces)


def solution(mesh):
    mesh = Mesh(mesh.devices.reshape(4, 2, 4, 4, 2), TOK + EXP)
    placed = (P(TOK, None), P(None, EXP), P(EXP, TOK, None), P(EXP, None, TOK))
    return jax.shard_map(
        local, mesh=mesh, in_specs=placed, out_specs=P(TOK, EXP), check_vma=False
    )
```

```python
import jax
import jax.numpy as jnp
from jax import lax
from jax.experimental import pallas as pl
from jax.experimental.pallas import tpu as pltpu
from jax.sharding import Mesh, PartitionSpec as P

BF16, F32 = jnp.bfloat16, jnp.float32
TOK, EXP = ("x", "zl", "y"), ("zh", "c")
CHUNKS = 4
STATS = 16
VMEM = 60 * 2**20


def split3(value):
    head = value.astype(BF16)
    rest = value - head.astype(F32)
    mid = rest.astype(BF16)
    return [head, mid, (rest - mid.astype(F32)).astype(BF16)]


def join3(parts):
    return parts[0].astype(F32) + parts[1].astype(F32) + parts[2].astype(F32)


def route_kernel(tokens_hbm, params_hbm, own_ref, sent_hbm, tokens, params, logits, sent_ref, sem, out_sem):
    rows, width = tokens.shape
    slots = params.shape[1]
    n_tok, _, block = sent_ref.shape
    span = width // CHUNKS

    def copies(i):
        cut = pl.ds(i * span, span)
        return (
            pltpu.make_async_copy(tokens_hbm.at[:, cut], tokens.at[:, cut], sem.at[0, i]),
            pltpu.make_async_copy(params_hbm.at[cut, :], params.at[cut, :], sem.at[1, i]),
        )

    for i in range(CHUNKS):
        for copy in copies(i):
            copy.start()
    for i in range(CHUNKS):
        for copy in copies(i):
            copy.wait()
        part = jnp.dot(
            tokens[:, i * span : (i + 1) * span],
            params[i * span : (i + 1) * span, :],
            preferred_element_type=F32,
        )
        if i == 0:
            logits[...] = part
        else:
            logits[...] += part

    values = logits[...]
    row_max = jnp.max(values, axis=1, keepdims=True)
    row_exp = jnp.exp(values - row_max)
    row_total = jnp.sum(row_exp, axis=1, keepdims=True)
    own_ref[:rows, :] = row_exp.astype(BF16)
    lane = lax.broadcasted_iota(jnp.int32, (rows, 128), 1)
    pair = jnp.where(lane == 0, row_max, jnp.where(lane == 1, row_total, 0.0)).T[:8]
    terms = jnp.concatenate([term.astype(F32)[:2] for term in split3(pair)] + [jnp.zeros((2, rows), F32)], axis=0)
    own_ref[rows:, :] = jnp.concatenate([terms[:, i * slots : (i + 1) * slots] for i in range(rows // slots)], axis=0).astype(BF16)

    col_max = jnp.max(values, axis=0, keepdims=True)
    shifted = jnp.exp(values - col_max)
    col_total = jnp.sum(shifted, axis=0, keepdims=True)
    dispatch = shifted.T.astype(BF16)
    terms = split3(col_max) + split3(col_total)
    stats = jnp.concatenate([t[:, i * block : (i + 1) * block].astype(F32) for t in terms for i in range(slots // block)]
                            + [jnp.zeros((STATS - len(terms) * (slots // block), block), F32)], axis=0).astype(BF16)
    per = n_tok // CHUNKS
    leave = []
    for i in range(CHUNKS):
        sums = jnp.dot(dispatch, tokens[:, i * span : (i + 1) * span], preferred_element_type=F32).astype(BF16)
        for j in range(per):
            sent_ref[i * per + j, :slots, :] = sums[:, j * block : (j + 1) * block]
            sent_ref[i * per + j, slots:, :] = stats
        cut = pl.ds(i * per, per)
        leave.append(pltpu.make_async_copy(sent_ref.at[cut], sent_hbm.at[cut], out_sem.at[i]))
        leave[-1].start()
    for copy in leave:
        copy.wait()


def route(tokens, params, n_tok):
    rows, width = tokens.shape
    slots = params.shape[1]
    return pl.pallas_call(
        route_kernel,
        out_shape=(
            jax.ShapeDtypeStruct((rows + STATS, slots), BF16),
            jax.ShapeDtypeStruct((n_tok, slots + STATS, width // n_tok), BF16),
        ),
        in_specs=[pl.BlockSpec(memory_space=pltpu.HBM)] * 2,
        out_specs=[pl.BlockSpec(memory_space=pltpu.VMEM), pl.BlockSpec(memory_space=pltpu.HBM)],
        scratch_shapes=[
            pltpu.VMEM((rows, width), BF16),
            pltpu.VMEM((width, slots), BF16),
            pltpu.VMEM((rows, slots), F32),
            pltpu.VMEM((n_tok, slots + STATS, width // n_tok), BF16),
            pltpu.SemaphoreType.DMA((2, CHUNKS)),
            pltpu.SemaphoreType.DMA((CHUNKS,)),
        ],
        compiler_params=pltpu.CompilerParams(vmem_limit_bytes=VMEM),
        cost_estimate=pl.CostEstimate(flops=4 * rows * width * slots, bytes_accessed=10 * 2**20, transcendentals=2 * rows * slots),
        name="route",
    )(tokens, params)


def expand_kernel(came_hbm, weight_hbm, out_ref, came_ref, weight_ref, stats_ref, came_sem, weight_sem, stats_sem):
    n_tok, total_rows, block = came_ref.shape
    slots = total_rows - STATS
    experts, _, ff = weight_ref.shape
    cuts = slots // block
    per = slots // experts
    _, high, wide = out_ref.shape
    group = n_tok // CHUNKS
    stats_copy = pltpu.make_async_copy(came_hbm.at[:, pl.ds(slots, STATS), :], stats_ref, stats_sem)
    came_copies = [
        pltpu.make_async_copy(came_hbm.at[pl.ds(i * group, group)], came_ref.at[pl.ds(i * group, group)], came_sem.at[i])
        for i in range(CHUNKS)
    ]
    weight_copies = [pltpu.make_async_copy(weight_hbm.at[e], weight_ref.at[e], weight_sem.at[e]) for e in range(experts)]
    for copy in [stats_copy] + came_copies + weight_copies:
        copy.start()
    stats_copy.wait()
    stats = stats_ref[...].astype(F32)
    terms = [stats[:, i * cuts : (i + 1) * cuts] for i in range(6)]
    peaks = terms[0] + terms[1] + terms[2]
    totals = terms[3] + terms[4] + terms[5]
    scale = jnp.exp(peaks - jnp.max(peaks, axis=0, keepdims=True))
    scale = scale / jnp.sum(scale * totals, axis=0, keepdims=True)
    columns = [
        jnp.concatenate([scale[:, c, :], jnp.zeros((block - n_tok, block), F32)], axis=0).T for c in range(cuts)
    ]
    parts = [None] * cuts
    for i in range(CHUNKS):
        came_copies[i].wait()
        for c in range(cuts):
            for t in range(i * group, (i + 1) * group):
                part = came_ref[t, c * block : (c + 1) * block, :].astype(F32) * columns[c][:, t : t + 1]
                parts[c] = part if parts[c] is None else parts[c] + part
    inputs = jnp.concatenate([part.astype(BF16) for part in parts], axis=0)
    for e in range(experts):
        weight_copies[e].wait()
        pre = jnp.dot(inputs[e * per : (e + 1) * per], weight_ref[e], preferred_element_type=F32).astype(BF16)
        for i in range(per // high):
            for j in range(ff // wide):
                out_ref[(e * (per // high) + i) * (ff // wide) + j] = pre[i * high : (i + 1) * high, j * wide : (j + 1) * wide]


def expand(came, weight_in):
    n_tok, total_rows, block = came.shape
    slots = total_rows - STATS
    experts, _, ff = weight_in.shape
    high = 16
    return pl.pallas_call(
        expand_kernel,
        out_shape=jax.ShapeDtypeStruct((n_tok, high, slots * ff // (n_tok * high)), BF16),
        in_specs=[pl.BlockSpec(memory_space=pltpu.HBM)] * 2,
        out_specs=pl.BlockSpec(memory_space=pltpu.VMEM),
        scratch_shapes=[
            pltpu.VMEM(came.shape, BF16),
            pltpu.VMEM(weight_in.shape, BF16),
            pltpu.VMEM((n_tok, STATS, block), BF16),
            pltpu.SemaphoreType.DMA((CHUNKS,)),
            pltpu.SemaphoreType.DMA((experts,)),
            pltpu.SemaphoreType.DMA,
        ],
        compiler_params=pltpu.CompilerParams(vmem_limit_bytes=58 * 2**20),
        cost_estimate=pl.CostEstimate(flops=2 * slots * block * ff, bytes_accessed=6 * 2**20, transcendentals=0),
        name="expand",
    )(came, weight_in)


def produce_kernel(hidden_hbm, weight_hbm, out_ref, hidden_ref, weight_ref, hidden_sem, weight_sem):
    _, high, wide = hidden_ref.shape
    experts, ff, block = weight_ref.shape
    per = out_ref.shape[0] // experts
    halves, chunks = ff // wide, per // high
    hidden_copy = pltpu.make_async_copy(hidden_hbm, hidden_ref, hidden_sem)
    weight_copies = [pltpu.make_async_copy(weight_hbm.at[e], weight_ref.at[e], weight_sem.at[e]) for e in range(experts)]
    for copy in [hidden_copy] + weight_copies:
        copy.start()
    hidden_copy.wait()
    for e in range(experts):
        weight_copies[e].wait()
        total = None
        for j in range(halves):
            rows = jnp.concatenate([hidden_ref[(e * chunks + i) * halves + j] for i in range(chunks)], axis=0)
            part = jnp.dot(rows, weight_ref[e, j * wide : (j + 1) * wide, :], preferred_element_type=F32)
            total = part if total is None else total + part
        out_ref[e * per : (e + 1) * per, :] = total.astype(BF16)


def produce(hidden, weight_out):
    n_tok, high, wide = hidden.shape
    experts, ff, block = weight_out.shape
    slots = n_tok * high * wide // ff
    return pl.pallas_call(
        produce_kernel,
        out_shape=jax.ShapeDtypeStruct((slots, block), BF16),
        in_specs=[pl.BlockSpec(memory_space=pltpu.HBM)] * 2,
        out_specs=pl.BlockSpec(memory_space=pltpu.VMEM),
        scratch_shapes=[
            pltpu.VMEM(hidden.shape, BF16),
            pltpu.VMEM(weight_out.shape, BF16),
            pltpu.SemaphoreType.DMA,
            pltpu.SemaphoreType.DMA((experts,)),
        ],
        compiler_params=pltpu.CompilerParams(vmem_limit_bytes=57 * 2**20),
        cost_estimate=pl.CostEstimate(flops=2 * slots * ff * block, bytes_accessed=3 * 2**20, transcendentals=0),
        name="produce",
    )(hidden, weight_out)


def combine_kernel(own_ref, twin_ref, near_ref, far_ref, rest_ref, out_ref):
    total_rows, slots = own_ref.shape
    rows = total_rows - STATS
    here, core = lax.axis_index("zh"), lax.axis_index("c")
    n_hi = out_ref.shape[0] // 2
    step = 2 * core - 1
    blocks = [
        (own_ref, 0, 0, 0), (twin_ref, 0, 0, 1), (near_ref, 0, 1, 0), (far_ref, 0, 1, 1), (far_ref, total_rows, 2, 0),
        (rest_ref, 0, -1, 1), (rest_ref, total_rows, -1, 0), (rest_ref, 2 * total_rows, -2, 1),
    ]
    peaks, totals = [], []
    for ref, at, _, _ in blocks:
        stats = ref[at + rows : at + total_rows, :].astype(F32)
        stats = jnp.concatenate([stats[i * 8 : (i + 1) * 8] for i in range(rows // slots)], axis=1)
        joined = stats[0:2] + stats[2:4] + stats[4:6]
        peaks.append(joined[0:1])
        totals.append(joined[1:2])
    peaks, totals = jnp.concatenate(peaks, axis=0), jnp.concatenate(totals, axis=0)
    scale = jnp.exp(peaks - jnp.max(peaks, axis=0, keepdims=True))
    scale = scale / jnp.sum(scale * totals, axis=0, keepdims=True)
    scale = jnp.concatenate([scale, jnp.zeros((128 - scale.shape[0], rows), F32)], axis=0).T
    for k, (ref, at, steps, flip) in enumerate(blocks):
        z = lax.rem(here + steps * step + 2 * n_hi, n_hi)
        e = 2 * z + (1 - core if flip else core)
        out_ref[e] = (ref[at : at + rows, :].astype(F32) * scale[:, k : k + 1]).astype(BF16)


def combine(own, twin, near, far, rest, n_exp):
    total_rows, slots = own.shape
    rows = total_rows - STATS
    return pl.pallas_call(
        combine_kernel,
        out_shape=jax.ShapeDtypeStruct((n_exp, rows, slots), BF16),
        in_specs=[pl.BlockSpec(memory_space=pltpu.VMEM)] * 5,
        out_specs=pl.BlockSpec(memory_space=pltpu.VMEM),
        compiler_params=pltpu.CompilerParams(vmem_limit_bytes=32 * 2**20),
        cost_estimate=pl.CostEstimate(flops=2 * n_exp * rows * slots, bytes_accessed=4 * 2**20, transcendentals=0),
        name="combine",
    )(own, twin, near, far, rest)


def final_kernel(weights_ref, pieces_ref, out_ref):
    n_exp, rows, slots = weights_ref.shape
    quarter = pieces_ref.shape[1]
    total = None
    for e in range(n_exp):
        values = jnp.concatenate([pieces_ref[e, q] for q in range(quarter)], axis=1)
        part = jnp.dot(weights_ref[e], values, preferred_element_type=F32)
        total = part if total is None else total + part
    out_ref[...] = total.astype(BF16)


def final(weights, pieces):
    n_exp, rows, slots = weights.shape
    columns = pieces.shape[1] * pieces.shape[3]
    return pl.pallas_call(
        final_kernel,
        out_shape=jax.ShapeDtypeStruct((rows, columns), BF16),
        in_specs=[pl.BlockSpec(memory_space=pltpu.VMEM)] * 2,
        out_specs=pl.BlockSpec(memory_space=pltpu.VMEM),
        compiler_params=pltpu.CompilerParams(vmem_limit_bytes=40 * 2**20),
        cost_estimate=pl.CostEstimate(flops=2 * n_exp * rows * slots * columns, bytes_accessed=5 * 2**20, transcendentals=0),
        name="final",
    )(weights, pieces)


def local(tokens, slot_params, weight_in, weight_out):
    n_tok, n_exp, n_hi = lax.axis_size(TOK), lax.axis_size(EXP), lax.axis_size("zh")
    block, slots = weight_in.shape[1], slot_params.shape[1]
    swap = [(0, 1), (1, 0)]
    along = [
        (2 * z + c, 2 * ((z + (1 if c == 0 else -1)) % n_hi) + c) for z in range(n_hi) for c in range(2)
    ]
    own, sent = route(tokens, slot_params, n_tok)

    near = lax.ppermute(own, EXP, along)
    twin = lax.ppermute(own, "c", swap)
    sent, twin = lax.optimization_barrier((sent, twin))
    came = lax.all_to_all(sent, TOK, 0, 0, tiled=True)
    came, near = lax.optimization_barrier((came, near))
    far = lax.ppermute(jnp.concatenate([twin, near]), EXP, along)

    pre = lax.all_to_all(expand(came, weight_in), TOK, 0, 0, tiled=True)
    pre = jnp.sum(pre.astype(F32), axis=0)
    hidden = jax.nn.gelu(pre, approximate=False).astype(BF16)
    hidden = lax.all_to_all(
        jnp.broadcast_to(hidden[None], (n_tok,) + hidden.shape), TOK, 0, 0, tiled=True
    )
    hidden, far = lax.optimization_barrier((hidden, far))
    rest = lax.ppermute(jnp.concatenate([near, far]), "c", swap)
    produced = produce(hidden, weight_out)

    group = n_tok // n_exp
    moves = [
        (t * n_exp + e, (e * group + t % group) * n_exp + t // group)
        for t in range(n_tok)
        for e in range(n_exp)
    ]
    piece = lax.ppermute(produced, TOK + EXP, moves)
    pieces = lax.all_to_all(
        jnp.broadcast_to(piece[None], (n_tok,) + piece.shape), TOK, 0, 0, tiled=True
    ).reshape(n_exp, group, slots, block)
    return final(combine(own, twin, near, far, rest, n_exp), pieces)


def solution(mesh):
    mesh = Mesh(mesh.devices.reshape(4, 2, 4, 4, 2), TOK + EXP)
    placed = (P(TOK, None), P(None, EXP), P(EXP, TOK, None), P(EXP, None, TOK))
    return jax.shard_map(
        local, mesh=mesh, in_specs=placed, out_specs=P(TOK, EXP), check_vma=False
    )
```

```python
import jax
import jax.numpy as jnp
from jax import lax
from jax.experimental import pallas as pl
from jax.experimental.pallas import tpu as pltpu
from jax.sharding import Mesh, PartitionSpec as P

BF16, F32 = jnp.bfloat16, jnp.float32
TOK, EXP = ("x", "zl", "y"), ("zh", "c")
ALL = TOK + EXP
CHUNKS = 4
STATS = 16
VMEM = 60 * 2**20


def split3(value):
    head = value.astype(BF16)
    rest = value - head.astype(F32)
    mid = rest.astype(BF16)
    return [head, mid, (rest - mid.astype(F32)).astype(BF16)]


def join3(parts):
    return parts[0].astype(F32) + parts[1].astype(F32) + parts[2].astype(F32)


def place(t, core):
    return jnp.where(core == 0, (t % 4) * 8 + t // 4, t)


def route_kernel(tokens_hbm, params_hbm, own_ref, sent_hbm, tokens, params, logits, sent_ref, stats_ref, sem, out_sem, stats_sem):
    rows, width = tokens.shape
    slots = params.shape[1]
    n_tok, _, block = sent_ref.shape
    groups = sent_hbm.shape[0]
    each = n_tok // groups
    core = lax.axis_index("c")
    span = width // CHUNKS

    def copies(i):
        cut = pl.ds(i * span, span)
        return (
            pltpu.make_async_copy(tokens_hbm.at[:, cut], tokens.at[:, cut], sem.at[0, i]),
            pltpu.make_async_copy(params_hbm.at[cut, :], params.at[cut, :], sem.at[1, i]),
        )

    for i in range(CHUNKS):
        for copy in copies(i):
            copy.start()
    for i in range(CHUNKS):
        for copy in copies(i):
            copy.wait()
        part = jnp.dot(
            tokens[:, i * span : (i + 1) * span],
            params[i * span : (i + 1) * span, :],
            preferred_element_type=F32,
        )
        if i == 0:
            logits[...] = part
        else:
            logits[...] += part

    values = logits[...]
    row_max = jnp.max(values, axis=1, keepdims=True)
    row_exp = jnp.exp(values - row_max)
    row_total = jnp.sum(row_exp, axis=1, keepdims=True)
    own_ref[:rows, :] = row_exp.astype(BF16)
    lane = lax.broadcasted_iota(jnp.int32, (rows, 128), 1)
    pair = jnp.where(lane == 0, row_max, jnp.where(lane == 1, row_total, 0.0)).T[:8]
    terms = jnp.concatenate([term.astype(F32)[:2] for term in split3(pair)] + [jnp.zeros((2, rows), F32)], axis=0)
    own_ref[rows:, :] = jnp.concatenate([terms[:, i * slots : (i + 1) * slots] for i in range(rows // slots)], axis=0).astype(BF16)

    col_max = jnp.max(values, axis=0, keepdims=True)
    shifted = jnp.exp(values - col_max)
    col_total = jnp.sum(shifted, axis=0, keepdims=True)
    dispatch = shifted.T.astype(BF16)
    terms = split3(col_max) + split3(col_total)
    stats = jnp.concatenate([t[:, i * block : (i + 1) * block].astype(F32) for t in terms for i in range(slots // block)]
                            + [jnp.zeros((STATS - len(terms) * (slots // block), block), F32)], axis=0).astype(BF16)
    stats_ref[...] = stats
    leave = [
        pltpu.make_async_copy(stats_ref, sent_hbm.at[g, pl.ds(each * slots, STATS)], stats_sem.at[g])
        for g in range(groups)
    ]
    for copy in leave:
        copy.start()
    per = n_tok // CHUNKS
    for i in range(CHUNKS):
        sums = jnp.dot(dispatch, tokens[:, i * span : (i + 1) * span], preferred_element_type=F32).astype(BF16)
        for j in range(per):
            t = i * per + j
            sent_ref[t] = sums[:, j * block : (j + 1) * block]
            at = place(t, core)
            copy = pltpu.make_async_copy(
                sent_ref.at[t], sent_hbm.at[at // each, pl.ds(pl.multiple_of((at % each) * slots, slots), slots)], out_sem.at[t]
            )
            copy.start()
            leave.append(copy)
    for copy in leave:
        copy.wait()


def route(tokens, params, n_tok):
    rows, width = tokens.shape
    slots = params.shape[1]
    return pl.pallas_call(
        route_kernel,
        out_shape=(
            jax.ShapeDtypeStruct((rows + STATS, slots), BF16),
            jax.ShapeDtypeStruct((4, n_tok // 4 * slots + STATS, width // n_tok), BF16),
        ),
        in_specs=[pl.BlockSpec(memory_space=pltpu.HBM)] * 2,
        out_specs=[pl.BlockSpec(memory_space=pltpu.VMEM), pl.BlockSpec(memory_space=pltpu.HBM)],
        scratch_shapes=[
            pltpu.VMEM((rows, width), BF16),
            pltpu.VMEM((width, slots), BF16),
            pltpu.VMEM((rows, slots), F32),
            pltpu.VMEM((n_tok, slots, width // n_tok), BF16),
            pltpu.VMEM((STATS, width // n_tok), BF16),
            pltpu.SemaphoreType.DMA((2, CHUNKS)),
            pltpu.SemaphoreType.DMA((n_tok,)),
            pltpu.SemaphoreType.DMA((4,)),
        ],
        compiler_params=pltpu.CompilerParams(vmem_limit_bytes=VMEM),
        cost_estimate=pl.CostEstimate(flops=4 * rows * width * slots, bytes_accessed=10 * 2**20, transcendentals=2 * rows * slots),
        name="route",
    )(tokens, params)


def scales(stats, cuts, block):
    senders = stats.shape[0]
    terms = [stats[:, i * cuts : (i + 1) * cuts] for i in range(6)]
    peaks = terms[0] + terms[1] + terms[2]
    totals = terms[3] + terms[4] + terms[5]
    peak = jnp.max(peaks, axis=0, keepdims=True)
    scale = jnp.exp(peaks - peak)
    total = jnp.sum(scale * totals, axis=0, keepdims=True)
    def columns(factor):
        return [
            jnp.concatenate([factor[:, c, :], jnp.zeros((block - senders, block), F32)], axis=0).T for c in range(cuts)
        ]
    return peak, total, scale, columns


def merge_kernel(came_ref, out_ref):
    senders, _, block = came_ref.shape
    each, total_rows, _ = out_ref.shape
    slots = total_rows - STATS
    cuts = slots // block
    peak, total, scale, columns = scales(came_ref[:, each * slots :, :].astype(F32), cuts, block)
    terms = split3(peak[0]) + split3(total[0])
    stats = jnp.concatenate([t.astype(F32) for t in terms] + [jnp.zeros((STATS - len(terms) * cuts, block), F32)], axis=0).astype(BF16)
    columns = columns(scale)
    for r in range(each):
        out_ref[r, slots:, :] = stats
    for c in range(cuts):
        factors = [jnp.broadcast_to(columns[c][:, t : t + 1], (block, block)) for t in range(senders)]
        for r in range(each):
            at = r * slots + c * block
            parts = [came_ref[t, at : at + block, :].astype(F32) * factors[t] for t in range(senders)]
            out_ref[r, c * block : (c + 1) * block, :] = sum(parts[1:], parts[0]).astype(BF16)


def merge(came, slots):
    senders, total_rows, block = came.shape
    each = total_rows // slots
    return pl.pallas_call(
        merge_kernel,
        out_shape=jax.ShapeDtypeStruct((each, slots + STATS, block), BF16),
        in_specs=[pl.BlockSpec(memory_space=pltpu.VMEM)],
        out_specs=pl.BlockSpec(memory_space=pltpu.VMEM),
        compiler_params=pltpu.CompilerParams(vmem_limit_bytes=32 * 2**20),
        cost_estimate=pl.CostEstimate(flops=2 * senders * each * slots * block, bytes_accessed=3 * 2**20, transcendentals=0),
        name="merge",
    )(came)


def expand_kernel(came_ref, weight_hbm, out_ref, weight_ref, weight_sem):
    senders, total_rows, block = came_ref.shape
    slots = total_rows - STATS
    experts, _, ff = weight_ref.shape
    cuts = slots // block
    per = slots // experts
    _, high, wide = out_ref.shape
    weight_copies = [pltpu.make_async_copy(weight_hbm.at[e], weight_ref.at[e], weight_sem.at[e]) for e in range(experts)]
    for copy in weight_copies:
        copy.start()
    _, total, scale, columns = scales(came_ref[:, slots:, :].astype(F32), cuts, block)
    columns = columns(scale / total)
    parts = []
    for c in range(cuts):
        part = [came_ref[t, c * block : (c + 1) * block, :].astype(F32) * columns[c][:, t : t + 1] for t in range(senders)]
        parts.append(sum(part[1:], part[0]).astype(BF16))
    inputs = jnp.concatenate(parts, axis=0)
    for e in range(experts):
        weight_copies[e].wait()
        pre = jnp.dot(inputs[e * per : (e + 1) * per], weight_ref[e], preferred_element_type=F32).astype(BF16)
        for i in range(per // high):
            for j in range(ff // wide):
                out_ref[(e * (per // high) + i) * (ff // wide) + j] = pre[i * high : (i + 1) * high, j * wide : (j + 1) * wide]


def expand(came, weight_in, n_tok):
    senders, total_rows, block = came.shape
    slots = total_rows - STATS
    experts, _, ff = weight_in.shape
    high = 16
    return pl.pallas_call(
        expand_kernel,
        out_shape=jax.ShapeDtypeStruct((n_tok, high, slots * ff // (n_tok * high)), BF16),
        in_specs=[pl.BlockSpec(memory_space=pltpu.VMEM), pl.BlockSpec(memory_space=pltpu.HBM)],
        out_specs=pl.BlockSpec(memory_space=pltpu.VMEM),
        scratch_shapes=[pltpu.VMEM(weight_in.shape, BF16), pltpu.SemaphoreType.DMA((experts,))],
        compiler_params=pltpu.CompilerParams(vmem_limit_bytes=57 * 2**20),
        cost_estimate=pl.CostEstimate(flops=2 * slots * block * ff, bytes_accessed=4 * 2**20, transcendentals=0),
        name="expand",
    )(came, weight_in)


def produce_kernel(hidden_ref, weight_hbm, out_ref, weight_ref, weight_sem):
    _, high, wide = hidden_ref.shape
    experts, ff, block = weight_ref.shape
    per = out_ref.shape[0] // experts
    halves, chunks = ff // wide, per // high
    weight_copies = [pltpu.make_async_copy(weight_hbm.at[e], weight_ref.at[e], weight_sem.at[e]) for e in range(experts)]
    for copy in weight_copies:
        copy.start()
    for e in range(experts):
        weight_copies[e].wait()
        total = None
        for j in range(halves):
            rows = jnp.concatenate([hidden_ref[(e * chunks + i) * halves + j] for i in range(chunks)], axis=0)
            part = jnp.dot(rows, weight_ref[e, j * wide : (j + 1) * wide, :], preferred_element_type=F32)
            total = part if total is None else total + part
        out_ref[e * per : (e + 1) * per, :] = total.astype(BF16)


def produce(hidden, weight_out):
    n_tok, high, wide = hidden.shape
    experts, ff, block = weight_out.shape
    slots = n_tok * high * wide // ff
    return pl.pallas_call(
        produce_kernel,
        out_shape=jax.ShapeDtypeStruct((slots, block), BF16),
        in_specs=[pl.BlockSpec(memory_space=pltpu.VMEM), pl.BlockSpec(memory_space=pltpu.HBM)],
        out_specs=pl.BlockSpec(memory_space=pltpu.VMEM),
        scratch_shapes=[pltpu.VMEM(weight_out.shape, BF16), pltpu.SemaphoreType.DMA((experts,))],
        compiler_params=pltpu.CompilerParams(vmem_limit_bytes=57 * 2**20),
        cost_estimate=pl.CostEstimate(flops=2 * slots * ff * block, bytes_accessed=3 * 2**20, transcendentals=0),
        name="produce",
    )(hidden, weight_out)


def combine_kernel(own_ref, twin_ref, near_ref, far_ref, rest_ref, out_ref):
    total_rows, slots = own_ref.shape
    rows = total_rows - STATS
    here, core = lax.axis_index("zh"), lax.axis_index("c")
    n_hi = out_ref.shape[0] // 2
    step = 2 * core - 1
    blocks = [
        (own_ref, 0, 0, 0), (twin_ref, 0, 0, 1), (near_ref, 0, 1, 0), (far_ref, 0, 1, 1), (far_ref, total_rows, 2, 0),
        (rest_ref, 0, -1, 1), (rest_ref, total_rows, -1, 0), (rest_ref, 2 * total_rows, -2, 1),
    ]
    peaks, totals = [], []
    for ref, at, _, _ in blocks:
        stats = ref[at + rows : at + total_rows, :].astype(F32)
        stats = jnp.concatenate([stats[i * 8 : (i + 1) * 8] for i in range(rows // slots)], axis=1)
        joined = stats[0:2] + stats[2:4] + stats[4:6]
        peaks.append(joined[0:1])
        totals.append(joined[1:2])
    peaks, totals = jnp.concatenate(peaks, axis=0), jnp.concatenate(totals, axis=0)
    scale = jnp.exp(peaks - jnp.max(peaks, axis=0, keepdims=True))
    scale = scale / jnp.sum(scale * totals, axis=0, keepdims=True)
    scale = jnp.concatenate([scale, jnp.zeros((128 - scale.shape[0], rows), F32)], axis=0).T
    for k, (ref, at, steps, flip) in enumerate(blocks):
        z = lax.rem(here + steps * step + 2 * n_hi, n_hi)
        e = 2 * z + (1 - core if flip else core)
        out_ref[e] = (ref[at : at + rows, :].astype(F32) * scale[:, k : k + 1]).astype(BF16)


def combine(own, twin, near, far, rest, n_exp):
    total_rows, slots = own.shape
    rows = total_rows - STATS
    return pl.pallas_call(
        combine_kernel,
        out_shape=jax.ShapeDtypeStruct((n_exp, rows, slots), BF16),
        in_specs=[pl.BlockSpec(memory_space=pltpu.VMEM)] * 5,
        out_specs=pl.BlockSpec(memory_space=pltpu.VMEM),
        compiler_params=pltpu.CompilerParams(vmem_limit_bytes=32 * 2**20),
        cost_estimate=pl.CostEstimate(flops=2 * n_exp * rows * slots, bytes_accessed=4 * 2**20, transcendentals=0),
        name="combine",
    )(own, twin, near, far, rest)


def final_kernel(weights_hbm, pieces_ref, out_ref, weights_ref, sem):
    n_exp, rows, slots = weights_ref.shape
    quarter = pieces_ref.shape[0] // n_exp
    copies = [pltpu.make_async_copy(weights_hbm.at[e], weights_ref.at[e], sem.at[e]) for e in range(n_exp)]
    for copy in copies:
        copy.start()
    here, core = lax.axis_index("zh"), lax.axis_index("c")
    total = None
    for e in range(n_exp):
        first = ((e // 2 + here) % 4) * 8 + (e % 2) * 4
        values = jnp.concatenate([pieces_ref[place(first + q, core)] for q in range(quarter)], axis=1)
        copies[e].wait()
        part = jnp.dot(weights_ref[e], values, preferred_element_type=F32)
        total = part if total is None else total + part
    out_ref[...] = total.astype(BF16)


def final(weights, pieces):
    n_exp, rows, slots = weights.shape
    columns = pieces.shape[0] // n_exp * pieces.shape[2]
    return pl.pallas_call(
        final_kernel,
        out_shape=jax.ShapeDtypeStruct((rows, columns), BF16),
        in_specs=[pl.BlockSpec(memory_space=pltpu.HBM), pl.BlockSpec(memory_space=pltpu.VMEM)],
        out_specs=pl.BlockSpec(memory_space=pltpu.VMEM),
        scratch_shapes=[pltpu.VMEM(weights.shape, BF16), pltpu.SemaphoreType.DMA((n_exp,))],
        compiler_params=pltpu.CompilerParams(vmem_limit_bytes=50 * 2**20),
        cost_estimate=pl.CostEstimate(flops=2 * n_exp * rows * slots * columns, bytes_accessed=5 * 2**20, transcendentals=0),
        name="final",
    )(weights, pieces)


def flat(x, zl, y, zh, c):
    return (((x * 2 + zl) * 4 + y) * 4 + zh) * 2 + c


def exchange_groups():
    four, eight = [], []
    for zh in range(4):
        four += [[flat(x, zl, y, zh, 0) for y in range(4)] for x in range(4) for zl in range(2)]
        four += [[flat(x, zl, y, zh, 1) for x in range(4)] for zl in range(2) for y in range(4)]
        eight += [[flat(x, zl, y, zh, 0) for x in range(4) for zl in range(2)] for y in range(4)]
        eight += [[flat(x, zl, y, zh, 1) for zl in range(2) for y in range(4)] for x in range(4)]
    return four, eight


def local(tokens, slot_params, weight_in, weight_out):
    n_tok, n_exp, n_hi = lax.axis_size(TOK), lax.axis_size(EXP), lax.axis_size("zh")
    block, slots = weight_in.shape[1], slot_params.shape[1]
    four, eight = exchange_groups()
    swap = [(0, 1), (1, 0)]
    along = [
        (2 * z + c, 2 * ((z + (1 if c == 0 else -1)) % n_hi) + c) for z in range(n_hi) for c in range(2)
    ]
    own, sent = route(tokens, slot_params, n_tok)

    near = lax.ppermute(own, EXP, along)
    twin = lax.ppermute(own, "c", swap)
    sent, twin = lax.optimization_barrier((sent, twin))
    came = lax.all_to_all(sent, ALL, 0, 0, axis_index_groups=four, tiled=True)
    came, near = lax.optimization_barrier((came, near))
    far = lax.ppermute(jnp.concatenate([twin, near]), EXP, along)
    came = lax.all_to_all(merge(came, slots), ALL, 0, 0, axis_index_groups=eight, tiled=True)

    pre = lax.all_to_all(expand(came, weight_in, n_tok), TOK, 0, 0, tiled=True)
    pre, far = lax.optimization_barrier((pre, far))
    rest = lax.ppermute(jnp.concatenate([near, far]), "c", swap)
    pre = jnp.sum(pre.astype(F32), axis=0)
    hidden = jax.nn.gelu(pre, approximate=False).astype(BF16)
    hidden = lax.all_to_all(
        jnp.broadcast_to(hidden[None], (n_tok,) + hidden.shape), TOK, 0, 0, tiled=True
    )
    produced = produce(hidden, weight_out)

    moves = [
        (flat(x, zl, y, zh, c), flat((x + zh) % 4, c, y, x, zl))
        for x in range(4) for zl in range(2) for y in range(4) for zh in range(4) for c in range(2)
    ]
    piece = lax.ppermute(produced, ALL, moves)
    pieces = jnp.broadcast_to(piece[None], (8,) + piece.shape)
    pieces = lax.all_to_all(pieces, ALL, 0, 0, axis_index_groups=eight, tiled=True)
    pieces = jnp.broadcast_to(pieces[None], (4,) + pieces.shape)
    pieces = lax.all_to_all(pieces, ALL, 0, 0, axis_index_groups=four, tiled=True)
    return final(combine(own, twin, near, far, rest, n_exp), pieces.reshape(n_tok, slots, block))


def solution(mesh):
    mesh = Mesh(mesh.devices.reshape(4, 2, 4, 4, 2), ALL)
    placed = (P(TOK, None), P(None, EXP), P(EXP, TOK, None), P(EXP, None, TOK))
    return jax.shard_map(
        local, mesh=mesh, in_specs=placed, out_specs=P(TOK, EXP), check_vma=False
    )
```

```python
import jax
import jax.numpy as jnp
from jax import lax
from jax.experimental import pallas as pl
from jax.experimental.pallas import tpu as pltpu
from jax.sharding import Mesh, PartitionSpec as P

BF16, F32 = jnp.bfloat16, jnp.float32
TOK, EXP = ("x", "zl", "y"), ("zh", "c")
ALL = TOK + EXP
CHUNKS = 4
STATS = 16
VMEM = 60 * 2**20


def split3(value):
    head = value.astype(BF16)
    rest = value - head.astype(F32)
    mid = rest.astype(BF16)
    return [head, mid, (rest - mid.astype(F32)).astype(BF16)]


def join3(parts):
    return parts[0].astype(F32) + parts[1].astype(F32) + parts[2].astype(F32)


def place(t, core):
    return jnp.where(core == 0, (t % 4) * 8 + t // 4, t)


def route_kernel(tokens_hbm, params_hbm, own_ref, sent_hbm, tokens, params, logits, sent_ref, stats_ref, sem, out_sem, stats_sem):
    rows, width = tokens.shape
    slots = params.shape[1]
    n_tok, _, block = sent_ref.shape
    groups = sent_hbm.shape[0]
    each = n_tok // groups
    core = lax.axis_index("c")
    span = width // CHUNKS

    def copies(i):
        cut = pl.ds(i * span, span)
        return (
            pltpu.make_async_copy(tokens_hbm.at[:, cut], tokens.at[:, cut], sem.at[0, i]),
            pltpu.make_async_copy(params_hbm.at[cut, :], params.at[cut, :], sem.at[1, i]),
        )

    for i in range(CHUNKS):
        for copy in copies(i):
            copy.start()
    for i in range(CHUNKS):
        for copy in copies(i):
            copy.wait()
        part = jnp.dot(
            tokens[:, i * span : (i + 1) * span],
            params[i * span : (i + 1) * span, :],
            preferred_element_type=F32,
        )
        if i == 0:
            logits[...] = part
        else:
            logits[...] += part

    values = logits[...]
    row_max = jnp.max(values, axis=1, keepdims=True)
    row_exp = jnp.exp(values - row_max)
    row_total = jnp.sum(row_exp, axis=1, keepdims=True)
    own_ref[:rows, :] = row_exp.astype(BF16)
    lane = lax.broadcasted_iota(jnp.int32, (rows, 128), 1)
    pair = jnp.where(lane == 0, row_max, jnp.where(lane == 1, row_total, 0.0)).T[:8]
    terms = jnp.concatenate([term.astype(F32)[:2] for term in split3(pair)] + [jnp.zeros((2, rows), F32)], axis=0)
    own_ref[rows:, :] = jnp.concatenate([terms[:, i * slots : (i + 1) * slots] for i in range(rows // slots)], axis=0).astype(BF16)

    col_max = jnp.max(values, axis=0, keepdims=True)
    shifted = jnp.exp(values - col_max)
    col_total = jnp.sum(shifted, axis=0, keepdims=True)
    dispatch = shifted.astype(BF16).T
    terms = split3(col_max) + split3(col_total)
    stats = jnp.concatenate([t[:, i * block : (i + 1) * block].astype(F32) for t in terms for i in range(slots // block)]
                            + [jnp.zeros((STATS - len(terms) * (slots // block), block), F32)], axis=0).astype(BF16)
    stats_ref[...] = stats
    leave = [
        pltpu.make_async_copy(stats_ref, sent_hbm.at[g, pl.ds(each * slots, STATS)], stats_sem.at[g])
        for g in range(groups)
    ]
    for copy in leave:
        copy.start()
    per = n_tok // CHUNKS
    for i in range(CHUNKS):
        sums = jnp.dot(dispatch, tokens[:, i * span : (i + 1) * span], preferred_element_type=F32).astype(BF16)
        for j in range(per):
            t = i * per + j
            sent_ref[t] = sums[:, j * block : (j + 1) * block]
            at = place(t, core)
            copy = pltpu.make_async_copy(
                sent_ref.at[t], sent_hbm.at[at // each, pl.ds(pl.multiple_of((at % each) * slots, slots), slots)], out_sem.at[t]
            )
            copy.start()
            leave.append(copy)
    for copy in leave:
        copy.wait()


def route(tokens, params, n_tok):
    rows, width = tokens.shape
    slots = params.shape[1]
    return pl.pallas_call(
        route_kernel,
        out_shape=(
            jax.ShapeDtypeStruct((rows + STATS, slots), BF16),
            jax.ShapeDtypeStruct((4, n_tok // 4 * slots + STATS, width // n_tok), BF16),
        ),
        in_specs=[pl.BlockSpec(memory_space=pltpu.HBM)] * 2,
        out_specs=[pl.BlockSpec(memory_space=pltpu.VMEM), pl.BlockSpec(memory_space=pltpu.HBM)],
        scratch_shapes=[
            pltpu.VMEM((rows, width), BF16),
            pltpu.VMEM((width, slots), BF16),
            pltpu.VMEM((rows, slots), F32),
            pltpu.VMEM((n_tok, slots, width // n_tok), BF16),
            pltpu.VMEM((STATS, width // n_tok), BF16),
            pltpu.SemaphoreType.DMA((2, CHUNKS)),
            pltpu.SemaphoreType.DMA((n_tok,)),
            pltpu.SemaphoreType.DMA((4,)),
        ],
        compiler_params=pltpu.CompilerParams(vmem_limit_bytes=VMEM),
        cost_estimate=pl.CostEstimate(flops=4 * rows * width * slots, bytes_accessed=10 * 2**20, transcendentals=2 * rows * slots),
        name="route",
    )(tokens, params)


def scales(stats, cuts, block):
    senders = stats.shape[0]
    terms = [stats[:, i * cuts : (i + 1) * cuts] for i in range(6)]
    peaks = terms[0] + terms[1] + terms[2]
    totals = terms[3] + terms[4] + terms[5]
    peak = jnp.max(peaks, axis=0, keepdims=True)
    scale = jnp.exp(peaks - peak)
    total = jnp.sum(scale * totals, axis=0, keepdims=True)
    def columns(factor):
        return [
            jnp.concatenate([factor[:, c, :], jnp.zeros((block - senders, block), F32)], axis=0).T for c in range(cuts)
        ]
    return peak, total, scale, columns


def merge_kernel(came_ref, out_ref):
    senders, _, block = came_ref.shape
    each, total_rows, _ = out_ref.shape
    slots = total_rows - STATS
    cuts = slots // block
    peak, total, scale, columns = scales(came_ref[:, each * slots :, :].astype(F32), cuts, block)
    terms = split3(peak[0]) + split3(total[0])
    stats = jnp.concatenate([t.astype(F32) for t in terms] + [jnp.zeros((STATS - len(terms) * cuts, block), F32)], axis=0).astype(BF16)
    columns = columns(scale)
    for r in range(each):
        out_ref[r, slots:, :] = stats
    for c in range(cuts):
        factors = [jnp.broadcast_to(columns[c][:, t : t + 1], (block, block)) for t in range(senders)]
        for r in range(each):
            at = r * slots + c * block
            parts = [came_ref[t, at : at + block, :].astype(F32) * factors[t] for t in range(senders)]
            out_ref[r, c * block : (c + 1) * block, :] = sum(parts[1:], parts[0]).astype(BF16)


def merge(came, slots):
    senders, total_rows, block = came.shape
    each = total_rows // slots
    return pl.pallas_call(
        merge_kernel,
        out_shape=jax.ShapeDtypeStruct((each, slots + STATS, block), BF16),
        in_specs=[pl.BlockSpec(memory_space=pltpu.VMEM)],
        out_specs=pl.BlockSpec(memory_space=pltpu.VMEM),
        compiler_params=pltpu.CompilerParams(vmem_limit_bytes=32 * 2**20),
        cost_estimate=pl.CostEstimate(flops=2 * senders * each * slots * block, bytes_accessed=3 * 2**20, transcendentals=0),
        name="merge",
    )(came)


def expand_kernel(came_hbm, weight_hbm, out_hbm, came_ref, weight_ref, out_ref, came_sem, weight_sem, out_sem):
    senders, total_rows, block = came_ref.shape
    slots = total_rows - STATS
    experts, _, ff = weight_ref.shape
    cuts = slots // block
    per = slots // experts
    n_out, high, wide = out_ref.shape
    each = n_out // experts
    came_copy = pltpu.make_async_copy(came_hbm, came_ref, came_sem)
    weight_copies = [pltpu.make_async_copy(weight_hbm.at[e], weight_ref.at[e], weight_sem.at[e]) for e in range(experts)]
    out_copies = [
        pltpu.make_async_copy(out_ref.at[pl.ds(e * each, each)], out_hbm.at[pl.ds(e * each, each)], out_sem.at[e]) for e in range(experts)
    ]
    for copy in [came_copy] + weight_copies:
        copy.start()
    came_copy.wait()
    _, total, scale, columns = scales(came_ref[:, slots:, :].astype(F32), cuts, block)
    columns = columns(scale / total)
    parts = []
    for c in range(cuts):
        part = [came_ref[t, c * block : (c + 1) * block, :].astype(F32) * columns[c][:, t : t + 1] for t in range(senders)]
        parts.append(sum(part[1:], part[0]).astype(BF16))
    inputs = jnp.concatenate(parts, axis=0)
    for e in range(experts):
        weight_copies[e].wait()
        pre = jnp.dot(inputs[e * per : (e + 1) * per], weight_ref[e], preferred_element_type=F32).astype(BF16)
        for i in range(per // high):
            for j in range(ff // wide):
                out_ref[e * each + i * (ff // wide) + j] = pre[i * high : (i + 1) * high, j * wide : (j + 1) * wide]
        out_copies[e].start()
    for copy in out_copies:
        copy.wait()


def expand(came, weight_in, n_tok):
    senders, total_rows, block = came.shape
    slots = total_rows - STATS
    experts, _, ff = weight_in.shape
    high = 16
    out = (n_tok, high, slots * ff // (n_tok * high))
    return pl.pallas_call(
        expand_kernel,
        out_shape=jax.ShapeDtypeStruct(out, BF16),
        in_specs=[pl.BlockSpec(memory_space=pltpu.HBM)] * 2,
        out_specs=pl.BlockSpec(memory_space=pltpu.HBM),
        scratch_shapes=[
            pltpu.VMEM(came.shape, BF16),
            pltpu.VMEM(weight_in.shape, BF16),
            pltpu.VMEM(out, BF16),
            pltpu.SemaphoreType.DMA,
            pltpu.SemaphoreType.DMA((experts,)),
            pltpu.SemaphoreType.DMA((experts,)),
        ],
        compiler_params=pltpu.CompilerParams(vmem_limit_bytes=57 * 2**20),
        cost_estimate=pl.CostEstimate(flops=2 * slots * block * ff, bytes_accessed=4 * 2**20, transcendentals=0),
        name="expand",
    )(came, weight_in)


def produce_kernel(hidden_hbm, weight_hbm, out_ref, hidden_ref, weight_ref, hidden_sem, weight_sem):
    n_tok, high, wide = hidden_ref.shape
    experts, ff, block = weight_ref.shape
    per = out_ref.shape[0] // experts
    halves, chunks = ff // wide, per // high
    each = n_tok // experts
    copies = [
        (
            pltpu.make_async_copy(hidden_hbm.at[pl.ds(e * each, each)], hidden_ref.at[pl.ds(e * each, each)], hidden_sem.at[e]),
            pltpu.make_async_copy(weight_hbm.at[e], weight_ref.at[e], weight_sem.at[e]),
        )
        for e in range(experts)
    ]
    for pair in copies:
        for copy in pair:
            copy.start()
    for e in range(experts):
        for copy in copies[e]:
            copy.wait()
        total = None
        for j in range(halves):
            rows = jnp.concatenate([hidden_ref[e * each + i * halves + j] for i in range(chunks)], axis=0)
            part = jnp.dot(rows, weight_ref[e, j * wide : (j + 1) * wide, :], preferred_element_type=F32)
            total = part if total is None else total + part
        out_ref[e * per : (e + 1) * per, :] = total.astype(BF16)


def produce(hidden, weight_out):
    n_tok, high, wide = hidden.shape
    experts, ff, block = weight_out.shape
    slots = n_tok * high * wide // ff
    return pl.pallas_call(
        produce_kernel,
        out_shape=jax.ShapeDtypeStruct((slots, block), BF16),
        in_specs=[pl.BlockSpec(memory_space=pltpu.HBM)] * 2,
        out_specs=pl.BlockSpec(memory_space=pltpu.VMEM),
        scratch_shapes=[
            pltpu.VMEM(hidden.shape, BF16),
            pltpu.VMEM(weight_out.shape, BF16),
            pltpu.SemaphoreType.DMA((experts,)),
            pltpu.SemaphoreType.DMA((experts,)),
        ],
        compiler_params=pltpu.CompilerParams(vmem_limit_bytes=57 * 2**20),
        cost_estimate=pl.CostEstimate(flops=2 * slots * ff * block, bytes_accessed=3 * 2**20, transcendentals=0),
        name="produce",
    )(hidden, weight_out)


def combine_kernel(own_ref, twin_ref, near_ref, far_ref, rest_ref, out_ref):
    total_rows, slots = own_ref.shape
    rows = total_rows - STATS
    here, core = lax.axis_index("zh"), lax.axis_index("c")
    n_hi = out_ref.shape[1] // slots // 2
    step = 2 * core - 1
    blocks = [
        (own_ref, 0, 0, 0), (twin_ref, 0, 0, 1), (near_ref, 0, 1, 0), (near_ref, total_rows, 1, 1), (far_ref, 0, 2, 0),
        (rest_ref, 0, -1, 1), (rest_ref, total_rows, -1, 0), (rest_ref, 2 * total_rows, -2, 1),
    ]
    peaks, totals = [], []
    for ref, at, _, _ in blocks:
        stats = ref[at + rows : at + total_rows, :].astype(F32)
        stats = jnp.concatenate([stats[i * 8 : (i + 1) * 8] for i in range(rows // slots)], axis=1)
        joined = stats[0:2] + stats[2:4] + stats[4:6]
        peaks.append(joined[0:1])
        totals.append(joined[1:2])
    peaks, totals = jnp.concatenate(peaks, axis=0), jnp.concatenate(totals, axis=0)
    scale = jnp.exp(peaks - jnp.max(peaks, axis=0, keepdims=True))
    scale = scale / jnp.sum(scale * totals, axis=0, keepdims=True)
    scale = jnp.concatenate([scale, jnp.zeros((128 - scale.shape[0], rows), F32)], axis=0).T
    for k, (ref, at, steps, flip) in enumerate(blocks):
        z = lax.rem(here + steps * step + 2 * n_hi, n_hi)
        e = 2 * z + (1 - core if flip else core)
        at_out = pl.ds(pl.multiple_of(e * slots, slots), slots)
        out_ref[:, at_out] = (ref[at : at + rows, :].astype(F32) * scale[:, k : k + 1]).astype(BF16)


def combine(own, twin, near, far, rest, n_exp):
    total_rows, slots = own.shape
    rows = total_rows - STATS
    return pl.pallas_call(
        combine_kernel,
        out_shape=jax.ShapeDtypeStruct((rows, n_exp * slots), BF16),
        in_specs=[pl.BlockSpec(memory_space=pltpu.VMEM)] * 5,
        out_specs=pl.BlockSpec(memory_space=pltpu.VMEM),
        compiler_params=pltpu.CompilerParams(vmem_limit_bytes=32 * 2**20),
        cost_estimate=pl.CostEstimate(flops=2 * n_exp * rows * slots, bytes_accessed=4 * 2**20, transcendentals=0),
        name="combine",
    )(own, twin, near, far, rest)


def final_kernel(weights_ref, pieces_hbm, out_ref, values, sem):
    rows, total = weights_ref.shape
    n_tok, slots, block = pieces_hbm.shape
    n_exp = total // slots
    quarter = n_tok // n_exp
    here, core = lax.axis_index("zh"), lax.axis_index("c")
    copies = []
    for e in range(n_exp):
        first = ((e // 2 + here) % 4) * 8 + (e % 2) * 4
        for q in range(quarter):
            into = values.at[pl.ds(e * slots, slots), pl.ds(q * block, block)]
            copies.append(pltpu.make_async_copy(pieces_hbm.at[place(first + q, core)], into, sem.at[e * quarter + q]))
            copies[-1].start()
    step = 2
    result = None
    for e in range(0, n_exp, step):
        for copy in copies[e * quarter : (e + step) * quarter]:
            copy.wait()
        cut = slice(e * slots, (e + step) * slots)
        part = jnp.dot(weights_ref[:, cut], values[cut, :], preferred_element_type=F32)
        result = part if result is None else result + part
    out_ref[...] = result.astype(BF16)


def final(weights, pieces):
    rows, total = weights.shape
    n_tok, slots, block = pieces.shape
    columns = n_tok * slots // total * block
    return pl.pallas_call(
        final_kernel,
        out_shape=jax.ShapeDtypeStruct((rows, columns), BF16),
        in_specs=[pl.BlockSpec(memory_space=pltpu.VMEM), pl.BlockSpec(memory_space=pltpu.HBM)],
        out_specs=pl.BlockSpec(memory_space=pltpu.VMEM),
        scratch_shapes=[pltpu.VMEM((total, columns), BF16), pltpu.SemaphoreType.DMA((n_tok,))],
        compiler_params=pltpu.CompilerParams(vmem_limit_bytes=50 * 2**20),
        cost_estimate=pl.CostEstimate(flops=2 * rows * total * columns, bytes_accessed=5 * 2**20, transcendentals=0),
        name="final",
    )(weights, pieces)


def flat(x, zl, y, zh, c):
    return (((x * 2 + zl) * 4 + y) * 4 + zh) * 2 + c


def exchange_groups():
    four, eight = [], []
    for zh in range(4):
        four += [[flat(x, zl, y, zh, 0) for y in range(4)] for x in range(4) for zl in range(2)]
        four += [[flat(x, zl, y, zh, 1) for x in range(4)] for zl in range(2) for y in range(4)]
        eight += [[flat(x, zl, y, zh, 0) for x in range(4) for zl in range(2)] for y in range(4)]
        eight += [[flat(x, zl, y, zh, 1) for zl in range(2) for y in range(4)] for x in range(4)]
    return four, eight


def local(tokens, slot_params, weight_in, weight_out):
    n_tok, n_exp, n_hi = lax.axis_size(TOK), lax.axis_size(EXP), lax.axis_size("zh")
    block, slots = weight_in.shape[1], slot_params.shape[1]
    four, eight = exchange_groups()
    swap = [(0, 1), (1, 0)]
    along = [
        (2 * z + c, 2 * ((z + (1 if c == 0 else -1)) % n_hi) + c) for z in range(n_hi) for c in range(2)
    ]
    own, sent = route(tokens, slot_params, n_tok)

    twin = lax.ppermute(own, "c", swap)
    near = lax.ppermute(jnp.concatenate([own, twin]), EXP, along)
    came = lax.all_to_all(sent, ALL, 0, 0, axis_index_groups=four, tiled=True)
    came, near = lax.optimization_barrier((came, near))
    far = lax.ppermute(near[: own.shape[0]], EXP, along)
    came = lax.all_to_all(merge(came, slots), ALL, 0, 0, axis_index_groups=eight, tiled=True)
    came, far = lax.optimization_barrier((came, far))
    rest = lax.ppermute(jnp.concatenate([near, far]), "c", swap)

    pre = lax.all_to_all(expand(came, weight_in, n_tok), TOK, 0, 0, tiled=True)
    pre = jnp.sum(pre.astype(F32), axis=0)
    hidden = jax.nn.gelu(pre, approximate=False).astype(BF16)
    hidden = lax.all_to_all(
        jnp.broadcast_to(hidden[None], (n_tok,) + hidden.shape), TOK, 0, 0, tiled=True
    )
    produced = produce(hidden, weight_out)

    moves = [
        (flat(x, zl, y, zh, c), flat((x + zh) % 4, c, y, x, zl))
        for x in range(4) for zl in range(2) for y in range(4) for zh in range(4) for c in range(2)
    ]
    piece = lax.ppermute(produced, ALL, moves)
    pieces = jnp.broadcast_to(piece[None], (8,) + piece.shape)
    pieces = lax.all_to_all(pieces, ALL, 0, 0, axis_index_groups=eight, tiled=True)
    pieces = jnp.broadcast_to(pieces[None], (4,) + pieces.shape)
    pieces = lax.all_to_all(pieces, ALL, 0, 0, axis_index_groups=four, tiled=True)
    return final(combine(own, twin, near, far, rest, n_exp), pieces.reshape(n_tok, slots, block))


def solution(mesh):
    mesh = Mesh(mesh.devices.reshape(4, 2, 4, 4, 2), ALL)
    placed = (P(TOK, None), P(None, EXP), P(EXP, TOK, None), P(EXP, None, TOK))
    return jax.shard_map(
        local, mesh=mesh, in_specs=placed, out_specs=P(TOK, EXP), check_vma=False
    )
```

```python
import jax
import jax.numpy as jnp
from jax import lax
from jax.experimental import pallas as pl
from jax.experimental.pallas import tpu as pltpu
from jax.sharding import Mesh, PartitionSpec as P

BF16, F32 = jnp.bfloat16, jnp.float32
TOK, EXP = ("x", "zl", "y"), ("zh", "c")
ALL = TOK + EXP
CHUNKS = 4
STATS = 16
VMEM = 60 * 2**20


def split3(value):
    head = value.astype(BF16)
    rest = value - head.astype(F32)
    mid = rest.astype(BF16)
    return [head, mid, (rest - mid.astype(F32)).astype(BF16)]


def join3(parts):
    return parts[0].astype(F32) + parts[1].astype(F32) + parts[2].astype(F32)


def place(t, core):
    return jnp.where(core == 0, (t % 4) * 8 + t // 4, t)


def route_kernel(tokens_hbm, params_hbm, own_ref, sent_hbm, tokens, params, logits, sent_ref, stats_ref, sem, out_sem, stats_sem):
    rows, width = tokens.shape
    slots = params.shape[1]
    n_tok, _, block = sent_ref.shape
    groups = sent_hbm.shape[0]
    each = n_tok // groups
    core = lax.axis_index("c")
    span = width // CHUNKS

    def copies(i):
        cut = pl.ds(i * span, span)
        return (
            pltpu.make_async_copy(tokens_hbm.at[:, cut], tokens.at[:, cut], sem.at[0, i]),
            pltpu.make_async_copy(params_hbm.at[cut, :], params.at[cut, :], sem.at[1, i]),
        )

    for i in range(CHUNKS):
        for copy in copies(i):
            copy.start()
    for i in range(CHUNKS):
        for copy in copies(i):
            copy.wait()
        part = jnp.dot(
            tokens[:, i * span : (i + 1) * span],
            params[i * span : (i + 1) * span, :],
            preferred_element_type=F32,
        )
        if i == 0:
            logits[...] = part
        else:
            logits[...] += part

    values = logits[...]
    row_max = jnp.max(values, axis=1, keepdims=True)
    row_exp = jnp.exp(values - row_max)
    row_total = jnp.sum(row_exp, axis=1, keepdims=True)
    own_ref[:rows, :] = row_exp.astype(BF16)
    lane = lax.broadcasted_iota(jnp.int32, (rows, 128), 1)
    pair = jnp.where(lane == 0, row_max, jnp.where(lane == 1, row_total, 0.0)).T[:8]
    terms = jnp.concatenate([term.astype(F32)[:2] for term in split3(pair)] + [jnp.zeros((2, rows), F32)], axis=0)
    own_ref[rows:, :] = jnp.concatenate([terms[:, i * slots : (i + 1) * slots] for i in range(rows // slots)], axis=0).astype(BF16)

    col_max = jnp.max(values, axis=0, keepdims=True)
    shifted = jnp.exp(values - col_max)
    col_total = jnp.sum(shifted, axis=0, keepdims=True)
    dispatch = shifted.astype(BF16).T
    terms = split3(col_max) + split3(col_total)
    stats = jnp.concatenate([t[:, i * block : (i + 1) * block].astype(F32) for t in terms for i in range(slots // block)]
                            + [jnp.zeros((STATS - len(terms) * (slots // block), block), F32)], axis=0).astype(BF16)
    stats_ref[...] = stats
    leave = [
        pltpu.make_async_copy(stats_ref, sent_hbm.at[g, pl.ds(each * slots, STATS)], stats_sem.at[g])
        for g in range(groups)
    ]
    for copy in leave:
        copy.start()
    per = n_tok // CHUNKS
    for i in range(CHUNKS):
        sums = jnp.dot(dispatch, tokens[:, i * span : (i + 1) * span], preferred_element_type=F32).astype(BF16)
        for j in range(per):
            t = i * per + j
            sent_ref[t] = sums[:, j * block : (j + 1) * block]
            at = place(t, core)
            copy = pltpu.make_async_copy(
                sent_ref.at[t], sent_hbm.at[at // each, pl.ds(pl.multiple_of((at % each) * slots, slots), slots)], out_sem.at[t]
            )
            copy.start()
            leave.append(copy)
    for copy in leave:
        copy.wait()


def route(tokens, params, n_tok):
    rows, width = tokens.shape
    slots = params.shape[1]
    return pl.pallas_call(
        route_kernel,
        out_shape=(
            jax.ShapeDtypeStruct((rows + STATS, slots), BF16),
            jax.ShapeDtypeStruct((4, n_tok // 4 * slots + STATS, width // n_tok), BF16),
        ),
        in_specs=[pl.BlockSpec(memory_space=pltpu.HBM)] * 2,
        out_specs=[pl.BlockSpec(memory_space=pltpu.VMEM), pl.BlockSpec(memory_space=pltpu.HBM)],
        scratch_shapes=[
            pltpu.VMEM((rows, width), BF16),
            pltpu.VMEM((width, slots), BF16),
            pltpu.VMEM((rows, slots), F32),
            pltpu.VMEM((n_tok, slots, width // n_tok), BF16),
            pltpu.VMEM((STATS, width // n_tok), BF16),
            pltpu.SemaphoreType.DMA((2, CHUNKS)),
            pltpu.SemaphoreType.DMA((n_tok,)),
            pltpu.SemaphoreType.DMA((4,)),
        ],
        compiler_params=pltpu.CompilerParams(vmem_limit_bytes=VMEM),
        cost_estimate=pl.CostEstimate(flops=4 * rows * width * slots, bytes_accessed=10 * 2**20, transcendentals=2 * rows * slots),
        name="route",
    )(tokens, params)


def scales(stats, cuts, block):
    senders = stats.shape[0]
    terms = [stats[:, i * cuts : (i + 1) * cuts] for i in range(6)]
    peaks = terms[0] + terms[1] + terms[2]
    totals = terms[3] + terms[4] + terms[5]
    peak = jnp.max(peaks, axis=0, keepdims=True)
    scale = jnp.exp(peaks - peak)
    total = jnp.sum(scale * totals, axis=0, keepdims=True)
    def columns(factor):
        return [
            jnp.concatenate([factor[:, c, :], jnp.zeros((block - senders, block), F32)], axis=0).T for c in range(cuts)
        ]
    return peak, total, scale, columns


def merge_kernel(came_ref, out_ref):
    senders, _, block = came_ref.shape
    each, total_rows, _ = out_ref.shape
    slots = total_rows - STATS
    cuts = slots // block
    peak, total, scale, columns = scales(came_ref[:, each * slots :, :].astype(F32), cuts, block)
    terms = split3(peak[0]) + split3(total[0])
    stats = jnp.concatenate([t.astype(F32) for t in terms] + [jnp.zeros((STATS - len(terms) * cuts, block), F32)], axis=0).astype(BF16)
    columns = columns(scale)
    for r in range(each):
        out_ref[r, slots:, :] = stats
    for c in range(cuts):
        factors = [jnp.broadcast_to(columns[c][:, t : t + 1], (block, block)) for t in range(senders)]
        for r in range(each):
            at = r * slots + c * block
            parts = [came_ref[t, at : at + block, :].astype(F32) * factors[t] for t in range(senders)]
            out_ref[r, c * block : (c + 1) * block, :] = sum(parts[1:], parts[0]).astype(BF16)


def merge(came, slots):
    senders, total_rows, block = came.shape
    each = total_rows // slots
    return pl.pallas_call(
        merge_kernel,
        out_shape=jax.ShapeDtypeStruct((each, slots + STATS, block), BF16),
        in_specs=[pl.BlockSpec(memory_space=pltpu.VMEM)],
        out_specs=pl.BlockSpec(memory_space=pltpu.VMEM),
        compiler_params=pltpu.CompilerParams(vmem_limit_bytes=32 * 2**20),
        cost_estimate=pl.CostEstimate(flops=2 * senders * each * slots * block, bytes_accessed=3 * 2**20, transcendentals=0),
        name="merge",
    )(came)


def expand_kernel(came_hbm, weight_hbm, out_hbm, came_ref, weight_ref, out_ref, came_sem, weight_sem, out_sem):
    senders, total_rows, block = came_ref.shape
    slots = total_rows - STATS
    experts, _, ff = weight_ref.shape
    cuts = slots // block
    per = slots // experts
    n_out, high, wide = out_ref.shape
    each = n_out // experts
    came_copy = pltpu.make_async_copy(came_hbm, came_ref, came_sem)
    weight_copies = [pltpu.make_async_copy(weight_hbm.at[e], weight_ref.at[e], weight_sem.at[e]) for e in range(experts)]
    out_copies = [
        pltpu.make_async_copy(out_ref.at[pl.ds(e * each, each)], out_hbm.at[pl.ds(e * each, each)], out_sem.at[e]) for e in range(experts)
    ]
    for copy in [came_copy] + weight_copies:
        copy.start()
    came_copy.wait()
    _, total, scale, columns = scales(came_ref[:, slots:, :].astype(F32), cuts, block)
    columns = columns(scale / total)
    parts = []
    for c in range(cuts):
        part = [came_ref[t, c * block : (c + 1) * block, :].astype(F32) * columns[c][:, t : t + 1] for t in range(senders)]
        parts.append(sum(part[1:], part[0]).astype(BF16))
    inputs = jnp.concatenate(parts, axis=0)
    for e in range(experts):
        weight_copies[e].wait()
        pre = jnp.dot(inputs[e * per : (e + 1) * per], weight_ref[e], preferred_element_type=F32).astype(BF16)
        for i in range(per // high):
            for j in range(ff // wide):
                out_ref[e * each + i * (ff // wide) + j] = pre[i * high : (i + 1) * high, j * wide : (j + 1) * wide]
        out_copies[e].start()
    for copy in out_copies:
        copy.wait()


def expand(came, weight_in, n_tok):
    senders, total_rows, block = came.shape
    slots = total_rows - STATS
    experts, _, ff = weight_in.shape
    high = 16
    out = (n_tok, high, slots * ff // (n_tok * high))
    return pl.pallas_call(
        expand_kernel,
        out_shape=jax.ShapeDtypeStruct(out, BF16),
        in_specs=[pl.BlockSpec(memory_space=pltpu.HBM)] * 2,
        out_specs=pl.BlockSpec(memory_space=pltpu.HBM),
        scratch_shapes=[
            pltpu.VMEM(came.shape, BF16),
            pltpu.VMEM(weight_in.shape, BF16),
            pltpu.VMEM(out, BF16),
            pltpu.SemaphoreType.DMA,
            pltpu.SemaphoreType.DMA((experts,)),
            pltpu.SemaphoreType.DMA((experts,)),
        ],
        compiler_params=pltpu.CompilerParams(vmem_limit_bytes=56 * 2**20),
        cost_estimate=pl.CostEstimate(flops=2 * slots * block * ff, bytes_accessed=4 * 2**20, transcendentals=0),
        name="expand",
    )(came, weight_in)


def produce_kernel(hidden_hbm, weight_hbm, out_ref, hidden_ref, weight_ref, hidden_sem, weight_sem):
    n_tok, high, wide = hidden_ref.shape
    experts, ff, block = weight_ref.shape
    per = out_ref.shape[0] // experts
    halves, chunks = ff // wide, per // high
    each = n_tok // experts
    copies = [
        (
            pltpu.make_async_copy(hidden_hbm.at[pl.ds(e * each, each)], hidden_ref.at[pl.ds(e * each, each)], hidden_sem.at[e]),
            pltpu.make_async_copy(weight_hbm.at[e], weight_ref.at[e], weight_sem.at[e]),
        )
        for e in range(experts)
    ]
    for pair in copies:
        for copy in pair:
            copy.start()
    for e in range(experts):
        for copy in copies[e]:
            copy.wait()
        total = None
        for j in range(halves):
            rows = jnp.concatenate([hidden_ref[e * each + i * halves + j] for i in range(chunks)], axis=0)
            part = jnp.dot(rows, weight_ref[e, j * wide : (j + 1) * wide, :], preferred_element_type=F32)
            total = part if total is None else total + part
        out_ref[e * per : (e + 1) * per, :] = total.astype(BF16)


def produce(hidden, weight_out):
    n_tok, high, wide = hidden.shape
    experts, ff, block = weight_out.shape
    slots = n_tok * high * wide // ff
    return pl.pallas_call(
        produce_kernel,
        out_shape=jax.ShapeDtypeStruct((slots, block), BF16),
        in_specs=[pl.BlockSpec(memory_space=pltpu.HBM)] * 2,
        out_specs=pl.BlockSpec(memory_space=pltpu.VMEM),
        scratch_shapes=[
            pltpu.VMEM(hidden.shape, BF16),
            pltpu.VMEM(weight_out.shape, BF16),
            pltpu.SemaphoreType.DMA((experts,)),
            pltpu.SemaphoreType.DMA((experts,)),
        ],
        compiler_params=pltpu.CompilerParams(vmem_limit_bytes=57 * 2**20),
        cost_estimate=pl.CostEstimate(flops=2 * slots * ff * block, bytes_accessed=3 * 2**20, transcendentals=0),
        name="produce",
    )(hidden, weight_out)


def combine_kernel(own_ref, twin_ref, near_ref, far_ref, rest_ref, out_ref):
    total_rows, slots = own_ref.shape
    rows = total_rows - STATS
    here, core = lax.axis_index("zh"), lax.axis_index("c")
    n_hi = out_ref.shape[1] // slots // 2
    step = 2 * core - 1
    blocks = [
        (own_ref, 0, 0, 0), (twin_ref, 0, 0, 1), (near_ref, 0, 1, 0), (near_ref, total_rows, 1, 1), (far_ref, 0, 2, 0),
        (rest_ref, 0, -1, 1), (rest_ref, total_rows, -1, 0), (rest_ref, 2 * total_rows, -2, 1),
    ]
    peaks, totals = [], []
    for ref, at, _, _ in blocks:
        stats = ref[at + rows : at + total_rows, :].astype(F32)
        stats = jnp.concatenate([stats[i * 8 : (i + 1) * 8] for i in range(rows // slots)], axis=1)
        joined = stats[0:2] + stats[2:4] + stats[4:6]
        peaks.append(joined[0:1])
        totals.append(joined[1:2])
    peaks, totals = jnp.concatenate(peaks, axis=0), jnp.concatenate(totals, axis=0)
    scale = jnp.exp(peaks - jnp.max(peaks, axis=0, keepdims=True))
    scale = scale / jnp.sum(scale * totals, axis=0, keepdims=True)
    scale = jnp.concatenate([scale, jnp.zeros((128 - scale.shape[0], rows), F32)], axis=0).T
    for k, (ref, at, steps, flip) in enumerate(blocks):
        z = lax.rem(here + steps * step + 2 * n_hi, n_hi)
        e = 2 * z + (1 - core if flip else core)
        at_out = pl.ds(pl.multiple_of(e * slots, slots), slots)
        out_ref[:, at_out] = (ref[at : at + rows, :].astype(F32) * scale[:, k : k + 1]).astype(BF16)


def combine(own, twin, near, far, rest, n_exp):
    total_rows, slots = own.shape
    rows = total_rows - STATS
    return pl.pallas_call(
        combine_kernel,
        out_shape=jax.ShapeDtypeStruct((rows, n_exp * slots), BF16),
        in_specs=[pl.BlockSpec(memory_space=pltpu.VMEM)] * 5,
        out_specs=pl.BlockSpec(memory_space=pltpu.VMEM),
        compiler_params=pltpu.CompilerParams(vmem_limit_bytes=32 * 2**20),
        cost_estimate=pl.CostEstimate(flops=2 * n_exp * rows * slots, bytes_accessed=4 * 2**20, transcendentals=0),
        name="combine",
    )(own, twin, near, far, rest)


def final_kernel(weights_ref, pieces_hbm, out_ref, values, sem):
    rows, total = weights_ref.shape
    n_tok, slots, block = pieces_hbm.shape
    n_exp = total // slots
    quarter = n_tok // n_exp
    here, core = lax.axis_index("zh"), lax.axis_index("c")
    copies = []
    for e in range(n_exp):
        first = ((e // 2 + here) % 4) * 8 + (e % 2) * 4
        for q in range(quarter):
            into = values.at[pl.ds(e * slots, slots), pl.ds(q * block, block)]
            copies.append(pltpu.make_async_copy(pieces_hbm.at[place(first + q, core)], into, sem.at[e * quarter + q]))
            copies[-1].start()
    step = 2
    result = None
    for e in range(0, n_exp, step):
        for copy in copies[e * quarter : (e + step) * quarter]:
            copy.wait()
        cut = slice(e * slots, (e + step) * slots)
        part = jnp.dot(weights_ref[:, cut], values[cut, :], preferred_element_type=F32)
        result = part if result is None else result + part
    out_ref[...] = result.astype(BF16)


def final(weights, pieces):
    rows, total = weights.shape
    n_tok, slots, block = pieces.shape
    columns = n_tok * slots // total * block
    return pl.pallas_call(
        final_kernel,
        out_shape=jax.ShapeDtypeStruct((rows, columns), BF16),
        in_specs=[pl.BlockSpec(memory_space=pltpu.VMEM), pl.BlockSpec(memory_space=pltpu.HBM)],
        out_specs=pl.BlockSpec(memory_space=pltpu.VMEM),
        scratch_shapes=[pltpu.VMEM((total, columns), BF16), pltpu.SemaphoreType.DMA((n_tok,))],
        compiler_params=pltpu.CompilerParams(vmem_limit_bytes=50 * 2**20),
        cost_estimate=pl.CostEstimate(flops=2 * rows * total * columns, bytes_accessed=5 * 2**20, transcendentals=0),
        name="final",
    )(weights, pieces)


def flat(x, zl, y, zh, c):
    return (((x * 2 + zl) * 4 + y) * 4 + zh) * 2 + c


def exchange_groups():
    four, eight = [], []
    for zh in range(4):
        four += [[flat(x, zl, y, zh, 0) for y in range(4)] for x in range(4) for zl in range(2)]
        four += [[flat(x, zl, y, zh, 1) for x in range(4)] for zl in range(2) for y in range(4)]
        eight += [[flat(x, zl, y, zh, 0) for x in range(4) for zl in range(2)] for y in range(4)]
        eight += [[flat(x, zl, y, zh, 1) for zl in range(2) for y in range(4)] for x in range(4)]
    return four, eight


def local(tokens, slot_params, weight_in, weight_out):
    n_tok, n_exp, n_hi = lax.axis_size(TOK), lax.axis_size(EXP), lax.axis_size("zh")
    block, slots = weight_in.shape[1], slot_params.shape[1]
    four, eight = exchange_groups()
    swap = [(0, 1), (1, 0)]
    along = [
        (2 * z + c, 2 * ((z + (1 if c == 0 else -1)) % n_hi) + c) for z in range(n_hi) for c in range(2)
    ]
    own, sent = route(tokens, slot_params, n_tok)

    twin = lax.ppermute(own, "c", swap)
    near = lax.ppermute(jnp.concatenate([own, twin]), EXP, along)
    came = lax.all_to_all(sent, ALL, 0, 0, axis_index_groups=four, tiled=True)
    came, near = lax.optimization_barrier((came, near))
    came = lax.all_to_all(merge(came, slots), ALL, 0, 0, axis_index_groups=eight, tiled=True)

    pre = lax.all_to_all(expand(came, weight_in, n_tok), TOK, 0, 0, tiled=True)
    pre = jnp.sum(pre.astype(F32), axis=0)
    hidden = jax.nn.gelu(pre, approximate=False).astype(BF16)
    hidden = lax.all_to_all(
        jnp.broadcast_to(hidden[None], (n_tok,) + hidden.shape), TOK, 0, 0, tiled=True
    )
    produced = produce(hidden, weight_out)

    moves = [
        (flat(x, zl, y, zh, c), flat((x + zh) % 4, c, y, x, zl))
        for x in range(4) for zl in range(2) for y in range(4) for zh in range(4) for c in range(2)
    ]
    piece = lax.ppermute(produced, ALL, moves)
    pieces = jnp.broadcast_to(piece[None], (8,) + piece.shape)
    pieces = lax.all_to_all(pieces, ALL, 0, 0, axis_index_groups=eight, tiled=True)
    pieces, forward = lax.optimization_barrier((pieces, near[: own.shape[0]]))
    far = lax.ppermute(forward, EXP, along)
    rest = lax.ppermute(jnp.concatenate([near, far]), "c", swap)
    pieces = jnp.broadcast_to(pieces[None], (4,) + pieces.shape)
    pieces = lax.all_to_all(pieces, ALL, 0, 0, axis_index_groups=four, tiled=True)
    return final(combine(own, twin, near, far, rest, n_exp), pieces.reshape(n_tok, slots, block))


def solution(mesh):
    mesh = Mesh(mesh.devices.reshape(4, 2, 4, 4, 2), ALL)
    placed = (P(TOK, None), P(None, EXP), P(EXP, TOK, None), P(EXP, None, TOK))
    return jax.shard_map(
        local, mesh=mesh, in_specs=placed, out_specs=P(TOK, EXP), check_vma=False
    )
```

```python
import jax
import jax.numpy as jnp
from jax import lax
from jax.experimental import pallas as pl
from jax.experimental.pallas import tpu as pltpu
from jax.sharding import Mesh, PartitionSpec as P

BF16, F32 = jnp.bfloat16, jnp.float32
TOK, EXP = ("x", "zl", "y"), ("zh", "c")
ALL = TOK + EXP
CHUNKS = 4
STATS = 16
VMEM = 60 * 2**20


def split3(value):
    head = value.astype(BF16)
    rest = value - head.astype(F32)
    mid = rest.astype(BF16)
    return [head, mid, (rest - mid.astype(F32)).astype(BF16)]


def join3(parts):
    return parts[0].astype(F32) + parts[1].astype(F32) + parts[2].astype(F32)


def place(t, core):
    return jnp.where(core == 0, (t % 4) * 8 + (t // 4) % 2 * 4 + t // 8, t)


def route_kernel(tokens_hbm, params_hbm, own_ref, sent_hbm, tokens, params, logits, sent_ref, stats_ref, sem, out_sem, stats_sem):
    rows, width = tokens.shape
    slots = params.shape[1]
    n_tok, _, block = sent_ref.shape
    groups = sent_hbm.shape[0]
    each = n_tok // groups
    core = lax.axis_index("c")
    span = width // CHUNKS

    def copies(i):
        cut = pl.ds(i * span, span)
        return (
            pltpu.make_async_copy(tokens_hbm.at[:, cut], tokens.at[:, cut], sem.at[0, i]),
            pltpu.make_async_copy(params_hbm.at[cut, :], params.at[cut, :], sem.at[1, i]),
        )

    for i in range(CHUNKS):
        for copy in copies(i):
            copy.start()
    for i in range(CHUNKS):
        for copy in copies(i):
            copy.wait()
        part = jnp.dot(
            tokens[:, i * span : (i + 1) * span],
            params[i * span : (i + 1) * span, :],
            preferred_element_type=F32,
        )
        if i == 0:
            logits[...] = part
        else:
            logits[...] += part

    values = logits[...]
    row_max = jnp.max(values, axis=1, keepdims=True)
    row_exp = jnp.exp(values - row_max)
    row_total = jnp.sum(row_exp, axis=1, keepdims=True)
    own_ref[:rows, :] = row_exp.astype(BF16)
    lane = lax.broadcasted_iota(jnp.int32, (rows, 128), 1)
    pair = jnp.where(lane == 0, row_max, jnp.where(lane == 1, row_total, 0.0)).T[:8]
    terms = jnp.concatenate([term.astype(F32)[:2] for term in split3(pair)] + [jnp.zeros((2, rows), F32)], axis=0)
    own_ref[rows:, :] = jnp.concatenate([terms[:, i * slots : (i + 1) * slots] for i in range(rows // slots)], axis=0).astype(BF16)

    col_max = jnp.max(values, axis=0, keepdims=True)
    shifted = jnp.exp(values - col_max)
    col_total = jnp.sum(shifted, axis=0, keepdims=True)
    dispatch = shifted.astype(BF16).T
    terms = split3(col_max) + split3(col_total)
    stats = jnp.concatenate([t[:, i * block : (i + 1) * block].astype(F32) for t in terms for i in range(slots // block)]
                            + [jnp.zeros((STATS - len(terms) * (slots // block), block), F32)], axis=0).astype(BF16)
    stats_ref[...] = stats
    leave = [
        pltpu.make_async_copy(stats_ref, sent_hbm.at[g, pl.ds(each * slots, STATS)], stats_sem.at[g])
        for g in range(groups)
    ]
    for copy in leave:
        copy.start()
    per = n_tok // CHUNKS
    for i in range(CHUNKS):
        sums = jnp.dot(dispatch, tokens[:, i * span : (i + 1) * span], preferred_element_type=F32).astype(BF16)
        for j in range(per):
            t = i * per + j
            sent_ref[t] = sums[:, j * block : (j + 1) * block]
            at = place(t, core)
            copy = pltpu.make_async_copy(
                sent_ref.at[t], sent_hbm.at[at // each, pl.ds(pl.multiple_of((at % each) * slots, slots), slots)], out_sem.at[t]
            )
            copy.start()
            leave.append(copy)
    for copy in leave:
        copy.wait()


def route(tokens, params, n_tok):
    rows, width = tokens.shape
    slots = params.shape[1]
    return pl.pallas_call(
        route_kernel,
        out_shape=(
            jax.ShapeDtypeStruct((rows + STATS, slots), BF16),
            jax.ShapeDtypeStruct((4, n_tok // 4 * slots + STATS, width // n_tok), BF16),
        ),
        in_specs=[pl.BlockSpec(memory_space=pltpu.HBM)] * 2,
        out_specs=[pl.BlockSpec(memory_space=pltpu.VMEM), pl.BlockSpec(memory_space=pltpu.HBM)],
        scratch_shapes=[
            pltpu.VMEM((rows, width), BF16),
            pltpu.VMEM((width, slots), BF16),
            pltpu.VMEM((rows, slots), F32),
            pltpu.VMEM((n_tok, slots, width // n_tok), BF16),
            pltpu.VMEM((STATS, width // n_tok), BF16),
            pltpu.SemaphoreType.DMA((2, CHUNKS)),
            pltpu.SemaphoreType.DMA((n_tok,)),
            pltpu.SemaphoreType.DMA((4,)),
        ],
        compiler_params=pltpu.CompilerParams(vmem_limit_bytes=VMEM),
        cost_estimate=pl.CostEstimate(flops=4 * rows * width * slots, bytes_accessed=10 * 2**20, transcendentals=2 * rows * slots),
        name="route",
    )(tokens, params)


def scales(stats, cuts, block):
    senders = stats.shape[0]
    terms = [stats[:, i * cuts : (i + 1) * cuts] for i in range(6)]
    peaks = terms[0] + terms[1] + terms[2]
    totals = terms[3] + terms[4] + terms[5]
    peak = jnp.max(peaks, axis=0, keepdims=True)
    scale = jnp.exp(peaks - peak)
    total = jnp.sum(scale * totals, axis=0, keepdims=True)
    def columns(factor):
        return [
            jnp.concatenate([factor[:, c, :], jnp.zeros((block - senders, block), F32)], axis=0).T for c in range(cuts)
        ]
    return peak, total, scale, columns


def merge_kernel(came_ref, out_ref):
    senders, _, block = came_ref.shape
    each, total_rows, _ = out_ref.shape
    slots = total_rows - STATS
    cuts = slots // block
    peak, total, scale, columns = scales(came_ref[:, each * slots :, :].astype(F32), cuts, block)
    terms = split3(peak[0]) + split3(total[0])
    stats = jnp.concatenate([t.astype(F32) for t in terms] + [jnp.zeros((STATS - len(terms) * cuts, block), F32)], axis=0).astype(BF16)
    columns = columns(scale)
    for r in range(each):
        out_ref[r, slots:, :] = stats
    for c in range(cuts):
        factors = [jnp.broadcast_to(columns[c][:, t : t + 1], (block, block)) for t in range(senders)]
        for r in range(each):
            at = r * slots + c * block
            parts = [came_ref[t, at : at + block, :].astype(F32) * factors[t] for t in range(senders)]
            out_ref[r, c * block : (c + 1) * block, :] = sum(parts[1:], parts[0]).astype(BF16)


def merge(came, slots):
    senders, total_rows, block = came.shape
    each = total_rows // slots
    return pl.pallas_call(
        merge_kernel,
        out_shape=jax.ShapeDtypeStruct((each, slots + STATS, block), BF16),
        in_specs=[pl.BlockSpec(memory_space=pltpu.VMEM)],
        out_specs=pl.BlockSpec(memory_space=pltpu.VMEM),
        compiler_params=pltpu.CompilerParams(vmem_limit_bytes=32 * 2**20),
        cost_estimate=pl.CostEstimate(flops=2 * senders * each * slots * block, bytes_accessed=3 * 2**20, transcendentals=0),
        name="merge",
    )(came)


def expand_kernel(came_hbm, weight_hbm, out_hbm, came_ref, weight_ref, out_ref, came_sem, weight_sem, out_sem):
    senders, total_rows, block = came_ref.shape
    slots = total_rows - STATS
    experts, _, ff = weight_ref.shape
    cuts = slots // block
    per = slots // experts
    n_out, high, wide = out_ref.shape
    each = n_out // experts
    came_copy = pltpu.make_async_copy(came_hbm, came_ref, came_sem)
    weight_copies = [pltpu.make_async_copy(weight_hbm.at[e], weight_ref.at[e], weight_sem.at[e]) for e in range(experts)]
    out_copies = [
        pltpu.make_async_copy(out_ref.at[pl.ds(e * each, each)], out_hbm.at[pl.ds(e * each, each)], out_sem.at[e]) for e in range(experts)
    ]
    for copy in [came_copy] + weight_copies:
        copy.start()
    came_copy.wait()
    _, total, scale, columns = scales(came_ref[:, slots:, :].astype(F32), cuts, block)
    columns = columns(scale / total)
    parts = []
    for c in range(cuts):
        part = [came_ref[t, c * block : (c + 1) * block, :].astype(F32) * columns[c][:, t : t + 1] for t in range(senders)]
        parts.append(sum(part[1:], part[0]).astype(BF16))
    inputs = jnp.concatenate(parts, axis=0)
    for e in range(experts):
        weight_copies[e].wait()
        pre = jnp.dot(inputs[e * per : (e + 1) * per], weight_ref[e], preferred_element_type=F32).astype(BF16)
        for i in range(per // high):
            for j in range(ff // wide):
                out_ref[e * each + i * (ff // wide) + j] = pre[i * high : (i + 1) * high, j * wide : (j + 1) * wide]
        out_copies[e].start()
    for copy in out_copies:
        copy.wait()


def expand(came, weight_in, n_tok):
    senders, total_rows, block = came.shape
    slots = total_rows - STATS
    experts, _, ff = weight_in.shape
    high = 16
    out = (n_tok, high, slots * ff // (n_tok * high))
    return pl.pallas_call(
        expand_kernel,
        out_shape=jax.ShapeDtypeStruct(out, BF16),
        in_specs=[pl.BlockSpec(memory_space=pltpu.HBM)] * 2,
        out_specs=pl.BlockSpec(memory_space=pltpu.HBM),
        scratch_shapes=[
            pltpu.VMEM(came.shape, BF16),
            pltpu.VMEM(weight_in.shape, BF16),
            pltpu.VMEM(out, BF16),
            pltpu.SemaphoreType.DMA,
            pltpu.SemaphoreType.DMA((experts,)),
            pltpu.SemaphoreType.DMA((experts,)),
        ],
        compiler_params=pltpu.CompilerParams(vmem_limit_bytes=56 * 2**20),
        cost_estimate=pl.CostEstimate(flops=2 * slots * block * ff, bytes_accessed=4 * 2**20, transcendentals=0),
        name="expand",
    )(came, weight_in)


def produce_kernel(hidden_hbm, weight_hbm, out_ref, hidden_ref, weight_ref, hidden_sem, weight_sem):
    n_tok, high, wide = hidden_ref.shape
    experts, ff, block = weight_ref.shape
    per = out_ref.shape[0] // experts
    halves, chunks = ff // wide, per // high
    each = n_tok // experts
    copies = [
        (
            pltpu.make_async_copy(hidden_hbm.at[pl.ds(e * each, each)], hidden_ref.at[pl.ds(e * each, each)], hidden_sem.at[e]),
            pltpu.make_async_copy(weight_hbm.at[e], weight_ref.at[e], weight_sem.at[e]),
        )
        for e in range(experts)
    ]
    for pair in copies:
        for copy in pair:
            copy.start()
    for e in range(experts):
        for copy in copies[e]:
            copy.wait()
        total = None
        for j in range(halves):
            rows = jnp.concatenate([hidden_ref[e * each + i * halves + j] for i in range(chunks)], axis=0)
            part = jnp.dot(rows, weight_ref[e, j * wide : (j + 1) * wide, :], preferred_element_type=F32)
            total = part if total is None else total + part
        out_ref[e * per : (e + 1) * per, :] = total.astype(BF16)


def produce(hidden, weight_out):
    n_tok, high, wide = hidden.shape
    experts, ff, block = weight_out.shape
    slots = n_tok * high * wide // ff
    return pl.pallas_call(
        produce_kernel,
        out_shape=jax.ShapeDtypeStruct((slots, block), BF16),
        in_specs=[pl.BlockSpec(memory_space=pltpu.HBM)] * 2,
        out_specs=pl.BlockSpec(memory_space=pltpu.VMEM),
        scratch_shapes=[
            pltpu.VMEM(hidden.shape, BF16),
            pltpu.VMEM(weight_out.shape, BF16),
            pltpu.SemaphoreType.DMA((experts,)),
            pltpu.SemaphoreType.DMA((experts,)),
        ],
        compiler_params=pltpu.CompilerParams(vmem_limit_bytes=57 * 2**20),
        cost_estimate=pl.CostEstimate(flops=2 * slots * ff * block, bytes_accessed=3 * 2**20, transcendentals=0),
        name="produce",
    )(hidden, weight_out)


def spread_kernel(piece_ref, out_hbm, sem):
    copies = [pltpu.make_async_copy(piece_ref, out_hbm.at[t], sem.at[t]) for t in range(out_hbm.shape[0])]
    for copy in copies:
        copy.start()
    for copy in copies:
        copy.wait()


def spread(piece, n_tok):
    return pl.pallas_call(
        spread_kernel,
        out_shape=jax.ShapeDtypeStruct((n_tok,) + piece.shape, BF16),
        in_specs=[pl.BlockSpec(memory_space=pltpu.VMEM)],
        out_specs=pl.BlockSpec(memory_space=pltpu.HBM),
        scratch_shapes=[pltpu.SemaphoreType.DMA((n_tok,))],
        compiler_params=pltpu.CompilerParams(vmem_limit_bytes=48 * 2**20),
        cost_estimate=pl.CostEstimate(flops=0, bytes_accessed=2 * 2**20, transcendentals=0),
        name="spread",
    )(piece)


def combine_kernel(own_ref, twin_ref, near_ref, far_ref, rest_ref, out_ref):
    total_rows, slots = own_ref.shape
    rows = total_rows - STATS
    here, core = lax.axis_index("zh"), lax.axis_index("c")
    n_hi = out_ref.shape[1] // slots // 2
    step = 2 * core - 1
    blocks = [
        (own_ref, 0, 0, 0), (twin_ref, 0, 0, 1), (near_ref, 0, 1, 0), (near_ref, total_rows, 1, 1), (far_ref, 0, 2, 0),
        (rest_ref, 0, -1, 1), (rest_ref, total_rows, -1, 0), (rest_ref, 2 * total_rows, -2, 1),
    ]
    peaks, totals = [], []
    for ref, at, _, _ in blocks:
        stats = ref[at + rows : at + total_rows, :].astype(F32)
        stats = jnp.concatenate([stats[i * 8 : (i + 1) * 8] for i in range(rows // slots)], axis=1)
        joined = stats[0:2] + stats[2:4] + stats[4:6]
        peaks.append(joined[0:1])
        totals.append(joined[1:2])
    peaks, totals = jnp.concatenate(peaks, axis=0), jnp.concatenate(totals, axis=0)
    scale = jnp.exp(peaks - jnp.max(peaks, axis=0, keepdims=True))
    scale = scale / jnp.sum(scale * totals, axis=0, keepdims=True)
    scale = jnp.concatenate([scale, jnp.zeros((128 - scale.shape[0], rows), F32)], axis=0).T
    for k, (ref, at, steps, flip) in enumerate(blocks):
        z = lax.rem(here + steps * step + 2 * n_hi, n_hi)
        e = 2 * z + (1 - core if flip else core)
        at_out = pl.ds(pl.multiple_of(e * slots, slots), slots)
        out_ref[:, at_out] = (ref[at : at + rows, :].astype(F32) * scale[:, k : k + 1]).astype(BF16)


def combine(own, twin, near, far, rest, n_exp):
    total_rows, slots = own.shape
    rows = total_rows - STATS
    return pl.pallas_call(
        combine_kernel,
        out_shape=jax.ShapeDtypeStruct((rows, n_exp * slots), BF16),
        in_specs=[pl.BlockSpec(memory_space=pltpu.VMEM)] * 5,
        out_specs=pl.BlockSpec(memory_space=pltpu.VMEM),
        compiler_params=pltpu.CompilerParams(vmem_limit_bytes=32 * 2**20),
        cost_estimate=pl.CostEstimate(flops=2 * n_exp * rows * slots, bytes_accessed=4 * 2**20, transcendentals=0),
        name="combine",
    )(own, twin, near, far, rest)


def final_kernel(weights_ref, pieces_hbm, out_ref, values, sem):
    rows, total = weights_ref.shape
    n_tok, slots, block = pieces_hbm.shape
    n_exp = total // slots
    quarter = n_tok // n_exp
    here = lax.axis_index("zh")
    copies = []
    for e in range(n_exp):
        first = ((e // 2 + here) % 4) * 8 + (e % 2) * 4
        for q in range(quarter):
            into = values.at[pl.ds(e * slots, slots), pl.ds(q * block, block)]
            copies.append(pltpu.make_async_copy(pieces_hbm.at[first + q], into, sem.at[e * quarter + q]))
            copies[-1].start()
    step = 2
    result = None
    for e in range(0, n_exp, step):
        for copy in copies[e * quarter : (e + step) * quarter]:
            copy.wait()
        cut = slice(e * slots, (e + step) * slots)
        part = jnp.dot(weights_ref[:, cut], values[cut, :], preferred_element_type=F32)
        result = part if result is None else result + part
    out_ref[...] = result.astype(BF16)


def final(weights, pieces):
    rows, total = weights.shape
    n_tok, slots, block = pieces.shape
    columns = n_tok * slots // total * block
    return pl.pallas_call(
        final_kernel,
        out_shape=jax.ShapeDtypeStruct((rows, columns), BF16),
        in_specs=[pl.BlockSpec(memory_space=pltpu.VMEM), pl.BlockSpec(memory_space=pltpu.HBM)],
        out_specs=pl.BlockSpec(memory_space=pltpu.VMEM),
        scratch_shapes=[pltpu.VMEM((total, columns), BF16), pltpu.SemaphoreType.DMA((n_tok,))],
        compiler_params=pltpu.CompilerParams(vmem_limit_bytes=50 * 2**20),
        cost_estimate=pl.CostEstimate(flops=2 * rows * total * columns, bytes_accessed=5 * 2**20, transcendentals=0),
        name="final",
    )(weights, pieces)


def flat(x, zl, y, zh, c):
    return (((x * 2 + zl) * 4 + y) * 4 + zh) * 2 + c


def exchange_groups():
    four, eight = [], []
    for zh in range(4):
        four += [[flat(x, zl, y, zh, 0) for y in range(4)] for x in range(4) for zl in range(2)]
        four += [[flat(x, zl, y, zh, 1) for x in range(4)] for zl in range(2) for y in range(4)]
        eight += [[flat(x, zl, y, zh, 0) for zl in range(2) for x in range(4)] for y in range(4)]
        eight += [[flat(x, zl, y, zh, 1) for zl in range(2) for y in range(4)] for x in range(4)]
    return four, eight


def local(tokens, slot_params, weight_in, weight_out):
    n_tok, n_exp, n_hi = lax.axis_size(TOK), lax.axis_size(EXP), lax.axis_size("zh")
    block, slots = weight_in.shape[1], slot_params.shape[1]
    four, eight = exchange_groups()
    swap = [(0, 1), (1, 0)]
    along = [
        (2 * z + c, 2 * ((z + (1 if c == 0 else -1)) % n_hi) + c) for z in range(n_hi) for c in range(2)
    ]
    own, sent = route(tokens, slot_params, n_tok)

    twin = lax.ppermute(own, "c", swap)
    near = lax.ppermute(jnp.concatenate([own, twin]), EXP, along)
    came = lax.all_to_all(sent, ALL, 0, 0, axis_index_groups=four, tiled=True)
    came, near = lax.optimization_barrier((came, near))
    came = lax.all_to_all(merge(came, slots), ALL, 0, 0, axis_index_groups=eight, tiled=True)

    pre = lax.all_to_all(expand(came, weight_in, n_tok), TOK, 0, 0, tiled=True)
    pre = jnp.sum(pre.astype(F32), axis=0)
    hidden = jax.nn.gelu(pre, approximate=False).astype(BF16)
    hidden = lax.all_to_all(
        jnp.broadcast_to(hidden[None], (n_tok,) + hidden.shape), TOK, 0, 0, tiled=True
    )
    produced = produce(hidden, weight_out)

    moves = [
        (flat(x, zl, y, zh, c), flat((x + zh) % 4, c, y, x, zl))
        for x in range(4) for zl in range(2) for y in range(4) for zh in range(4) for c in range(2)
    ]
    piece = lax.ppermute(produced, ALL, moves)
    piece, forward = lax.optimization_barrier((piece, near[: own.shape[0]]))
    far = lax.ppermute(forward, EXP, along)
    rest = lax.ppermute(jnp.concatenate([near, far]), "c", swap)
    pieces = lax.all_to_all(spread(piece, n_tok), TOK, 0, 0, tiled=True)
    return final(combine(own, twin, near, far, rest, n_exp), pieces)


def solution(mesh):
    mesh = Mesh(mesh.devices.reshape(4, 2, 4, 4, 2), ALL)
    placed = (P(TOK, None), P(None, EXP), P(EXP, TOK, None), P(EXP, None, TOK))
    return jax.shard_map(
        local, mesh=mesh, in_specs=placed, out_specs=P(TOK, EXP), check_vma=False
    )
```

```python
import jax
import jax.numpy as jnp
from jax import lax
from jax.experimental import pallas as pl
from jax.experimental.pallas import tpu as pltpu
from jax.sharding import Mesh, PartitionSpec as P

BF16, F32 = jnp.bfloat16, jnp.float32
TOK, EXP = ("x", "zl", "y"), ("zh", "c")
ALL = TOK + EXP
CHUNKS = 4
STATS = 16
VMEM = 60 * 2**20


def split3(value):
    head = value.astype(BF16)
    rest = value - head.astype(F32)
    mid = rest.astype(BF16)
    return [head, mid, (rest - mid.astype(F32)).astype(BF16)]


def join3(parts):
    return parts[0].astype(F32) + parts[1].astype(F32) + parts[2].astype(F32)


def place(t, core):
    return jnp.where(core == 0, (t % 4) * 8 + t // 4, t)


def route_kernel(tokens_hbm, params_hbm, own_ref, sent_hbm, tokens, params, logits, sent_ref, stats_ref, sem, out_sem, stats_sem):
    rows, width = tokens.shape
    slots = params.shape[1]
    n_tok, _, block = sent_ref.shape
    groups = sent_hbm.shape[0]
    each = n_tok // groups
    core = lax.axis_index("c")
    span = width // CHUNKS

    def copies(i):
        cut = pl.ds(i * span, span)
        return (
            pltpu.make_async_copy(tokens_hbm.at[:, cut], tokens.at[:, cut], sem.at[0, i]),
            pltpu.make_async_copy(params_hbm.at[cut, :], params.at[cut, :], sem.at[1, i]),
        )

    for i in range(CHUNKS):
        for copy in copies(i):
            copy.start()
    for i in range(CHUNKS):
        for copy in copies(i):
            copy.wait()
        part = jnp.dot(
            tokens[:, i * span : (i + 1) * span],
            params[i * span : (i + 1) * span, :],
            preferred_element_type=F32,
        )
        if i == 0:
            logits[...] = part
        else:
            logits[...] += part

    values = logits[...]
    row_max = jnp.max(values, axis=1, keepdims=True)
    row_exp = jnp.exp(values - row_max)
    row_total = jnp.sum(row_exp, axis=1, keepdims=True)
    own_ref[:rows, :] = row_exp.astype(BF16)
    lane = lax.broadcasted_iota(jnp.int32, (rows, 128), 1)
    pair = jnp.where(lane == 0, row_max, jnp.where(lane == 1, row_total, 0.0)).T[:8]
    terms = jnp.concatenate([term.astype(F32)[:2] for term in split3(pair)] + [jnp.zeros((2, rows), F32)], axis=0)
    own_ref[rows:, :] = jnp.concatenate([terms[:, i * slots : (i + 1) * slots] for i in range(rows // slots)], axis=0).astype(BF16)

    col_max = jnp.max(values, axis=0, keepdims=True)
    shifted = jnp.exp(values - col_max)
    col_total = jnp.sum(shifted, axis=0, keepdims=True)
    dispatch = shifted.astype(BF16).T
    terms = split3(col_max) + split3(col_total)
    stats = jnp.concatenate([t[:, i * block : (i + 1) * block].astype(F32) for t in terms for i in range(slots // block)]
                            + [jnp.zeros((STATS - len(terms) * (slots // block), block), F32)], axis=0).astype(BF16)
    stats_ref[...] = stats
    leave = [
        pltpu.make_async_copy(stats_ref, sent_hbm.at[g, pl.ds(each * slots, STATS)], stats_sem.at[g])
        for g in range(groups)
    ]
    for copy in leave:
        copy.start()
    per = n_tok // CHUNKS
    for i in range(CHUNKS):
        sums = jnp.dot(dispatch, tokens[:, i * span : (i + 1) * span], preferred_element_type=F32).astype(BF16)
        for j in range(per):
            t = i * per + j
            sent_ref[t] = sums[:, j * block : (j + 1) * block]
            at = place(t, core)
            copy = pltpu.make_async_copy(
                sent_ref.at[t], sent_hbm.at[at // each, pl.ds(pl.multiple_of((at % each) * slots, slots), slots)], out_sem.at[t]
            )
            copy.start()
            leave.append(copy)
    for copy in leave:
        copy.wait()


def route(tokens, params, n_tok):
    rows, width = tokens.shape
    slots = params.shape[1]
    return pl.pallas_call(
        route_kernel,
        out_shape=(
            jax.ShapeDtypeStruct((rows + STATS, slots), BF16),
            jax.ShapeDtypeStruct((4, n_tok // 4 * slots + STATS, width // n_tok), BF16),
        ),
        in_specs=[pl.BlockSpec(memory_space=pltpu.HBM)] * 2,
        out_specs=[pl.BlockSpec(memory_space=pltpu.VMEM), pl.BlockSpec(memory_space=pltpu.HBM)],
        scratch_shapes=[
            pltpu.VMEM((rows, width), BF16),
            pltpu.VMEM((width, slots), BF16),
            pltpu.VMEM((rows, slots), F32),
            pltpu.VMEM((n_tok, slots, width // n_tok), BF16),
            pltpu.VMEM((STATS, width // n_tok), BF16),
            pltpu.SemaphoreType.DMA((2, CHUNKS)),
            pltpu.SemaphoreType.DMA((n_tok,)),
            pltpu.SemaphoreType.DMA((4,)),
        ],
        compiler_params=pltpu.CompilerParams(vmem_limit_bytes=VMEM),
        cost_estimate=pl.CostEstimate(flops=4 * rows * width * slots, bytes_accessed=10 * 2**20, transcendentals=2 * rows * slots),
        name="route",
    )(tokens, params)


def scales(stats, cuts, block):
    senders = stats.shape[0]
    terms = [stats[:, i * cuts : (i + 1) * cuts] for i in range(6)]
    peaks = terms[0] + terms[1] + terms[2]
    totals = terms[3] + terms[4] + terms[5]
    peak = jnp.max(peaks, axis=0, keepdims=True)
    scale = jnp.exp(peaks - peak)
    total = jnp.sum(scale * totals, axis=0, keepdims=True)
    def columns(factor):
        return [
            jnp.concatenate([factor[:, c, :], jnp.zeros((block - senders, block), F32)], axis=0).T for c in range(cuts)
        ]
    return peak, total, scale, columns


def merge_kernel(came_ref, out_ref):
    senders, _, block = came_ref.shape
    each, total_rows, _ = out_ref.shape
    slots = total_rows - STATS
    cuts = slots // block
    peak, total, scale, columns = scales(came_ref[:, each * slots :, :].astype(F32), cuts, block)
    terms = split3(peak[0]) + split3(total[0])
    stats = jnp.concatenate([t.astype(F32) for t in terms] + [jnp.zeros((STATS - len(terms) * cuts, block), F32)], axis=0).astype(BF16)
    columns = columns(scale)
    for r in range(each):
        out_ref[r, slots:, :] = stats
    for c in range(cuts):
        factors = [jnp.broadcast_to(columns[c][:, t : t + 1], (block, block)) for t in range(senders)]
        for r in range(each):
            at = r * slots + c * block
            parts = [came_ref[t, at : at + block, :].astype(F32) * factors[t] for t in range(senders)]
            out_ref[r, c * block : (c + 1) * block, :] = sum(parts[1:], parts[0]).astype(BF16)


def merge(came, slots):
    senders, total_rows, block = came.shape
    each = total_rows // slots
    return pl.pallas_call(
        merge_kernel,
        out_shape=jax.ShapeDtypeStruct((each, slots + STATS, block), BF16),
        in_specs=[pl.BlockSpec(memory_space=pltpu.VMEM)],
        out_specs=pl.BlockSpec(memory_space=pltpu.VMEM),
        compiler_params=pltpu.CompilerParams(vmem_limit_bytes=32 * 2**20),
        cost_estimate=pl.CostEstimate(flops=2 * senders * each * slots * block, bytes_accessed=3 * 2**20, transcendentals=0),
        name="merge",
    )(came)


def expand_kernel(came_hbm, weight_hbm, out_hbm, came_ref, weight_ref, out_ref, came_sem, weight_sem, out_sem):
    senders, total_rows, block = came_ref.shape
    slots = total_rows - STATS
    experts, _, ff = weight_ref.shape
    cuts = slots // block
    per = slots // experts
    n_out, high, wide = out_ref.shape
    each = n_out // experts
    came_copy = pltpu.make_async_copy(came_hbm, came_ref, came_sem)
    weight_copies = [pltpu.make_async_copy(weight_hbm.at[e], weight_ref.at[e], weight_sem.at[e]) for e in range(experts)]
    out_copies = [
        pltpu.make_async_copy(out_ref.at[pl.ds(e * each, each)], out_hbm.at[pl.ds(e * each, each)], out_sem.at[e]) for e in range(experts)
    ]
    for copy in [came_copy] + weight_copies:
        copy.start()
    came_copy.wait()
    _, total, scale, columns = scales(came_ref[:, slots:, :].astype(F32), cuts, block)
    columns = columns(scale / total)
    parts = []
    for c in range(cuts):
        part = [came_ref[t, c * block : (c + 1) * block, :].astype(F32) * columns[c][:, t : t + 1] for t in range(senders)]
        parts.append(sum(part[1:], part[0]).astype(BF16))
    inputs = jnp.concatenate(parts, axis=0)
    for e in range(experts):
        weight_copies[e].wait()
        pre = jnp.dot(inputs[e * per : (e + 1) * per], weight_ref[e], preferred_element_type=F32).astype(BF16)
        for i in range(per // high):
            for j in range(ff // wide):
                out_ref[e * each + i * (ff // wide) + j] = pre[i * high : (i + 1) * high, j * wide : (j + 1) * wide]
        out_copies[e].start()
    for copy in out_copies:
        copy.wait()


def expand(came, weight_in, n_tok):
    senders, total_rows, block = came.shape
    slots = total_rows - STATS
    experts, _, ff = weight_in.shape
    high = 16
    out = (n_tok, high, slots * ff // (n_tok * high))
    return pl.pallas_call(
        expand_kernel,
        out_shape=jax.ShapeDtypeStruct(out, BF16),
        in_specs=[pl.BlockSpec(memory_space=pltpu.HBM)] * 2,
        out_specs=pl.BlockSpec(memory_space=pltpu.HBM),
        scratch_shapes=[
            pltpu.VMEM(came.shape, BF16),
            pltpu.VMEM(weight_in.shape, BF16),
            pltpu.VMEM(out, BF16),
            pltpu.SemaphoreType.DMA,
            pltpu.SemaphoreType.DMA((experts,)),
            pltpu.SemaphoreType.DMA((experts,)),
        ],
        compiler_params=pltpu.CompilerParams(vmem_limit_bytes=56 * 2**20),
        cost_estimate=pl.CostEstimate(flops=2 * slots * block * ff, bytes_accessed=4 * 2**20, transcendentals=0),
        name="expand",
    )(came, weight_in)


def produce_kernel(hidden_hbm, weight_hbm, out_ref, hidden_ref, weight_ref, hidden_sem, weight_sem):
    n_tok, high, wide = hidden_ref.shape
    experts, ff, block = weight_ref.shape
    per = out_ref.shape[0] // experts
    halves, chunks = ff // wide, per // high
    each = n_tok // experts
    copies = [
        (
            pltpu.make_async_copy(hidden_hbm.at[pl.ds(e * each, each)], hidden_ref.at[pl.ds(e * each, each)], hidden_sem.at[e]),
            pltpu.make_async_copy(weight_hbm.at[e], weight_ref.at[e], weight_sem.at[e]),
        )
        for e in range(experts)
    ]
    for pair in copies:
        for copy in pair:
            copy.start()
    for e in range(experts):
        for copy in copies[e]:
            copy.wait()
        total = None
        for j in range(halves):
            rows = jnp.concatenate([hidden_ref[e * each + i * halves + j] for i in range(chunks)], axis=0)
            part = jnp.dot(rows, weight_ref[e, j * wide : (j + 1) * wide, :], preferred_element_type=F32)
            total = part if total is None else total + part
        out_ref[e * per : (e + 1) * per, :] = total.astype(BF16)


def produce(hidden, weight_out):
    n_tok, high, wide = hidden.shape
    experts, ff, block = weight_out.shape
    slots = n_tok * high * wide // ff
    return pl.pallas_call(
        produce_kernel,
        out_shape=jax.ShapeDtypeStruct((slots, block), BF16),
        in_specs=[pl.BlockSpec(memory_space=pltpu.HBM)] * 2,
        out_specs=pl.BlockSpec(memory_space=pltpu.VMEM),
        scratch_shapes=[
            pltpu.VMEM(hidden.shape, BF16),
            pltpu.VMEM(weight_out.shape, BF16),
            pltpu.SemaphoreType.DMA((experts,)),
            pltpu.SemaphoreType.DMA((experts,)),
        ],
        compiler_params=pltpu.CompilerParams(vmem_limit_bytes=57 * 2**20),
        cost_estimate=pl.CostEstimate(flops=2 * slots * ff * block, bytes_accessed=3 * 2**20, transcendentals=0),
        name="produce",
    )(hidden, weight_out)


def combine_kernel(own_ref, twin_ref, near_ref, beside_ref, far_ref, rest_ref, last_ref, out_ref):
    total_rows, slots = own_ref.shape
    rows = total_rows - STATS
    here, core = lax.axis_index("zh"), lax.axis_index("c")
    n_hi = out_ref.shape[1] // slots // 2
    step = 2 * core - 1
    blocks = [
        (own_ref, 0, 0, 0), (twin_ref, 0, 0, 1), (near_ref, 0, 1, 0), (beside_ref, 0, 1, 1), (far_ref, 0, 2, 0),
        (rest_ref, 0, -1, 1), (rest_ref, total_rows, -1, 0), (last_ref, 0, -2, 1),
    ]
    peaks, totals = [], []
    for ref, at, _, _ in blocks:
        stats = ref[at + rows : at + total_rows, :].astype(F32)
        stats = jnp.concatenate([stats[i * 8 : (i + 1) * 8] for i in range(rows // slots)], axis=1)
        joined = stats[0:2] + stats[2:4] + stats[4:6]
        peaks.append(joined[0:1])
        totals.append(joined[1:2])
    peaks, totals = jnp.concatenate(peaks, axis=0), jnp.concatenate(totals, axis=0)
    scale = jnp.exp(peaks - jnp.max(peaks, axis=0, keepdims=True))
    scale = scale / jnp.sum(scale * totals, axis=0, keepdims=True)
    scale = jnp.concatenate([scale, jnp.zeros((128 - scale.shape[0], rows), F32)], axis=0).T
    for k, (ref, at, steps, flip) in enumerate(blocks):
        z = lax.rem(here + steps * step + 2 * n_hi, n_hi)
        e = 2 * z + (1 - core if flip else core)
        at_out = pl.ds(pl.multiple_of(e * slots, slots), slots)
        out_ref[:, at_out] = (ref[at : at + rows, :].astype(F32) * scale[:, k : k + 1]).astype(BF16)


def combine(own, twin, near, beside, far, rest, last, n_exp):
    total_rows, slots = own.shape
    rows = total_rows - STATS
    return pl.pallas_call(
        combine_kernel,
        out_shape=jax.ShapeDtypeStruct((rows, n_exp * slots), BF16),
        in_specs=[pl.BlockSpec(memory_space=pltpu.VMEM)] * 7,
        out_specs=pl.BlockSpec(memory_space=pltpu.VMEM),
        compiler_params=pltpu.CompilerParams(vmem_limit_bytes=32 * 2**20),
        cost_estimate=pl.CostEstimate(flops=2 * n_exp * rows * slots, bytes_accessed=4 * 2**20, transcendentals=0),
        name="combine",
    )(own, twin, near, beside, far, rest, last)


def final_kernel(weights_ref, pieces_hbm, out_ref, values, sem):
    rows, total = weights_ref.shape
    n_tok, slots, block = pieces_hbm.shape
    n_exp = total // slots
    quarter = n_tok // n_exp
    here, core = lax.axis_index("zh"), lax.axis_index("c")
    copies = []
    for e in range(n_exp):
        first = ((e // 2 + here) % 4) * 8 + (e % 2) * 4
        for q in range(quarter):
            into = values.at[pl.ds(e * slots, slots), pl.ds(q * block, block)]
            copies.append(pltpu.make_async_copy(pieces_hbm.at[place(first + q, core)], into, sem.at[e * quarter + q]))
            copies[-1].start()
    step = 2
    result = None
    for e in range(0, n_exp, step):
        for copy in copies[e * quarter : (e + step) * quarter]:
            copy.wait()
        cut = slice(e * slots, (e + step) * slots)
        part = jnp.dot(weights_ref[:, cut], values[cut, :], preferred_element_type=F32)
        result = part if result is None else result + part
    out_ref[...] = result.astype(BF16)


def final(weights, pieces):
    rows, total = weights.shape
    n_tok, slots, block = pieces.shape
    columns = n_tok * slots // total * block
    return pl.pallas_call(
        final_kernel,
        out_shape=jax.ShapeDtypeStruct((rows, columns), BF16),
        in_specs=[pl.BlockSpec(memory_space=pltpu.VMEM), pl.BlockSpec(memory_space=pltpu.HBM)],
        out_specs=pl.BlockSpec(memory_space=pltpu.VMEM),
        scratch_shapes=[pltpu.VMEM((total, columns), BF16), pltpu.SemaphoreType.DMA((n_tok,))],
        compiler_params=pltpu.CompilerParams(vmem_limit_bytes=50 * 2**20),
        cost_estimate=pl.CostEstimate(flops=2 * rows * total * columns, bytes_accessed=5 * 2**20, transcendentals=0),
        name="final",
    )(weights, pieces)


def flat(x, zl, y, zh, c):
    return (((x * 2 + zl) * 4 + y) * 4 + zh) * 2 + c


def exchange_groups():
    four, eight = [], []
    for zh in range(4):
        four += [[flat(x, zl, y, zh, 0) for y in range(4)] for x in range(4) for zl in range(2)]
        four += [[flat(x, zl, y, zh, 1) for x in range(4)] for zl in range(2) for y in range(4)]
        eight += [[flat(x, zl, y, zh, 0) for x in range(4) for zl in range(2)] for y in range(4)]
        eight += [[flat(x, zl, y, zh, 1) for zl in range(2) for y in range(4)] for x in range(4)]
    return four, eight


def local(tokens, slot_params, weight_in, weight_out):
    n_tok, n_exp, n_hi = lax.axis_size(TOK), lax.axis_size(EXP), lax.axis_size("zh")
    block, slots = weight_in.shape[1], slot_params.shape[1]
    four, eight = exchange_groups()
    swap = [(0, 1), (1, 0)]
    along = [
        (2 * z + c, 2 * ((z + (1 if c == 0 else -1)) % n_hi) + c) for z in range(n_hi) for c in range(2)
    ]
    own, sent = route(tokens, slot_params, n_tok)

    twin = lax.ppermute(own, "c", swap)
    near = lax.ppermute(own, EXP, along)
    beside = lax.ppermute(twin, EXP, along)
    came = lax.all_to_all(sent, ALL, 0, 0, axis_index_groups=four, tiled=True)
    came, near, beside = lax.optimization_barrier((came, near, beside))
    came = lax.all_to_all(merge(came, slots), ALL, 0, 0, axis_index_groups=eight, tiled=True)

    pre = lax.all_to_all(expand(came, weight_in, n_tok), TOK, 0, 0, tiled=True)
    pre = jnp.sum(pre.astype(F32), axis=0)
    hidden = jax.nn.gelu(pre, approximate=False).astype(BF16)
    hidden = lax.all_to_all(
        jnp.broadcast_to(hidden[None], (n_tok,) + hidden.shape), TOK, 0, 0, tiled=True
    )
    produced = produce(hidden, weight_out)

    moves = [
        (flat(x, zl, y, zh, c), flat((x + zh) % 4, c, y, x, zl))
        for x in range(4) for zl in range(2) for y in range(4) for zh in range(4) for c in range(2)
    ]
    piece = lax.ppermute(produced, ALL, moves)
    pieces = jnp.broadcast_to(piece[None], (8,) + piece.shape)
    pieces = lax.all_to_all(pieces, ALL, 0, 0, axis_index_groups=eight, tiled=True)
    rest = lax.ppermute(jnp.concatenate([near, beside]), "c", swap)
    pieces, forward, rest = lax.optimization_barrier((pieces, near, rest))
    far = lax.ppermute(forward, EXP, along)
    last = lax.ppermute(far, "c", swap)
    pieces = jnp.broadcast_to(pieces[None], (4,) + pieces.shape)
    pieces = lax.all_to_all(pieces, ALL, 0, 0, axis_index_groups=four, tiled=True)
    return final(combine(own, twin, near, beside, far, rest, last, n_exp), pieces.reshape(n_tok, slots, block))


def solution(mesh):
    mesh = Mesh(mesh.devices.reshape(4, 2, 4, 4, 2), ALL)
    placed = (P(TOK, None), P(None, EXP), P(EXP, TOK, None), P(EXP, None, TOK))
    return jax.shard_map(
        local, mesh=mesh, in_specs=placed, out_specs=P(TOK, EXP), check_vma=False
    )
```

```python
import jax
import jax.numpy as jnp
from jax import lax
from jax.experimental import pallas as pl
from jax.experimental.pallas import tpu as pltpu
from jax.sharding import Mesh, PartitionSpec as P

BF16, F32 = jnp.bfloat16, jnp.float32
TOK, EXP = ("x", "zl", "y"), ("zh", "c")
ALL = TOK + EXP
CHUNKS = 4
STATS = 16
VMEM = 60 * 2**20


def split3(value):
    head = value.astype(BF16)
    rest = value - head.astype(F32)
    mid = rest.astype(BF16)
    return [head, mid, (rest - mid.astype(F32)).astype(BF16)]


def join3(parts):
    return parts[0].astype(F32) + parts[1].astype(F32) + parts[2].astype(F32)


def place(t, core):
    return jnp.where(core == 0, (t % 4) * 8 + t // 4, t)


def route_kernel(tokens_hbm, params_hbm, own_ref, sent_hbm, tokens, params, logits, sent_ref, stats_ref, sem, out_sem, stats_sem):
    rows, width = tokens.shape
    slots = params.shape[1]
    n_tok, _, block = sent_ref.shape
    groups = sent_hbm.shape[0]
    each = n_tok // groups
    core = lax.axis_index("c")
    span = width // CHUNKS

    def copies(i):
        cut = pl.ds(i * span, span)
        return (
            pltpu.make_async_copy(tokens_hbm.at[:, cut], tokens.at[:, cut], sem.at[0, i]),
            pltpu.make_async_copy(params_hbm.at[cut, :], params.at[cut, :], sem.at[1, i]),
        )

    for i in range(CHUNKS):
        for copy in copies(i):
            copy.start()
    for i in range(CHUNKS):
        for copy in copies(i):
            copy.wait()
        part = jnp.dot(
            tokens[:, i * span : (i + 1) * span],
            params[i * span : (i + 1) * span, :],
            preferred_element_type=F32,
        )
        if i == 0:
            logits[...] = part
        else:
            logits[...] += part

    values = logits[...]
    row_max = jnp.max(values, axis=1, keepdims=True)
    row_exp = jnp.exp(values - row_max)
    row_total = jnp.sum(row_exp, axis=1, keepdims=True)
    own_ref[:rows, :] = row_exp.astype(BF16)
    lane = lax.broadcasted_iota(jnp.int32, (rows, 128), 1)
    pair = jnp.where(lane == 0, row_max, jnp.where(lane == 1, row_total, 0.0)).T[:8]
    terms = jnp.concatenate([term.astype(F32)[:2] for term in split3(pair)] + [jnp.zeros((2, rows), F32)], axis=0)
    own_ref[rows:, :] = jnp.concatenate([terms[:, i * slots : (i + 1) * slots] for i in range(rows // slots)], axis=0).astype(BF16)

    col_max = jnp.max(values, axis=0, keepdims=True)
    shifted = jnp.exp(values - col_max)
    col_total = jnp.sum(shifted, axis=0, keepdims=True)
    dispatch = shifted.astype(BF16).T
    terms = split3(col_max) + split3(col_total)
    stats = jnp.concatenate([t[:, i * block : (i + 1) * block].astype(F32) for t in terms for i in range(slots // block)]
                            + [jnp.zeros((STATS - len(terms) * (slots // block), block), F32)], axis=0).astype(BF16)
    stats_ref[...] = stats
    leave = [
        pltpu.make_async_copy(stats_ref, sent_hbm.at[g, pl.ds(each * slots, STATS)], stats_sem.at[g])
        for g in range(groups)
    ]
    for copy in leave:
        copy.start()
    per = n_tok // CHUNKS
    for i in range(CHUNKS):
        sums = jnp.dot(dispatch, tokens[:, i * span : (i + 1) * span], preferred_element_type=F32).astype(BF16)
        for j in range(per):
            t = i * per + j
            sent_ref[t] = sums[:, j * block : (j + 1) * block]
            at = place(t, core)
            copy = pltpu.make_async_copy(
                sent_ref.at[t], sent_hbm.at[at // each, pl.ds(pl.multiple_of((at % each) * slots, slots), slots)], out_sem.at[t]
            )
            copy.start()
            leave.append(copy)
    for copy in leave:
        copy.wait()


def route(tokens, params, n_tok):
    rows, width = tokens.shape
    slots = params.shape[1]
    return pl.pallas_call(
        route_kernel,
        out_shape=(
            jax.ShapeDtypeStruct((rows + STATS, slots), BF16),
            jax.ShapeDtypeStruct((4, n_tok // 4 * slots + STATS, width // n_tok), BF16),
        ),
        in_specs=[pl.BlockSpec(memory_space=pltpu.HBM)] * 2,
        out_specs=[pl.BlockSpec(memory_space=pltpu.VMEM), pl.BlockSpec(memory_space=pltpu.HBM)],
        scratch_shapes=[
            pltpu.VMEM((rows, width), BF16),
            pltpu.VMEM((width, slots), BF16),
            pltpu.VMEM((rows, slots), F32),
            pltpu.VMEM((n_tok, slots, width // n_tok), BF16),
            pltpu.VMEM((STATS, width // n_tok), BF16),
            pltpu.SemaphoreType.DMA((2, CHUNKS)),
            pltpu.SemaphoreType.DMA((n_tok,)),
            pltpu.SemaphoreType.DMA((4,)),
        ],
        compiler_params=pltpu.CompilerParams(vmem_limit_bytes=VMEM),
        cost_estimate=pl.CostEstimate(flops=4 * rows * width * slots, bytes_accessed=10 * 2**20, transcendentals=2 * rows * slots),
        name="route",
    )(tokens, params)


def scales(stats, cuts, block):
    senders = stats.shape[0]
    terms = [stats[:, i * cuts : (i + 1) * cuts] for i in range(6)]
    peaks = terms[0] + terms[1] + terms[2]
    totals = terms[3] + terms[4] + terms[5]
    peak = jnp.max(peaks, axis=0, keepdims=True)
    scale = jnp.exp(peaks - peak)
    total = jnp.sum(scale * totals, axis=0, keepdims=True)
    def columns(factor):
        return [
            jnp.concatenate([factor[:, c, :], jnp.zeros((block - senders, block), F32)], axis=0).T for c in range(cuts)
        ]
    return peak, total, scale, columns


def merge_kernel(came_ref, out_ref):
    senders, _, block = came_ref.shape
    each, total_rows, _ = out_ref.shape
    slots = total_rows - STATS
    cuts = slots // block
    peak, total, scale, columns = scales(came_ref[:, each * slots :, :].astype(F32), cuts, block)
    terms = split3(peak[0]) + split3(total[0])
    stats = jnp.concatenate([t.astype(F32) for t in terms] + [jnp.zeros((STATS - len(terms) * cuts, block), F32)], axis=0).astype(BF16)
    columns = columns(scale)
    for r in range(each):
        out_ref[r, slots:, :] = stats
    for c in range(cuts):
        factors = [jnp.broadcast_to(columns[c][:, t : t + 1], (block, block)) for t in range(senders)]
        for r in range(each):
            at = r * slots + c * block
            parts = [came_ref[t, at : at + block, :].astype(F32) * factors[t] for t in range(senders)]
            out_ref[r, c * block : (c + 1) * block, :] = sum(parts[1:], parts[0]).astype(BF16)


def merge(came, slots):
    senders, total_rows, block = came.shape
    each = total_rows // slots
    return pl.pallas_call(
        merge_kernel,
        out_shape=jax.ShapeDtypeStruct((each, slots + STATS, block), BF16),
        in_specs=[pl.BlockSpec(memory_space=pltpu.VMEM)],
        out_specs=pl.BlockSpec(memory_space=pltpu.VMEM),
        compiler_params=pltpu.CompilerParams(vmem_limit_bytes=32 * 2**20),
        cost_estimate=pl.CostEstimate(flops=2 * senders * each * slots * block, bytes_accessed=3 * 2**20, transcendentals=0),
        name="merge",
    )(came)


def expand_kernel(came_ref, weight_ref, out_ref):
    senders, total_rows, block = came_ref.shape
    slots = total_rows - STATS
    experts, _, ff = weight_ref.shape
    cuts = slots // block
    per = slots // experts
    n_out, high, wide = out_ref.shape
    each = n_out // experts
    _, total, scale, columns = scales(came_ref[:, slots:, :].astype(F32), cuts, block)
    columns = columns(scale / total)
    parts = []
    for c in range(cuts):
        part = [came_ref[t, c * block : (c + 1) * block, :].astype(F32) * columns[c][:, t : t + 1] for t in range(senders)]
        parts.append(sum(part[1:], part[0]).astype(BF16))
    inputs = jnp.concatenate(parts, axis=0)
    for e in range(experts):
        pre = jnp.dot(inputs[e * per : (e + 1) * per], weight_ref[e], preferred_element_type=F32).astype(BF16)
        for i in range(per // high):
            for j in range(ff // wide):
                out_ref[e * each + i * (ff // wide) + j] = pre[i * high : (i + 1) * high, j * wide : (j + 1) * wide]


def expand(came, weight_in, n_tok):
    senders, total_rows, block = came.shape
    slots = total_rows - STATS
    experts, _, ff = weight_in.shape
    high = 16
    out = (n_tok, high, slots * ff // (n_tok * high))
    return pl.pallas_call(
        expand_kernel,
        out_shape=jax.ShapeDtypeStruct(out, BF16),
        in_specs=[pl.BlockSpec(memory_space=pltpu.VMEM)] * 2,
        out_specs=pl.BlockSpec(memory_space=pltpu.VMEM),
        compiler_params=pltpu.CompilerParams(vmem_limit_bytes=40 * 2**20),
        cost_estimate=pl.CostEstimate(flops=2 * slots * block * ff, bytes_accessed=4 * 2**20, transcendentals=0),
        name="expand",
    )(came, weight_in)


def produce_kernel(hidden_ref, weight_ref, out_ref):
    n_tok, high, wide = hidden_ref.shape
    experts, ff, block = weight_ref.shape
    per = out_ref.shape[0] // experts
    halves, chunks = ff // wide, per // high
    each = n_tok // experts
    for e in range(experts):
        total = None
        for j in range(halves):
            rows = jnp.concatenate([hidden_ref[e * each + i * halves + j] for i in range(chunks)], axis=0)
            part = jnp.dot(rows, weight_ref[e, j * wide : (j + 1) * wide, :], preferred_element_type=F32)
            total = part if total is None else total + part
        out_ref[e * per : (e + 1) * per, :] = total.astype(BF16)


def produce(hidden, weight_out):
    n_tok, high, wide = hidden.shape
    experts, ff, block = weight_out.shape
    slots = n_tok * high * wide // ff
    return pl.pallas_call(
        produce_kernel,
        out_shape=jax.ShapeDtypeStruct((slots, block), BF16),
        in_specs=[pl.BlockSpec(memory_space=pltpu.VMEM)] * 2,
        out_specs=pl.BlockSpec(memory_space=pltpu.VMEM),
        compiler_params=pltpu.CompilerParams(vmem_limit_bytes=40 * 2**20),
        cost_estimate=pl.CostEstimate(flops=2 * slots * ff * block, bytes_accessed=3 * 2**20, transcendentals=0),
        name="produce",
    )(hidden, weight_out)


def combine_kernel(own_ref, twin_ref, near_ref, beside_ref, far_ref, rest_ref, last_ref, out_ref):
    total_rows, slots = own_ref.shape
    rows = total_rows - STATS
    here, core = lax.axis_index("zh"), lax.axis_index("c")
    n_hi = out_ref.shape[1] // slots // 2
    step = 2 * core - 1
    blocks = [
        (own_ref, 0, 0, 0), (twin_ref, 0, 0, 1), (near_ref, 0, 1, 0), (beside_ref, 0, 1, 1), (far_ref, 0, 2, 0),
        (rest_ref, 0, -1, 1), (rest_ref, total_rows, -1, 0), (last_ref, 0, -2, 1),
    ]
    peaks, totals = [], []
    for ref, at, _, _ in blocks:
        stats = ref[at + rows : at + total_rows, :].astype(F32)
        stats = jnp.concatenate([stats[i * 8 : (i + 1) * 8] for i in range(rows // slots)], axis=1)
        joined = stats[0:2] + stats[2:4] + stats[4:6]
        peaks.append(joined[0:1])
        totals.append(joined[1:2])
    peaks, totals = jnp.concatenate(peaks, axis=0), jnp.concatenate(totals, axis=0)
    scale = jnp.exp(peaks - jnp.max(peaks, axis=0, keepdims=True))
    scale = scale / jnp.sum(scale * totals, axis=0, keepdims=True)
    scale = jnp.concatenate([scale, jnp.zeros((128 - scale.shape[0], rows), F32)], axis=0).T
    for k, (ref, at, steps, flip) in enumerate(blocks):
        z = lax.rem(here + steps * step + 2 * n_hi, n_hi)
        e = 2 * z + (1 - core if flip else core)
        at_out = pl.ds(pl.multiple_of(e * slots, slots), slots)
        out_ref[:, at_out] = (ref[at : at + rows, :].astype(F32) * scale[:, k : k + 1]).astype(BF16)


def combine(own, twin, near, beside, far, rest, last, n_exp):
    total_rows, slots = own.shape
    rows = total_rows - STATS
    return pl.pallas_call(
        combine_kernel,
        out_shape=jax.ShapeDtypeStruct((rows, n_exp * slots), BF16),
        in_specs=[pl.BlockSpec(memory_space=pltpu.VMEM)] * 7,
        out_specs=pl.BlockSpec(memory_space=pltpu.VMEM),
        compiler_params=pltpu.CompilerParams(vmem_limit_bytes=32 * 2**20),
        cost_estimate=pl.CostEstimate(flops=2 * n_exp * rows * slots, bytes_accessed=4 * 2**20, transcendentals=0),
        name="combine",
    )(own, twin, near, beside, far, rest, last)


def final_kernel(weights_ref, pieces_hbm, out_ref, values, sem):
    rows, total = weights_ref.shape
    n_tok, slots, block = pieces_hbm.shape
    n_exp = total // slots
    quarter = n_tok // n_exp
    here, core = lax.axis_index("zh"), lax.axis_index("c")
    copies = []
    for e in range(n_exp):
        first = ((e // 2 + here) % 4) * 8 + (e % 2) * 4
        for q in range(quarter):
            into = values.at[pl.ds(e * slots, slots), pl.ds(q * block, block)]
            copies.append(pltpu.make_async_copy(pieces_hbm.at[place(first + q, core)], into, sem.at[e * quarter + q]))
            copies[-1].start()
    step = 2
    result = None
    for e in range(0, n_exp, step):
        for copy in copies[e * quarter : (e + step) * quarter]:
            copy.wait()
        cut = slice(e * slots, (e + step) * slots)
        part = jnp.dot(weights_ref[:, cut], values[cut, :], preferred_element_type=F32)
        result = part if result is None else result + part
    out_ref[...] = result.astype(BF16)


def final(weights, pieces):
    rows, total = weights.shape
    n_tok, slots, block = pieces.shape
    columns = n_tok * slots // total * block
    return pl.pallas_call(
        final_kernel,
        out_shape=jax.ShapeDtypeStruct((rows, columns), BF16),
        in_specs=[pl.BlockSpec(memory_space=pltpu.VMEM), pl.BlockSpec(memory_space=pltpu.HBM)],
        out_specs=pl.BlockSpec(memory_space=pltpu.VMEM),
        scratch_shapes=[pltpu.VMEM((total, columns), BF16), pltpu.SemaphoreType.DMA((n_tok,))],
        compiler_params=pltpu.CompilerParams(vmem_limit_bytes=50 * 2**20),
        cost_estimate=pl.CostEstimate(flops=2 * rows * total * columns, bytes_accessed=5 * 2**20, transcendentals=0),
        name="final",
    )(weights, pieces)


def flat(x, zl, y, zh, c):
    return (((x * 2 + zl) * 4 + y) * 4 + zh) * 2 + c


def exchange_groups():
    four, eight = [], []
    for zh in range(4):
        four += [[flat(x, zl, y, zh, 0) for y in range(4)] for x in range(4) for zl in range(2)]
        four += [[flat(x, zl, y, zh, 1) for x in range(4)] for zl in range(2) for y in range(4)]
        eight += [[flat(x, zl, y, zh, 0) for x in range(4) for zl in range(2)] for y in range(4)]
        eight += [[flat(x, zl, y, zh, 1) for zl in range(2) for y in range(4)] for x in range(4)]
    return four, eight


def local(tokens, slot_params, weight_in, weight_out):
    n_tok, n_exp, n_hi = lax.axis_size(TOK), lax.axis_size(EXP), lax.axis_size("zh")
    block, slots = weight_in.shape[1], slot_params.shape[1]
    four, eight = exchange_groups()
    swap = [(0, 1), (1, 0)]
    along = [
        (2 * z + c, 2 * ((z + (1 if c == 0 else -1)) % n_hi) + c) for z in range(n_hi) for c in range(2)
    ]
    own, sent = route(tokens, slot_params, n_tok)

    twin = lax.ppermute(own, "c", swap)
    near = lax.ppermute(own, EXP, along)
    beside = lax.ppermute(twin, EXP, along)
    came = lax.all_to_all(sent, ALL, 0, 0, axis_index_groups=four, tiled=True)
    came, near, beside = lax.optimization_barrier((came, near, beside))
    came = lax.all_to_all(merge(came, slots), ALL, 0, 0, axis_index_groups=eight, tiled=True)

    pre = lax.all_to_all(expand(came, weight_in, n_tok), TOK, 0, 0, tiled=True)
    pre = jnp.sum(pre.astype(F32), axis=0)
    hidden = jax.nn.gelu(pre, approximate=False).astype(BF16)
    hidden = lax.all_to_all(
        jnp.broadcast_to(hidden[None], (n_tok,) + hidden.shape), TOK, 0, 0, tiled=True
    )
    produced = produce(hidden, weight_out)

    moves = [
        (flat(x, zl, y, zh, c), flat((x + zh) % 4, c, y, x, zl))
        for x in range(4) for zl in range(2) for y in range(4) for zh in range(4) for c in range(2)
    ]
    piece = lax.ppermute(produced, ALL, moves)
    pieces = jnp.broadcast_to(piece[None], (8,) + piece.shape)
    pieces = lax.all_to_all(pieces, ALL, 0, 0, axis_index_groups=eight, tiled=True)
    rest = lax.ppermute(jnp.concatenate([near, beside]), "c", swap)
    pieces, forward, rest = lax.optimization_barrier((pieces, near, rest))
    far = lax.ppermute(forward, EXP, along)
    last = lax.ppermute(far, "c", swap)
    pieces = jnp.broadcast_to(pieces[None], (4,) + pieces.shape)
    pieces = lax.all_to_all(pieces, ALL, 0, 0, axis_index_groups=four, tiled=True)
    return final(combine(own, twin, near, beside, far, rest, last, n_exp), pieces.reshape(n_tok, slots, block))


def solution(mesh):
    mesh = Mesh(mesh.devices.reshape(4, 2, 4, 4, 2), ALL)
    placed = (P(TOK, None), P(None, EXP), P(EXP, TOK, None), P(EXP, None, TOK))
    return jax.shard_map(
        local, mesh=mesh, in_specs=placed, out_specs=P(TOK, EXP), check_vma=False
    )
```

```python
import jax
import jax.numpy as jnp
from jax import lax
from jax.experimental import pallas as pl
from jax.experimental.pallas import tpu as pltpu
from jax.sharding import Mesh, PartitionSpec as P

BF16, F32 = jnp.bfloat16, jnp.float32
TOK, EXP = ("x", "zl", "y"), ("zh", "c")
ALL = TOK + EXP
CHUNKS = 4
STATS = 16
VMEM = 60 * 2**20


def split3(value):
    head = value.astype(BF16)
    rest = value - head.astype(F32)
    mid = rest.astype(BF16)
    return [head, mid, (rest - mid.astype(F32)).astype(BF16)]


def join3(parts):
    return parts[0].astype(F32) + parts[1].astype(F32) + parts[2].astype(F32)


def place(t, core):
    return jnp.where(core == 0, (t % 4) * 8 + t // 4, t)


def route_kernel(tokens_hbm, params_hbm, own_ref, sent_hbm, tokens, params, logits, sent_ref, stats_ref, sem, out_sem, stats_sem):
    rows, width = tokens.shape
    slots = params.shape[1]
    n_tok, _, block = sent_ref.shape
    groups = sent_hbm.shape[0]
    each = n_tok // groups
    core = lax.axis_index("c")
    span = width // CHUNKS

    def copies(i):
        cut = pl.ds(i * span, span)
        return (
            pltpu.make_async_copy(tokens_hbm.at[:, cut], tokens.at[:, cut], sem.at[0, i]),
            pltpu.make_async_copy(params_hbm.at[cut, :], params.at[cut, :], sem.at[1, i]),
        )

    for i in range(CHUNKS):
        for copy in copies(i):
            copy.start()
    for i in range(CHUNKS):
        for copy in copies(i):
            copy.wait()
        part = jnp.dot(
            tokens[:, i * span : (i + 1) * span],
            params[i * span : (i + 1) * span, :],
            preferred_element_type=F32,
        )
        if i == 0:
            logits[...] = part
        else:
            logits[...] += part

    values = logits[...]
    row_max = jnp.max(values, axis=1, keepdims=True)
    row_exp = jnp.exp(values - row_max)
    row_total = jnp.sum(row_exp, axis=1, keepdims=True)
    own_ref[:rows, :] = row_exp.astype(BF16)
    lane = lax.broadcasted_iota(jnp.int32, (rows, 128), 1)
    pair = jnp.where(lane == 0, row_max, jnp.where(lane == 1, row_total, 0.0)).T[:8]
    terms = jnp.concatenate([term.astype(F32)[:2] for term in split3(pair)] + [jnp.zeros((2, rows), F32)], axis=0)
    own_ref[rows:, :] = jnp.concatenate([terms[:, i * slots : (i + 1) * slots] for i in range(rows // slots)], axis=0).astype(BF16)

    col_max = jnp.max(values, axis=0, keepdims=True)
    shifted = jnp.exp(values - col_max)
    col_total = jnp.sum(shifted, axis=0, keepdims=True)
    dispatch = shifted.astype(BF16).T
    terms = split3(col_max) + split3(col_total)
    stats = jnp.concatenate([t[:, i * block : (i + 1) * block].astype(F32) for t in terms for i in range(slots // block)]
                            + [jnp.zeros((STATS - len(terms) * (slots // block), block), F32)], axis=0).astype(BF16)
    stats_ref[...] = stats
    leave = [
        pltpu.make_async_copy(stats_ref, sent_hbm.at[g, pl.ds(each * slots, STATS)], stats_sem.at[g])
        for g in range(groups)
    ]
    for copy in leave:
        copy.start()
    per = n_tok // CHUNKS
    for i in range(CHUNKS):
        sums = jnp.dot(dispatch, tokens[:, i * span : (i + 1) * span], preferred_element_type=F32).astype(BF16)
        for j in range(per):
            t = i * per + j
            sent_ref[t] = sums[:, j * block : (j + 1) * block]
            at = place(t, core)
            copy = pltpu.make_async_copy(
                sent_ref.at[t], sent_hbm.at[at // each, pl.ds(pl.multiple_of((at % each) * slots, slots), slots)], out_sem.at[t]
            )
            copy.start()
            leave.append(copy)
    for copy in leave:
        copy.wait()


def route(tokens, params, n_tok):
    rows, width = tokens.shape
    slots = params.shape[1]
    return pl.pallas_call(
        route_kernel,
        out_shape=(
            jax.ShapeDtypeStruct((rows + STATS, slots), BF16),
            jax.ShapeDtypeStruct((4, n_tok // 4 * slots + STATS, width // n_tok), BF16),
        ),
        in_specs=[pl.BlockSpec(memory_space=pltpu.HBM)] * 2,
        out_specs=[pl.BlockSpec(memory_space=pltpu.VMEM), pl.BlockSpec(memory_space=pltpu.HBM)],
        scratch_shapes=[
            pltpu.VMEM((rows, width), BF16),
            pltpu.VMEM((width, slots), BF16),
            pltpu.VMEM((rows, slots), F32),
            pltpu.VMEM((n_tok, slots, width // n_tok), BF16),
            pltpu.VMEM((STATS, width // n_tok), BF16),
            pltpu.SemaphoreType.DMA((2, CHUNKS)),
            pltpu.SemaphoreType.DMA((n_tok,)),
            pltpu.SemaphoreType.DMA((4,)),
        ],
        compiler_params=pltpu.CompilerParams(vmem_limit_bytes=VMEM),
        cost_estimate=pl.CostEstimate(flops=4 * rows * width * slots, bytes_accessed=10 * 2**20, transcendentals=2 * rows * slots),
        name="route",
    )(tokens, params)


def scales(stats, cuts, block):
    senders = stats.shape[0]
    terms = [stats[:, i * cuts : (i + 1) * cuts] for i in range(6)]
    peaks = terms[0] + terms[1] + terms[2]
    totals = terms[3] + terms[4] + terms[5]
    peak = jnp.max(peaks, axis=0, keepdims=True)
    scale = jnp.exp(peaks - peak)
    total = jnp.sum(scale * totals, axis=0, keepdims=True)
    def columns(factor):
        return [
            jnp.concatenate([factor[:, c, :], jnp.zeros((block - senders, block), F32)], axis=0).T for c in range(cuts)
        ]
    return peak, total, scale, columns


def merge_kernel(came_ref, out_ref):
    senders, _, block = came_ref.shape
    each, total_rows, _ = out_ref.shape
    slots = total_rows - STATS
    cuts = slots // block
    peak, total, scale, columns = scales(came_ref[:, each * slots :, :].astype(F32), cuts, block)
    terms = split3(peak[0]) + split3(total[0])
    stats = jnp.concatenate([t.astype(F32) for t in terms] + [jnp.zeros((STATS - len(terms) * cuts, block), F32)], axis=0).astype(BF16)
    columns = columns(scale)
    for r in range(each):
        out_ref[r, slots:, :] = stats
    for c in range(cuts):
        factors = [jnp.broadcast_to(columns[c][:, t : t + 1], (block, block)) for t in range(senders)]
        for r in range(each):
            at = r * slots + c * block
            parts = [came_ref[t, at : at + block, :].astype(F32) * factors[t] for t in range(senders)]
            out_ref[r, c * block : (c + 1) * block, :] = sum(parts[1:], parts[0]).astype(BF16)


def merge(came, slots):
    senders, total_rows, block = came.shape
    each = total_rows // slots
    return pl.pallas_call(
        merge_kernel,
        out_shape=jax.ShapeDtypeStruct((each, slots + STATS, block), BF16),
        in_specs=[pl.BlockSpec(memory_space=pltpu.VMEM)],
        out_specs=pl.BlockSpec(memory_space=pltpu.VMEM),
        compiler_params=pltpu.CompilerParams(vmem_limit_bytes=32 * 2**20),
        cost_estimate=pl.CostEstimate(flops=2 * senders * each * slots * block, bytes_accessed=3 * 2**20, transcendentals=0),
        name="merge",
    )(came)


def expand_kernel(came_ref, weight_ref, out_ref):
    senders, total_rows, block = came_ref.shape
    slots = total_rows - STATS
    experts, _, ff = weight_ref.shape
    cuts = slots // block
    per = slots // experts
    n_out, high, wide = out_ref.shape
    each = n_out // experts
    _, total, scale, columns = scales(came_ref[:, slots:, :].astype(F32), cuts, block)
    columns = columns(scale / total)
    parts = []
    for c in range(cuts):
        part = [came_ref[t, c * block : (c + 1) * block, :].astype(F32) * columns[c][:, t : t + 1] for t in range(senders)]
        parts.append(sum(part[1:], part[0]).astype(BF16))
    inputs = jnp.concatenate(parts, axis=0)
    for e in range(experts):
        pre = jnp.dot(inputs[e * per : (e + 1) * per], weight_ref[e], preferred_element_type=F32).astype(BF16)
        for i in range(per // high):
            for j in range(ff // wide):
                out_ref[e * each + i * (ff // wide) + j] = pre[i * high : (i + 1) * high, j * wide : (j + 1) * wide]


def expand(came, weight_in, n_tok):
    senders, total_rows, block = came.shape
    slots = total_rows - STATS
    experts, _, ff = weight_in.shape
    high = 16
    out = (n_tok, high, slots * ff // (n_tok * high))
    return pl.pallas_call(
        expand_kernel,
        out_shape=jax.ShapeDtypeStruct(out, BF16),
        in_specs=[pl.BlockSpec(memory_space=pltpu.VMEM)] * 2,
        out_specs=pl.BlockSpec(memory_space=pltpu.VMEM),
        compiler_params=pltpu.CompilerParams(vmem_limit_bytes=40 * 2**20),
        cost_estimate=pl.CostEstimate(flops=2 * slots * block * ff, bytes_accessed=4 * 2**20, transcendentals=0),
        name="expand",
    )(came, weight_in)


def produce_kernel(hidden_ref, weight_ref, out_ref):
    n_tok, high, wide = hidden_ref.shape
    experts, ff, block = weight_ref.shape
    per = out_ref.shape[0] // experts
    halves, chunks = ff // wide, per // high
    each = n_tok // experts
    for e in range(experts):
        total = None
        for j in range(halves):
            rows = jnp.concatenate([hidden_ref[e * each + i * halves + j] for i in range(chunks)], axis=0)
            part = jnp.dot(rows, weight_ref[e, j * wide : (j + 1) * wide, :], preferred_element_type=F32)
            total = part if total is None else total + part
        out_ref[e * per : (e + 1) * per, :] = total.astype(BF16)


def produce(hidden, weight_out):
    n_tok, high, wide = hidden.shape
    experts, ff, block = weight_out.shape
    slots = n_tok * high * wide // ff
    return pl.pallas_call(
        produce_kernel,
        out_shape=jax.ShapeDtypeStruct((slots, block), BF16),
        in_specs=[pl.BlockSpec(memory_space=pltpu.VMEM)] * 2,
        out_specs=pl.BlockSpec(memory_space=pltpu.VMEM),
        compiler_params=pltpu.CompilerParams(vmem_limit_bytes=40 * 2**20),
        cost_estimate=pl.CostEstimate(flops=2 * slots * ff * block, bytes_accessed=3 * 2**20, transcendentals=0),
        name="produce",
    )(hidden, weight_out)


def combine_kernel(own_ref, twin_ref, near_ref, beside_ref, far_ref, rest_ref, last_ref, out_ref):
    total_rows, slots = own_ref.shape
    rows = total_rows - STATS
    here, core = lax.axis_index("zh"), lax.axis_index("c")
    n_hi = out_ref.shape[1] // slots // 2
    step = 2 * core - 1
    blocks = [
        (own_ref, 0, 0, 0), (twin_ref, 0, 0, 1), (near_ref, 0, 1, 0), (beside_ref, 0, 1, 1), (far_ref, 0, 2, 0),
        (rest_ref, 0, -1, 1), (rest_ref, total_rows, -1, 0), (last_ref, 0, -2, 1),
    ]
    peaks, totals = [], []
    for ref, at, _, _ in blocks:
        stats = ref[at + rows : at + total_rows, :].astype(F32)
        stats = jnp.concatenate([stats[i * 8 : (i + 1) * 8] for i in range(rows // slots)], axis=1)
        joined = stats[0:2] + stats[2:4] + stats[4:6]
        peaks.append(joined[0:1])
        totals.append(joined[1:2])
    peaks, totals = jnp.concatenate(peaks, axis=0), jnp.concatenate(totals, axis=0)
    scale = jnp.exp(peaks - jnp.max(peaks, axis=0, keepdims=True))
    scale = scale / jnp.sum(scale * totals, axis=0, keepdims=True)
    scale = jnp.concatenate([scale, jnp.zeros((128 - scale.shape[0], rows), F32)], axis=0).T
    for k, (ref, at, steps, flip) in enumerate(blocks):
        z = lax.rem(here + steps * step + 2 * n_hi, n_hi)
        e = 2 * z + (1 - core if flip else core)
        at_out = pl.ds(pl.multiple_of(e * slots, slots), slots)
        out_ref[:, at_out] = (ref[at : at + rows, :].astype(F32) * scale[:, k : k + 1]).astype(BF16)


def combine(own, twin, near, beside, far, rest, last, n_exp):
    total_rows, slots = own.shape
    rows = total_rows - STATS
    return pl.pallas_call(
        combine_kernel,
        out_shape=jax.ShapeDtypeStruct((rows, n_exp * slots), BF16),
        in_specs=[pl.BlockSpec(memory_space=pltpu.VMEM)] * 7,
        out_specs=pl.BlockSpec(memory_space=pltpu.VMEM),
        compiler_params=pltpu.CompilerParams(vmem_limit_bytes=32 * 2**20),
        cost_estimate=pl.CostEstimate(flops=2 * n_exp * rows * slots, bytes_accessed=4 * 2**20, transcendentals=0),
        name="combine",
    )(own, twin, near, beside, far, rest, last)


def final_kernel(weights_ref, pieces_ref, out_ref):
    rows, total = weights_ref.shape
    n_tok, slots, block = pieces_ref.shape
    n_exp = total // slots
    quarter = n_tok // n_exp
    here, core = lax.axis_index("zh"), lax.axis_index("c")
    result = None
    for e in range(n_exp):
        first = ((e // 2 + here) % 4) * 8 + (e % 2) * 4
        values = jnp.concatenate([pieces_ref[place(first + q, core)] for q in range(quarter)], axis=1)
        part = jnp.dot(weights_ref[:, e * slots : (e + 1) * slots], values, preferred_element_type=F32)
        result = part if result is None else result + part
    out_ref[...] = result.astype(BF16)


def final(weights, pieces):
    rows, total = weights.shape
    n_tok, slots, block = pieces.shape
    columns = n_tok * slots // total * block
    return pl.pallas_call(
        final_kernel,
        out_shape=jax.ShapeDtypeStruct((rows, columns), BF16),
        in_specs=[pl.BlockSpec(memory_space=pltpu.VMEM)] * 2,
        out_specs=pl.BlockSpec(memory_space=pltpu.VMEM),
        compiler_params=pltpu.CompilerParams(vmem_limit_bytes=40 * 2**20),
        cost_estimate=pl.CostEstimate(flops=2 * rows * total * columns, bytes_accessed=5 * 2**20, transcendentals=0),
        name="final",
    )(weights, pieces)


def flat(x, zl, y, zh, c):
    return (((x * 2 + zl) * 4 + y) * 4 + zh) * 2 + c


def exchange_groups():
    four, eight = [], []
    for zh in range(4):
        four += [[flat(x, zl, y, zh, 0) for y in range(4)] for x in range(4) for zl in range(2)]
        four += [[flat(x, zl, y, zh, 1) for x in range(4)] for zl in range(2) for y in range(4)]
        eight += [[flat(x, zl, y, zh, 0) for x in range(4) for zl in range(2)] for y in range(4)]
        eight += [[flat(x, zl, y, zh, 1) for zl in range(2) for y in range(4)] for x in range(4)]
    return four, eight


def local(tokens, slot_params, weight_in, weight_out):
    n_tok, n_exp, n_hi = lax.axis_size(TOK), lax.axis_size(EXP), lax.axis_size("zh")
    block, slots = weight_in.shape[1], slot_params.shape[1]
    four, eight = exchange_groups()
    swap = [(0, 1), (1, 0)]
    along = [
        (2 * z + c, 2 * ((z + (1 if c == 0 else -1)) % n_hi) + c) for z in range(n_hi) for c in range(2)
    ]
    own, sent = route(tokens, slot_params, n_tok)

    twin = lax.ppermute(own, "c", swap)
    near = lax.ppermute(own, EXP, along)
    beside = lax.ppermute(twin, EXP, along)
    came = lax.all_to_all(sent, ALL, 0, 0, axis_index_groups=four, tiled=True)
    came, near, beside = lax.optimization_barrier((came, near, beside))
    came = lax.all_to_all(merge(came, slots), ALL, 0, 0, axis_index_groups=eight, tiled=True)

    pre = lax.all_to_all(expand(came, weight_in, n_tok), TOK, 0, 0, tiled=True)
    pre = jnp.sum(pre.astype(F32), axis=0)
    hidden = jax.nn.gelu(pre, approximate=False).astype(BF16)
    hidden = lax.all_to_all(
        jnp.broadcast_to(hidden[None], (n_tok,) + hidden.shape), TOK, 0, 0, tiled=True
    )
    produced = produce(hidden, weight_out)

    moves = [
        (flat(x, zl, y, zh, c), flat((x + zh) % 4, c, y, x, zl))
        for x in range(4) for zl in range(2) for y in range(4) for zh in range(4) for c in range(2)
    ]
    piece = lax.ppermute(produced, ALL, moves)
    piece, forward, rest = lax.optimization_barrier((piece, near, jnp.concatenate([near, beside])))
    far = lax.ppermute(forward, EXP, along)
    rest = lax.ppermute(rest, "c", swap)
    last = lax.ppermute(far, "c", swap)
    weights = combine(own, twin, near, beside, far, rest, last, n_exp)
    pieces = jnp.broadcast_to(piece[None], (8,) + piece.shape)
    pieces = lax.all_to_all(pieces, ALL, 0, 0, axis_index_groups=eight, tiled=True)
    pieces, weights = lax.optimization_barrier((pieces, weights))
    pieces = jnp.broadcast_to(pieces[None], (4,) + pieces.shape)
    pieces = lax.all_to_all(pieces, ALL, 0, 0, axis_index_groups=four, tiled=True)
    return final(weights, pieces.reshape(n_tok, slots, block))


def solution(mesh):
    mesh = Mesh(mesh.devices.reshape(4, 2, 4, 4, 2), ALL)
    placed = (P(TOK, None), P(None, EXP), P(EXP, TOK, None), P(EXP, None, TOK))
    return jax.shard_map(
        local, mesh=mesh, in_specs=placed, out_specs=P(TOK, EXP), check_vma=False
    )
```

```python
import jax
import jax.numpy as jnp
from jax import lax
from jax.experimental import pallas as pl
from jax.experimental.pallas import tpu as pltpu
from jax.sharding import Mesh, PartitionSpec as P

BF16, F32 = jnp.bfloat16, jnp.float32
TOK, EXP = ("x", "zl", "y"), ("zh", "c")
ALL = TOK + EXP
CHUNKS = 4
STATS = 16
VMEM = 60 * 2**20


def split3(value):
    head = value.astype(BF16)
    rest = value - head.astype(F32)
    mid = rest.astype(BF16)
    return [head, mid, (rest - mid.astype(F32)).astype(BF16)]


def join3(parts):
    return parts[0].astype(F32) + parts[1].astype(F32) + parts[2].astype(F32)


def place(t, core):
    return jnp.where(core == 0, (t % 4) * 8 + t // 4, t)


def route_kernel(tokens_hbm, params_hbm, own_ref, sent_hbm, tokens, params, logits, sent_ref, stats_ref, sem, out_sem, stats_sem):
    rows, width = tokens.shape
    slots = params.shape[1]
    n_tok, _, block = sent_ref.shape
    groups = sent_hbm.shape[0]
    each = n_tok // groups
    core = lax.axis_index("c")
    span = width // CHUNKS

    def copies(i):
        cut = pl.ds(i * span, span)
        return (
            pltpu.make_async_copy(tokens_hbm.at[:, cut], tokens.at[:, cut], sem.at[0, i]),
            pltpu.make_async_copy(params_hbm.at[cut, :], params.at[cut, :], sem.at[1, i]),
        )

    for i in range(CHUNKS):
        for copy in copies(i):
            copy.start()
    for i in range(CHUNKS):
        for copy in copies(i):
            copy.wait()
        part = jnp.dot(
            tokens[:, i * span : (i + 1) * span],
            params[i * span : (i + 1) * span, :],
            preferred_element_type=F32,
        )
        if i == 0:
            logits[...] = part
        else:
            logits[...] += part

    values = logits[...]
    row_max = jnp.max(values, axis=1, keepdims=True)
    row_exp = jnp.exp(values - row_max)
    row_total = jnp.sum(row_exp, axis=1, keepdims=True)
    own_ref[:rows, :] = row_exp.astype(BF16)
    lane = lax.broadcasted_iota(jnp.int32, (rows, 128), 1)
    pair = jnp.where(lane == 0, row_max, jnp.where(lane == 1, row_total, 0.0)).T[:8]
    terms = jnp.concatenate([term.astype(F32)[:2] for term in split3(pair)] + [jnp.zeros((2, rows), F32)], axis=0)
    own_ref[rows:, :] = jnp.concatenate([terms[:, i * slots : (i + 1) * slots] for i in range(rows // slots)], axis=0).astype(BF16)

    col_max = jnp.max(values, axis=0, keepdims=True)
    shifted = jnp.exp(values - col_max)
    col_total = jnp.sum(shifted, axis=0, keepdims=True)
    dispatch = shifted.astype(BF16).T
    terms = split3(col_max) + split3(col_total)
    stats = jnp.concatenate([t[:, i * block : (i + 1) * block].astype(F32) for t in terms for i in range(slots // block)]
                            + [jnp.zeros((STATS - len(terms) * (slots // block), block), F32)], axis=0).astype(BF16)
    stats_ref[...] = stats
    leave = [
        pltpu.make_async_copy(stats_ref, sent_hbm.at[g, pl.ds(each * slots, STATS)], stats_sem.at[g])
        for g in range(groups)
    ]
    for copy in leave:
        copy.start()
    per = n_tok // CHUNKS
    for i in range(CHUNKS):
        sums = jnp.dot(dispatch, tokens[:, i * span : (i + 1) * span], preferred_element_type=F32).astype(BF16)
        for j in range(per):
            t = i * per + j
            sent_ref[t] = sums[:, j * block : (j + 1) * block]
            at = place(t, core)
            copy = pltpu.make_async_copy(
                sent_ref.at[t], sent_hbm.at[at // each, pl.ds(pl.multiple_of((at % each) * slots, slots), slots)], out_sem.at[t]
            )
            copy.start()
            leave.append(copy)
    for copy in leave:
        copy.wait()


def route(tokens, params, n_tok):
    rows, width = tokens.shape
    slots = params.shape[1]
    return pl.pallas_call(
        route_kernel,
        out_shape=(
            jax.ShapeDtypeStruct((rows + STATS, slots), BF16),
            jax.ShapeDtypeStruct((4, n_tok // 4 * slots + STATS, width // n_tok), BF16),
        ),
        in_specs=[pl.BlockSpec(memory_space=pltpu.HBM)] * 2,
        out_specs=[pl.BlockSpec(memory_space=pltpu.VMEM), pl.BlockSpec(memory_space=pltpu.HBM)],
        scratch_shapes=[
            pltpu.VMEM((rows, width), BF16),
            pltpu.VMEM((width, slots), BF16),
            pltpu.VMEM((rows, slots), F32),
            pltpu.VMEM((n_tok, slots, width // n_tok), BF16),
            pltpu.VMEM((STATS, width // n_tok), BF16),
            pltpu.SemaphoreType.DMA((2, CHUNKS)),
            pltpu.SemaphoreType.DMA((n_tok,)),
            pltpu.SemaphoreType.DMA((4,)),
        ],
        compiler_params=pltpu.CompilerParams(vmem_limit_bytes=VMEM),
        cost_estimate=pl.CostEstimate(flops=4 * rows * width * slots, bytes_accessed=10 * 2**20, transcendentals=2 * rows * slots),
        name="route",
    )(tokens, params)


def scales(stats, cuts, block):
    senders = stats.shape[0]
    terms = [stats[:, i * cuts : (i + 1) * cuts] for i in range(6)]
    peaks = terms[0] + terms[1] + terms[2]
    totals = terms[3] + terms[4] + terms[5]
    peak = jnp.max(peaks, axis=0, keepdims=True)
    scale = jnp.exp(peaks - peak)
    total = jnp.sum(scale * totals, axis=0, keepdims=True)
    def columns(factor):
        return [
            jnp.concatenate([factor[:, c, :], jnp.zeros((block - senders, block), F32)], axis=0).T for c in range(cuts)
        ]
    return peak, total, scale, columns


def merge_kernel(came_ref, out_ref):
    senders, _, block = came_ref.shape
    each, total_rows, _ = out_ref.shape
    slots = total_rows - STATS
    cuts = slots // block
    peak, total, scale, columns = scales(came_ref[:, each * slots :, :].astype(F32), cuts, block)
    terms = split3(peak[0]) + split3(total[0])
    stats = jnp.concatenate([t.astype(F32) for t in terms] + [jnp.zeros((STATS - len(terms) * cuts, block), F32)], axis=0).astype(BF16)
    columns = columns(scale)
    for r in range(each):
        out_ref[r, slots:, :] = stats
    for c in range(cuts):
        factors = [jnp.broadcast_to(columns[c][:, t : t + 1], (block, block)) for t in range(senders)]
        for r in range(each):
            at = r * slots + c * block
            parts = [came_ref[t, at : at + block, :].astype(F32) * factors[t] for t in range(senders)]
            out_ref[r, c * block : (c + 1) * block, :] = sum(parts[1:], parts[0]).astype(BF16)


def merge(came, slots):
    senders, total_rows, block = came.shape
    each = total_rows // slots
    return pl.pallas_call(
        merge_kernel,
        out_shape=jax.ShapeDtypeStruct((each, slots + STATS, block), BF16),
        in_specs=[pl.BlockSpec(memory_space=pltpu.VMEM)],
        out_specs=pl.BlockSpec(memory_space=pltpu.VMEM),
        compiler_params=pltpu.CompilerParams(vmem_limit_bytes=32 * 2**20),
        cost_estimate=pl.CostEstimate(flops=2 * senders * each * slots * block, bytes_accessed=3 * 2**20, transcendentals=0),
        name="merge",
    )(came)


def expand_kernel(came_ref, weight_ref, out_ref):
    senders, total_rows, block = came_ref.shape
    slots = total_rows - STATS
    experts, _, ff = weight_ref.shape
    cuts = slots // block
    per = slots // experts
    n_out, high, wide = out_ref.shape
    each = n_out // experts
    _, total, scale, columns = scales(came_ref[:, slots:, :].astype(F32), cuts, block)
    columns = columns(scale / total)
    parts = []
    for c in range(cuts):
        part = [came_ref[t, c * block : (c + 1) * block, :].astype(F32) * columns[c][:, t : t + 1] for t in range(senders)]
        parts.append(sum(part[1:], part[0]).astype(BF16))
    inputs = jnp.concatenate(parts, axis=0)
    for e in range(experts):
        pre = jnp.dot(inputs[e * per : (e + 1) * per], weight_ref[e], preferred_element_type=F32).astype(BF16)
        for i in range(per // high):
            for j in range(ff // wide):
                out_ref[e * each + i * (ff // wide) + j] = pre[i * high : (i + 1) * high, j * wide : (j + 1) * wide]


def expand(came, weight_in, n_tok):
    senders, total_rows, block = came.shape
    slots = total_rows - STATS
    experts, _, ff = weight_in.shape
    high = 16
    out = (n_tok, high, slots * ff // (n_tok * high))
    return pl.pallas_call(
        expand_kernel,
        out_shape=jax.ShapeDtypeStruct(out, BF16),
        in_specs=[pl.BlockSpec(memory_space=pltpu.VMEM)] * 2,
        out_specs=pl.BlockSpec(memory_space=pltpu.VMEM),
        compiler_params=pltpu.CompilerParams(vmem_limit_bytes=40 * 2**20),
        cost_estimate=pl.CostEstimate(flops=2 * slots * block * ff, bytes_accessed=4 * 2**20, transcendentals=0),
        name="expand",
    )(came, weight_in)


def produce_kernel(hidden_ref, weight_ref, out_ref):
    n_tok, high, wide = hidden_ref.shape
    experts, ff, block = weight_ref.shape
    per = out_ref.shape[0] // experts
    halves, chunks = ff // wide, per // high
    each = n_tok // experts
    for e in range(experts):
        total = None
        for j in range(halves):
            rows = jnp.concatenate([hidden_ref[e * each + i * halves + j] for i in range(chunks)], axis=0)
            part = jnp.dot(rows, weight_ref[e, j * wide : (j + 1) * wide, :], preferred_element_type=F32)
            total = part if total is None else total + part
        out_ref[e * per : (e + 1) * per, :] = total.astype(BF16)


def produce(hidden, weight_out):
    n_tok, high, wide = hidden.shape
    experts, ff, block = weight_out.shape
    slots = n_tok * high * wide // ff
    return pl.pallas_call(
        produce_kernel,
        out_shape=jax.ShapeDtypeStruct((slots, block), BF16),
        in_specs=[pl.BlockSpec(memory_space=pltpu.VMEM)] * 2,
        out_specs=pl.BlockSpec(memory_space=pltpu.VMEM),
        compiler_params=pltpu.CompilerParams(vmem_limit_bytes=40 * 2**20),
        cost_estimate=pl.CostEstimate(flops=2 * slots * ff * block, bytes_accessed=3 * 2**20, transcendentals=0),
        name="produce",
    )(hidden, weight_out)


def combine_kernel(own_ref, twin_ref, near_ref, beside_ref, far_ref, rest_ref, last_ref, out_ref):
    total_rows, slots = own_ref.shape
    rows = total_rows - STATS
    here, core = lax.axis_index("zh"), lax.axis_index("c")
    n_hi = out_ref.shape[1] // slots // 2
    step = 2 * core - 1
    blocks = [
        (own_ref, 0, 0, 0), (twin_ref, 0, 0, 1), (near_ref, 0, 1, 0), (beside_ref, 0, 1, 1), (far_ref, 0, 2, 0),
        (rest_ref, 0, -1, 1), (rest_ref, total_rows, -1, 0), (last_ref, 0, -2, 1),
    ]
    peaks, totals = [], []
    for ref, at, _, _ in blocks:
        stats = ref[at + rows : at + total_rows, :].astype(F32)
        stats = jnp.concatenate([stats[i * 8 : (i + 1) * 8] for i in range(rows // slots)], axis=1)
        joined = stats[0:2] + stats[2:4] + stats[4:6]
        peaks.append(joined[0:1])
        totals.append(joined[1:2])
    peaks, totals = jnp.concatenate(peaks, axis=0), jnp.concatenate(totals, axis=0)
    scale = jnp.exp(peaks - jnp.max(peaks, axis=0, keepdims=True))
    scale = scale / jnp.sum(scale * totals, axis=0, keepdims=True)
    scale = jnp.concatenate([scale, jnp.zeros((128 - scale.shape[0], rows), F32)], axis=0).T
    for k, (ref, at, steps, flip) in enumerate(blocks):
        z = lax.rem(here + steps * step + 2 * n_hi, n_hi)
        e = 2 * z + (1 - core if flip else core)
        at_out = pl.ds(pl.multiple_of(e * slots, slots), slots)
        out_ref[:, at_out] = (ref[at : at + rows, :].astype(F32) * scale[:, k : k + 1]).astype(BF16)


def combine(own, twin, near, beside, far, rest, last, n_exp):
    total_rows, slots = own.shape
    rows = total_rows - STATS
    return pl.pallas_call(
        combine_kernel,
        out_shape=jax.ShapeDtypeStruct((rows, n_exp * slots), BF16),
        in_specs=[pl.BlockSpec(memory_space=pltpu.VMEM)] * 7,
        out_specs=pl.BlockSpec(memory_space=pltpu.VMEM),
        compiler_params=pltpu.CompilerParams(vmem_limit_bytes=32 * 2**20),
        cost_estimate=pl.CostEstimate(flops=2 * n_exp * rows * slots, bytes_accessed=4 * 2**20, transcendentals=0),
        name="combine",
    )(own, twin, near, beside, far, rest, last)


def final_kernel(weights_ref, pieces_hbm, out_ref, values, sem):
    rows, total = weights_ref.shape
    n_tok, slots, block = pieces_hbm.shape
    n_exp = total // slots
    quarter = n_tok // n_exp
    here, core = lax.axis_index("zh"), lax.axis_index("c")
    copies = []
    for e in range(n_exp):
        first = ((e // 2 + here) % 4) * 8 + (e % 2) * 4
        for q in range(quarter):
            into = values.at[pl.ds(e * slots, slots), pl.ds(q * block, block)]
            copies.append(pltpu.make_async_copy(pieces_hbm.at[place(first + q, core)], into, sem.at[e * quarter + q]))
            copies[-1].start()
    step = 1
    result = None
    for e in range(0, n_exp, step):
        for copy in copies[e * quarter : (e + step) * quarter]:
            copy.wait()
        cut = slice(e * slots, (e + step) * slots)
        part = jnp.dot(weights_ref[:, cut], values[cut, :], preferred_element_type=F32)
        result = part if result is None else result + part
    out_ref[...] = result.astype(BF16)


def final(weights, pieces):
    rows, total = weights.shape
    n_tok, slots, block = pieces.shape
    columns = n_tok * slots // total * block
    return pl.pallas_call(
        final_kernel,
        out_shape=jax.ShapeDtypeStruct((rows, columns), BF16),
        in_specs=[pl.BlockSpec(memory_space=pltpu.VMEM), pl.BlockSpec(memory_space=pltpu.HBM)],
        out_specs=pl.BlockSpec(memory_space=pltpu.VMEM),
        scratch_shapes=[pltpu.VMEM((total, columns), BF16), pltpu.SemaphoreType.DMA((n_tok,))],
        compiler_params=pltpu.CompilerParams(vmem_limit_bytes=50 * 2**20),
        cost_estimate=pl.CostEstimate(flops=2 * rows * total * columns, bytes_accessed=5 * 2**20, transcendentals=0),
        name="final",
    )(weights, pieces)


def flat(x, zl, y, zh, c):
    return (((x * 2 + zl) * 4 + y) * 4 + zh) * 2 + c


def exchange_groups():
    four, eight = [], []
    for zh in range(4):
        four += [[flat(x, zl, y, zh, 0) for y in range(4)] for x in range(4) for zl in range(2)]
        four += [[flat(x, zl, y, zh, 1) for x in range(4)] for zl in range(2) for y in range(4)]
        eight += [[flat(x, zl, y, zh, 0) for x in range(4) for zl in range(2)] for y in range(4)]
        eight += [[flat(x, zl, y, zh, 1) for zl in range(2) for y in range(4)] for x in range(4)]
    return four, eight


def local(tokens, slot_params, weight_in, weight_out):
    n_tok, n_exp, n_hi = lax.axis_size(TOK), lax.axis_size(EXP), lax.axis_size("zh")
    block, slots = weight_in.shape[1], slot_params.shape[1]
    four, eight = exchange_groups()
    swap = [(0, 1), (1, 0)]
    along = [
        (2 * z + c, 2 * ((z + (1 if c == 0 else -1)) % n_hi) + c) for z in range(n_hi) for c in range(2)
    ]
    own, sent = route(tokens, slot_params, n_tok)

    twin = lax.ppermute(own, "c", swap)
    near = lax.ppermute(own, EXP, along)
    beside = lax.ppermute(twin, EXP, along)
    came = lax.all_to_all(sent, ALL, 0, 0, axis_index_groups=four, tiled=True)
    came, near, beside = lax.optimization_barrier((came, near, beside))
    came = lax.all_to_all(merge(came, slots), ALL, 0, 0, axis_index_groups=eight, tiled=True)

    pre = lax.all_to_all(expand(came, weight_in, n_tok), TOK, 0, 0, tiled=True)
    pre = jnp.sum(pre.astype(F32), axis=0)
    hidden = jax.nn.gelu(pre, approximate=False).astype(BF16)
    hidden = lax.all_to_all(
        jnp.broadcast_to(hidden[None], (n_tok,) + hidden.shape), TOK, 0, 0, tiled=True
    )
    produced = produce(hidden, weight_out)

    moves = [
        (flat(x, zl, y, zh, c), flat((x + zh) % 4, c, y, x, zl))
        for x in range(4) for zl in range(2) for y in range(4) for zh in range(4) for c in range(2)
    ]
    piece = lax.ppermute(produced, ALL, moves)
    piece, rest = lax.optimization_barrier((piece, jnp.concatenate([near, beside])))
    pieces = jnp.broadcast_to(piece[None], (8,) + piece.shape)
    pieces = lax.all_to_all(pieces, ALL, 0, 0, axis_index_groups=eight, tiled=True)
    pieces, forward, rest = lax.optimization_barrier((pieces, near, rest))
    far = lax.ppermute(forward, EXP, along)
    rest = lax.ppermute(rest, "c", swap)
    last = lax.ppermute(far, "c", swap)
    pieces = jnp.broadcast_to(pieces[None], (4,) + pieces.shape)
    pieces = lax.all_to_all(pieces, ALL, 0, 0, axis_index_groups=four, tiled=True)
    return final(combine(own, twin, near, beside, far, rest, last, n_exp), pieces.reshape(n_tok, slots, block))


def solution(mesh):
    mesh = Mesh(mesh.devices.reshape(4, 2, 4, 4, 2), ALL)
    placed = (P(TOK, None), P(None, EXP), P(EXP, TOK, None), P(EXP, None, TOK))
    return jax.shard_map(
        local, mesh=mesh, in_specs=placed, out_specs=P(TOK, EXP), check_vma=False
    )
```

```python
import jax
import jax.numpy as jnp
from jax import lax
from jax.experimental import pallas as pl
from jax.experimental.pallas import tpu as pltpu
from jax.sharding import Mesh, PartitionSpec as P

BF16, F32 = jnp.bfloat16, jnp.float32
TOK, EXP = ("x", "zl", "y"), ("zh", "c")
ALL = TOK + EXP
CHUNKS = 4
STATS = 16
VMEM = 60 * 2**20


def split3(value):
    head = value.astype(BF16)
    rest = value - head.astype(F32)
    mid = rest.astype(BF16)
    return [head, mid, (rest - mid.astype(F32)).astype(BF16)]


def join3(parts):
    return parts[0].astype(F32) + parts[1].astype(F32) + parts[2].astype(F32)


def place(t, core):
    ux, uy = (t // 8 + 3 * core) % 4, (t % 4 + 3 * core) % 4
    return ((ux % 2) * 2 + uy % 2) * 8 + (t // 4) % 2 * 4 + (ux // 2) * 2 + uy // 2


def route_kernel(tokens_hbm, params_hbm, own_ref, sent_hbm, tokens, params, logits, sent_ref, stats_ref, sem, out_sem, stats_sem):
    rows, width = tokens.shape
    slots = params.shape[1]
    n_tok, _, block = sent_ref.shape
    groups = sent_hbm.shape[0]
    each = n_tok // groups
    core = lax.axis_index("c")
    span = width // CHUNKS

    def copies(i):
        cut = pl.ds(i * span, span)
        return (
            pltpu.make_async_copy(tokens_hbm.at[:, cut], tokens.at[:, cut], sem.at[0, i]),
            pltpu.make_async_copy(params_hbm.at[cut, :], params.at[cut, :], sem.at[1, i]),
        )

    for i in range(CHUNKS):
        for copy in copies(i):
            copy.start()
    for i in range(CHUNKS):
        for copy in copies(i):
            copy.wait()
        part = jnp.dot(
            tokens[:, i * span : (i + 1) * span],
            params[i * span : (i + 1) * span, :],
            preferred_element_type=F32,
        )
        if i == 0:
            logits[...] = part
        else:
            logits[...] += part

    values = logits[...]
    row_max = jnp.max(values, axis=1, keepdims=True)
    row_exp = jnp.exp(values - row_max)
    row_total = jnp.sum(row_exp, axis=1, keepdims=True)
    own_ref[:rows, :] = row_exp.astype(BF16)
    lane = lax.broadcasted_iota(jnp.int32, (rows, 128), 1)
    pair = jnp.where(lane == 0, row_max, jnp.where(lane == 1, row_total, 0.0)).T[:8]
    terms = jnp.concatenate([term.astype(F32)[:2] for term in split3(pair)] + [jnp.zeros((2, rows), F32)], axis=0)
    own_ref[rows:, :] = jnp.concatenate([terms[:, i * slots : (i + 1) * slots] for i in range(rows // slots)], axis=0).astype(BF16)

    col_max = jnp.max(values, axis=0, keepdims=True)
    shifted = jnp.exp(values - col_max)
    col_total = jnp.sum(shifted, axis=0, keepdims=True)
    dispatch = shifted.astype(BF16).T
    terms = split3(col_max) + split3(col_total)
    stats = jnp.concatenate([t[:, i * block : (i + 1) * block].astype(F32) for t in terms for i in range(slots // block)]
                            + [jnp.zeros((STATS - len(terms) * (slots // block), block), F32)], axis=0).astype(BF16)
    stats_ref[...] = stats
    leave = [
        pltpu.make_async_copy(stats_ref, sent_hbm.at[g, pl.ds(each * slots, STATS)], stats_sem.at[g])
        for g in range(groups)
    ]
    for copy in leave:
        copy.start()
    per = n_tok // CHUNKS
    for i in range(CHUNKS):
        sums = jnp.dot(dispatch, tokens[:, i * span : (i + 1) * span], preferred_element_type=F32).astype(BF16)
        for j in range(per):
            t = i * per + j
            sent_ref[t] = sums[:, j * block : (j + 1) * block]
            at = place(t, core)
            copy = pltpu.make_async_copy(
                sent_ref.at[t], sent_hbm.at[at // each, pl.ds(pl.multiple_of((at % each) * slots, slots), slots)], out_sem.at[t]
            )
            copy.start()
            leave.append(copy)
    for copy in leave:
        copy.wait()


def route(tokens, params, n_tok):
    rows, width = tokens.shape
    slots = params.shape[1]
    return pl.pallas_call(
        route_kernel,
        out_shape=(
            jax.ShapeDtypeStruct((rows + STATS, slots), BF16),
            jax.ShapeDtypeStruct((4, n_tok // 4 * slots + STATS, width // n_tok), BF16),
        ),
        in_specs=[pl.BlockSpec(memory_space=pltpu.HBM)] * 2,
        out_specs=[pl.BlockSpec(memory_space=pltpu.VMEM), pl.BlockSpec(memory_space=pltpu.HBM)],
        scratch_shapes=[
            pltpu.VMEM((rows, width), BF16),
            pltpu.VMEM((width, slots), BF16),
            pltpu.VMEM((rows, slots), F32),
            pltpu.VMEM((n_tok, slots, width // n_tok), BF16),
            pltpu.VMEM((STATS, width // n_tok), BF16),
            pltpu.SemaphoreType.DMA((2, CHUNKS)),
            pltpu.SemaphoreType.DMA((n_tok,)),
            pltpu.SemaphoreType.DMA((4,)),
        ],
        compiler_params=pltpu.CompilerParams(vmem_limit_bytes=VMEM),
        cost_estimate=pl.CostEstimate(flops=4 * rows * width * slots, bytes_accessed=10 * 2**20, transcendentals=2 * rows * slots),
        name="route",
    )(tokens, params)


def scales(stats, cuts, block):
    senders = stats.shape[0]
    terms = [stats[:, i * cuts : (i + 1) * cuts] for i in range(6)]
    peaks = terms[0] + terms[1] + terms[2]
    totals = terms[3] + terms[4] + terms[5]
    peak = jnp.max(peaks, axis=0, keepdims=True)
    scale = jnp.exp(peaks - peak)
    total = jnp.sum(scale * totals, axis=0, keepdims=True)
    def columns(factor):
        return [
            jnp.concatenate([factor[:, c, :], jnp.zeros((block - senders, block), F32)], axis=0).T for c in range(cuts)
        ]
    return peak, total, scale, columns


def merge_kernel(came_ref, out_ref):
    senders, _, block = came_ref.shape
    each, total_rows, _ = out_ref.shape
    slots = total_rows - STATS
    cuts = slots // block
    peak, total, scale, columns = scales(came_ref[:, each * slots :, :].astype(F32), cuts, block)
    terms = split3(peak[0]) + split3(total[0])
    stats = jnp.concatenate([t.astype(F32) for t in terms] + [jnp.zeros((STATS - len(terms) * cuts, block), F32)], axis=0).astype(BF16)
    columns = columns(scale)
    for r in range(each):
        out_ref[r, slots:, :] = stats
    for c in range(cuts):
        factors = [jnp.broadcast_to(columns[c][:, t : t + 1], (block, block)) for t in range(senders)]
        for r in range(each):
            at = r * slots + c * block
            parts = [came_ref[t, at : at + block, :].astype(F32) * factors[t] for t in range(senders)]
            out_ref[r, c * block : (c + 1) * block, :] = sum(parts[1:], parts[0]).astype(BF16)


def merge(came, slots):
    senders, total_rows, block = came.shape
    each = total_rows // slots
    return pl.pallas_call(
        merge_kernel,
        out_shape=jax.ShapeDtypeStruct((each, slots + STATS, block), BF16),
        in_specs=[pl.BlockSpec(memory_space=pltpu.VMEM)],
        out_specs=pl.BlockSpec(memory_space=pltpu.VMEM),
        compiler_params=pltpu.CompilerParams(vmem_limit_bytes=32 * 2**20),
        cost_estimate=pl.CostEstimate(flops=2 * senders * each * slots * block, bytes_accessed=3 * 2**20, transcendentals=0),
        name="merge",
    )(came)


def expand_kernel(came_ref, weight_ref, out_ref):
    senders, total_rows, block = came_ref.shape
    slots = total_rows - STATS
    experts, _, ff = weight_ref.shape
    cuts = slots // block
    per = slots // experts
    n_out, high, wide = out_ref.shape
    each = n_out // experts
    _, total, scale, columns = scales(came_ref[:, slots:, :].astype(F32), cuts, block)
    columns = columns(scale / total)
    parts = []
    for c in range(cuts):
        part = [came_ref[t, c * block : (c + 1) * block, :].astype(F32) * columns[c][:, t : t + 1] for t in range(senders)]
        parts.append(sum(part[1:], part[0]).astype(BF16))
    inputs = jnp.concatenate(parts, axis=0)
    for e in range(experts):
        pre = jnp.dot(inputs[e * per : (e + 1) * per], weight_ref[e], preferred_element_type=F32).astype(BF16)
        for i in range(per // high):
            for j in range(ff // wide):
                out_ref[e * each + i * (ff // wide) + j] = pre[i * high : (i + 1) * high, j * wide : (j + 1) * wide]


def expand(came, weight_in, n_tok):
    senders, total_rows, block = came.shape
    slots = total_rows - STATS
    experts, _, ff = weight_in.shape
    high = 16
    out = (n_tok, high, slots * ff // (n_tok * high))
    return pl.pallas_call(
        expand_kernel,
        out_shape=jax.ShapeDtypeStruct(out, BF16),
        in_specs=[pl.BlockSpec(memory_space=pltpu.VMEM)] * 2,
        out_specs=pl.BlockSpec(memory_space=pltpu.VMEM),
        compiler_params=pltpu.CompilerParams(vmem_limit_bytes=40 * 2**20),
        cost_estimate=pl.CostEstimate(flops=2 * slots * block * ff, bytes_accessed=4 * 2**20, transcendentals=0),
        name="expand",
    )(came, weight_in)


def produce_kernel(hidden_ref, weight_ref, out_ref):
    n_tok, high, wide = hidden_ref.shape
    experts, ff, block = weight_ref.shape
    per = out_ref.shape[0] // experts
    halves, chunks = ff // wide, per // high
    each = n_tok // experts
    for e in range(experts):
        total = None
        for j in range(halves):
            rows = jnp.concatenate([hidden_ref[e * each + i * halves + j] for i in range(chunks)], axis=0)
            part = jnp.dot(rows, weight_ref[e, j * wide : (j + 1) * wide, :], preferred_element_type=F32)
            total = part if total is None else total + part
        out_ref[e * per : (e + 1) * per, :] = total.astype(BF16)


def produce(hidden, weight_out):
    n_tok, high, wide = hidden.shape
    experts, ff, block = weight_out.shape
    slots = n_tok * high * wide // ff
    return pl.pallas_call(
        produce_kernel,
        out_shape=jax.ShapeDtypeStruct((slots, block), BF16),
        in_specs=[pl.BlockSpec(memory_space=pltpu.VMEM)] * 2,
        out_specs=pl.BlockSpec(memory_space=pltpu.VMEM),
        compiler_params=pltpu.CompilerParams(vmem_limit_bytes=40 * 2**20),
        cost_estimate=pl.CostEstimate(flops=2 * slots * ff * block, bytes_accessed=3 * 2**20, transcendentals=0),
        name="produce",
    )(hidden, weight_out)


def combine_kernel(own_ref, twin_ref, near_ref, beside_ref, far_ref, rest_ref, last_ref, out_ref):
    total_rows, slots = own_ref.shape
    rows = total_rows - STATS
    here, core = lax.axis_index("zh"), lax.axis_index("c")
    n_hi = out_ref.shape[1] // slots // 2
    step = 2 * core - 1
    blocks = [
        (own_ref, 0, 0, 0), (twin_ref, 0, 0, 1), (near_ref, 0, 1, 0), (beside_ref, 0, 1, 1), (far_ref, 0, 2, 0),
        (rest_ref, 0, -1, 1), (rest_ref, total_rows, -1, 0), (last_ref, 0, -2, 1),
    ]
    peaks, totals = [], []
    for ref, at, _, _ in blocks:
        stats = ref[at + rows : at + total_rows, :].astype(F32)
        stats = jnp.concatenate([stats[i * 8 : (i + 1) * 8] for i in range(rows // slots)], axis=1)
        joined = stats[0:2] + stats[2:4] + stats[4:6]
        peaks.append(joined[0:1])
        totals.append(joined[1:2])
    peaks, totals = jnp.concatenate(peaks, axis=0), jnp.concatenate(totals, axis=0)
    scale = jnp.exp(peaks - jnp.max(peaks, axis=0, keepdims=True))
    scale = scale / jnp.sum(scale * totals, axis=0, keepdims=True)
    scale = jnp.concatenate([scale, jnp.zeros((128 - scale.shape[0], rows), F32)], axis=0).T
    for k, (ref, at, steps, flip) in enumerate(blocks):
        z = lax.rem(here + steps * step + 2 * n_hi, n_hi)
        e = 2 * z + (1 - core if flip else core)
        at_out = pl.ds(pl.multiple_of(e * slots, slots), slots)
        out_ref[:, at_out] = (ref[at : at + rows, :].astype(F32) * scale[:, k : k + 1]).astype(BF16)


def combine(own, twin, near, beside, far, rest, last, n_exp):
    total_rows, slots = own.shape
    rows = total_rows - STATS
    return pl.pallas_call(
        combine_kernel,
        out_shape=jax.ShapeDtypeStruct((rows, n_exp * slots), BF16),
        in_specs=[pl.BlockSpec(memory_space=pltpu.VMEM)] * 7,
        out_specs=pl.BlockSpec(memory_space=pltpu.VMEM),
        compiler_params=pltpu.CompilerParams(vmem_limit_bytes=32 * 2**20),
        cost_estimate=pl.CostEstimate(flops=2 * n_exp * rows * slots, bytes_accessed=4 * 2**20, transcendentals=0),
        name="combine",
    )(own, twin, near, beside, far, rest, last)


def final_kernel(weights_ref, pieces_hbm, out_ref, values, sem):
    rows, total = weights_ref.shape
    n_tok, slots, block = pieces_hbm.shape
    n_exp = total // slots
    quarter = n_tok // n_exp
    here, core = lax.axis_index("zh"), lax.axis_index("c")
    copies = []
    for e in range(n_exp):
        first = ((e // 2 + here) % 4) * 8 + (e % 2) * 4
        for q in range(quarter):
            into = values.at[pl.ds(e * slots, slots), pl.ds(q * block, block)]
            copies.append(pltpu.make_async_copy(pieces_hbm.at[place(first + q, core)], into, sem.at[e * quarter + q]))
            copies[-1].start()
    step = 1
    result = None
    for e in range(0, n_exp, step):
        for copy in copies[e * quarter : (e + step) * quarter]:
            copy.wait()
        cut = slice(e * slots, (e + step) * slots)
        part = jnp.dot(weights_ref[:, cut], values[cut, :], preferred_element_type=F32)
        result = part if result is None else result + part
    out_ref[...] = result.astype(BF16)


def final(weights, pieces):
    rows, total = weights.shape
    n_tok, slots, block = pieces.shape
    columns = n_tok * slots // total * block
    return pl.pallas_call(
        final_kernel,
        out_shape=jax.ShapeDtypeStruct((rows, columns), BF16),
        in_specs=[pl.BlockSpec(memory_space=pltpu.VMEM), pl.BlockSpec(memory_space=pltpu.HBM)],
        out_specs=pl.BlockSpec(memory_space=pltpu.VMEM),
        scratch_shapes=[pltpu.VMEM((total, columns), BF16), pltpu.SemaphoreType.DMA((n_tok,))],
        compiler_params=pltpu.CompilerParams(vmem_limit_bytes=50 * 2**20),
        cost_estimate=pl.CostEstimate(flops=2 * rows * total * columns, bytes_accessed=5 * 2**20, transcendentals=0),
        name="final",
    )(weights, pieces)


def flat(x, zl, y, zh, c):
    return (((x * 2 + zl) * 4 + y) * 4 + zh) * 2 + c


def exchange_groups():
    four, eight, two = [], [], range(2)
    for zh in range(4):
        for c in two:
            def device(gx, gy, zl, px, py):
                return flat((px * 2 + gx + c) % 4, zl, (py * 2 + gy + c) % 4, zh, c)
            four += [[device(gx, gy, zl, px, py) for gx in two for gy in two] for zl in two for px in two for py in two]
            eight += [[device(gx, gy, zl, px, py) for zl in two for px in two for py in two] for gx in two for gy in two]
    return four, eight


def local(tokens, slot_params, weight_in, weight_out):
    n_tok, n_exp, n_hi = lax.axis_size(TOK), lax.axis_size(EXP), lax.axis_size("zh")
    block, slots = weight_in.shape[1], slot_params.shape[1]
    four, eight = exchange_groups()
    swap = [(0, 1), (1, 0)]
    along = [
        (2 * z + c, 2 * ((z + (1 if c == 0 else -1)) % n_hi) + c) for z in range(n_hi) for c in range(2)
    ]
    own, sent = route(tokens, slot_params, n_tok)

    twin = lax.ppermute(own, "c", swap)
    near = lax.ppermute(own, EXP, along)
    beside = lax.ppermute(twin, EXP, along)
    came = lax.all_to_all(sent, ALL, 0, 0, axis_index_groups=four, tiled=True)
    came, near, beside = lax.optimization_barrier((came, near, beside))
    came = lax.all_to_all(merge(came, slots), ALL, 0, 0, axis_index_groups=eight, tiled=True)

    pre = lax.all_to_all(expand(came, weight_in, n_tok), TOK, 0, 0, tiled=True)
    pre = jnp.sum(pre.astype(F32), axis=0)
    hidden = jax.nn.gelu(pre, approximate=False).astype(BF16)
    hidden = lax.all_to_all(
        jnp.broadcast_to(hidden[None], (n_tok,) + hidden.shape), TOK, 0, 0, tiled=True
    )
    produced = produce(hidden, weight_out)

    moves = [
        (flat(x, zl, y, zh, c), flat((x + zh) % 4, c, y, x, zl))
        for x in range(4) for zl in range(2) for y in range(4) for zh in range(4) for c in range(2)
    ]
    piece = lax.ppermute(produced, ALL, moves)
    piece, rest = lax.optimization_barrier((piece, jnp.concatenate([near, beside])))
    pieces = jnp.broadcast_to(piece[None], (8,) + piece.shape)
    pieces = lax.all_to_all(pieces, ALL, 0, 0, axis_index_groups=eight, tiled=True)
    pieces, forward, rest = lax.optimization_barrier((pieces, near, rest))
    far = lax.ppermute(forward, EXP, along)
    rest = lax.ppermute(rest, "c", swap)
    last = lax.ppermute(far, "c", swap)
    pieces = jnp.broadcast_to(pieces[None], (4,) + pieces.shape)
    pieces = lax.all_to_all(pieces, ALL, 0, 0, axis_index_groups=four, tiled=True)
    return final(combine(own, twin, near, beside, far, rest, last, n_exp), pieces.reshape(n_tok, slots, block))


def solution(mesh):
    mesh = Mesh(mesh.devices.reshape(4, 2, 4, 4, 2), ALL)
    placed = (P(TOK, None), P(None, EXP), P(EXP, TOK, None), P(EXP, None, TOK))
    return jax.shard_map(
        local, mesh=mesh, in_specs=placed, out_specs=P(TOK, EXP), check_vma=False
    )
```
